32 devices in a mesh: shard: 2 (over x), ctx: 4 (over z), tp: 4 (over y, core).
Axes of the slice: x: 2, y: 2, z: 4, core: 2. Of those that a mesh axis runs over, the one named last changes fastest.
Arguments:
- hidden_in: bfloat16 [16, 1024, 1024], P(('shard', 'tp'), 'ctx'), may hold values from -6 to 6
- doc_starts: int32 [16, 4], P('shard'), may hold values from 0 to 1023, as said below
- grad_out: float32 [16, 1024, 1024], P(('shard', 'tp'), 'ctx'), may hold values from -6 to 6
- qkv_weight: float32 [1024, 3, 1024], P('shard', None, 'tp'), may hold values from -0.1875 to 0.1875
- output_weight: float32 [1024, 1024], P('tp', 'shard'), may hold values from -1 to 1
- geglu_weight: float32 [1024, 2, 2624], P('shard', None, 'tp'), may hold values from -0.1875 to 0.1875
- down_weight: float32 [2624, 1024], P('tp', 'shard'), may hold values from -0.125 to 0.125
- norm_gains: float32 [2, 1024], P(None, 'shard'), may hold values from 0.5 to 1.5
- qkv_momentum: float32 [1024, 3, 1024], P('shard', None, 'tp'), may hold values from -40 to 40
- qkv_variance: float32 [1024, 3, 1024], P('shard', None, 'tp'), may hold values from 42.5984 to 671.744
- output_momentum: float32 [1024, 1024], P('tp', 'shard'), may hold values from -6 to 6
- output_variance: float32 [1024, 1024], P('tp', 'shard'), may hold values from 3.76832 to 60.6208
- geglu_momentum: float32 [1024, 2, 2624], P('shard', None, 'tp'), may hold values from -32 to 32
- geglu_variance: float32 [1024, 2, 2624], P('shard', None, 'tp'), may hold values from 22.9376 to 360.448
- down_momentum: float32 [2624, 1024], P('tp', 'shard'), may hold values from -56 to 56
- down_variance: float32 [2624, 1024], P('tp', 'shard'), may hold values from 70.4512 to 1130.496
- gains_momentum: float32 [2, 1024], P(None, 'shard'), may hold values from -64 to 64
- gains_variance: float32 [2, 1024], P(None, 'shard'), may hold values from 121.2416 to 1933.312
Outputs:
- hidden_out: bfloat16 [16, 1024, 1024], P(('shard', 'tp'), 'ctx')
- grad_in: float32 [16, 1024, 1024], P(('shard', 'tp'), 'ctx')
- qkv_updated: float32 [1024, 3, 1024], P('shard', None, 'tp')
- momentum_qkv: float32 [1024, 3, 1024], P('shard', None, 'tp')
- variance_qkv: float32 [1024, 3, 1024], P('shard', None, 'tp')
- output_updated: float32 [1024, 1024], P('tp', 'shard')
- momentum_output: float32 [1024, 1024], P('tp', 'shard')
- variance_output: float32 [1024, 1024], P('tp', 'shard')
- geglu_updated: float32 [1024, 2, 2624], P('shard', None, 'tp')
- momentum_geglu: float32 [1024, 2, 2624], P('shard', None, 'tp')
- variance_geglu: float32 [1024, 2, 2624], P('shard', None, 'tp')
- down_updated: float32 [2624, 1024], P('tp', 'shard')
- momentum_down: float32 [2624, 1024], P('tp', 'shard')
- variance_down: float32 [2624, 1024], P('tp', 'shard')
- gains_updated: float32 [2, 1024], P(None, 'shard')
- momentum_gains: float32 [2, 1024], P(None, 'shard')
- variance_gains: float32 [2, 1024], P(None, 'shard')
The draws below stay inside these ranges and needn't reach their ends.
Inputs may be any that keep to these rules, and one draw needn't show every extreme that they name: `doc_starts`: in each row the 4 document starts rise strictly from 0.
All inputs are finite; a program needn't handle non-finite values.
Results may differ from the reference program's by a relative error of at most 0.024.
Values may be sent and summed in bfloat16 or wider, within the bound.
No kernel may reach another device: no remote copies, remote signals or barrier semaphores. Data moves between devices by JAX's collectives and lax.ppermute only.
A program may use at most 192 MiB of HBM per device.

```python
import math
from functools import partial
import jax
import jax.numpy as jnp
from jax import lax

D = 1024
HEADS = 16
HD = 64
FF = 2624
HALF = 64
L = 1024
STEP = 10
HIDQ = 1024
ROWS = 16
TOKENS = 16384
N_CTX = 4


def draw_doc_starts(key, part):
    key = jax.random.fold_in(key, 7)
    subkeys = jax.random.split(key, 4)
    seg_len = L // N_CTX
    last_start = (N_CTX - 1) * seg_len
    first_cut = jax.random.randint(subkeys[0], (ROWS,), 1, seg_len)
    second_cut = jax.random.randint(subkeys[1], (ROWS,), last_start + 1, last_start + seg_len // 2 + 1)
    third_cut = jax.random.randint(subkeys[2], (ROWS,), second_cut + 1, L)
    third_cut = third_cut.at[0].set(L - 1)
    flipped = jax.random.randint(subkeys[3], (ROWS,), 0, 2)
    flipped = flipped.at[0].set(0)
    leading = jnp.zeros((ROWS,), jnp.int32)
    drawn = jnp.stack([leading, first_cut, second_cut, third_cut], axis=1)
    mirror = jnp.stack([leading, L - third_cut, L - second_cut, L - first_cut], axis=1)
    return jnp.where(flipped[:, None] == 1, mirror, drawn).astype(jnp.int32)


def level_of(own_key, extent, shards, low, high):
    factor_of, own = 1.0, jax.random.fold_in(own_key, 6)
    for position, shards_of in shards:
        draws = jnp.exp(jax.random.uniform(jax.random.fold_in(own, position), (shards_of,), jnp.float32, low / len(shards), high / len(shards)))
        factor_of = factor_of * jnp.repeat(draws, extent[position] // shards_of).reshape([-1 if axis == position else 1 for axis in range(len(extent))])
    return factor_of


def gaussian(stream_key, extent, scale, reach, pieces=(), kind=jnp.bfloat16):
    gain = level_of(stream_key, extent, pieces, -0.22, 0.18) if pieces else 1.0
    entries = jax.random.normal(stream_key, extent, jnp.float32) * scale * gain
    return jnp.minimum(jnp.maximum(entries, -reach), reach).astype(kind)


def setup_inputs(seed: int = 0) -> dict:
    keys = jax.random.split(jax.random.key(seed), 19)
    return {
        "hidden_in": gaussian(keys[0], (ROWS, L, D), 1.0, 6.0, ((0, 8), (1, 4))),
        "doc_starts": draw_doc_starts(jax.random.fold_in(keys[18], 71), 0),
        "grad_out": gaussian(keys[2], (ROWS, L, D), 1.0, 6.0, ((0, 8), (1, 4)), jnp.float32),
        "qkv_weight": gaussian(keys[3], (D, 3, HIDQ), D ** -0.5, 0.1875, ((0, 2), (2, 4)), jnp.float32),
        "output_weight": gaussian(keys[4], (HIDQ, D), (2 * D // HALF) ** -0.5, 1.0, ((0, 4), (1, 2)), jnp.float32),
        "geglu_weight": gaussian(keys[5], (D, 2, FF), D ** -0.5, 0.1875, ((0, 2), (2, 4)), jnp.float32),
        "down_weight": gaussian(keys[6], (FF, D), FF ** -0.5, 0.125, ((0, 4), (1, 2)), jnp.float32),
        "norm_gains": jnp.clip(1.0 + 0.1 * jax.random.normal(keys[7], (2, D), jnp.float32), 0.5, 1.5),
        "qkv_momentum": gaussian(keys[8], (D, 3, HIDQ), (0.055 * TOKENS ** 0.5), 40.0, ((0, 2), (2, 4)), jnp.float32),
        "qkv_variance": jnp.clip(jnp.exp(math.log(671.744) - 2.7580606 * jax.random.uniform(keys[9], (D, 3, HIDQ), jnp.float32) ** level_of(keys[9], (D, 3, HIDQ), ((0, 2), (2, 4)), -0.2, 0.2)), 42.5984, 671.744),
        "output_momentum": gaussian(keys[10], (HIDQ, D), (0.017 * TOKENS ** 0.5), 6.0, ((0, 4), (1, 2)), jnp.float32),
        "output_variance": jnp.clip(jnp.exp(math.log(60.6208) - 2.7780088 * jax.random.uniform(keys[11], (HIDQ, D), jnp.float32) ** level_of(keys[11], (HIDQ, D), ((0, 4), (1, 2)), -0.2, 0.2)), 3.76832, 60.6208),
        "geglu_momentum": gaussian(keys[12], (D, 2, FF), (0.041 * TOKENS ** 0.5), 32.0, ((0, 2), (2, 4)), jnp.float32),
        "geglu_variance": jnp.clip(jnp.exp(math.log(360.448) - 2.7545702 * jax.random.uniform(keys[13], (D, 2, FF), jnp.float32) ** level_of(keys[13], (D, 2, FF), ((0, 2), (2, 4)), -0.2, 0.2)), 22.9376, 360.448),
        "down_momentum": gaussian(keys[14], (FF, D), (0.072 * TOKENS ** 0.5), 56.0, ((0, 4), (1, 2)), jnp.float32),
        "down_variance": jnp.clip(jnp.exp(math.log(1130.496) - 2.7754914 * jax.random.uniform(keys[15], (FF, D), jnp.float32) ** level_of(keys[15], (FF, D), ((0, 4), (1, 2)), -0.2, 0.2)), 70.4512, 1130.496),
        "gains_momentum": gaussian(keys[16], (2, D), (0.094 * TOKENS ** 0.5), 64.0, ((1, 2),), jnp.float32),
        "gains_variance": jnp.clip(jnp.exp(math.log(1933.312) - 2.7692046 * jax.random.uniform(keys[17], (2, D), jnp.float32) ** level_of(keys[17], (2, D), ((1, 2),), -0.2, 0.2)), 121.2416, 1933.312),
    }


@jax.custom_vjp
def low(v):
    return lax.optimization_barrier(v.astype(jnp.bfloat16)).astype(jnp.float32)

@jax.custom_vjp
def low_back(v):
    return v

def low_keep(v):
    return (low(v), None)

def low_pass(kept, grad):
    return (grad,)

def back_keep(v):
    return (v, None)

def back_low(kept, grad):
    return (low(grad),)
low.defvjp(low_keep, low_pass)
low_back.defvjp(back_keep, back_low)
theta_base = 10000.0
norm_eps = 1e-05
beta_first = 0.9
beta_second = 0.98
adam_eps = 1e-06
decay_rate = 1e-05
rate_qkv = 0.06
rate_output = 0.35
rate_geglu = 0.06
rate_down = 0.04
rate_gains = 0.5
masked_value = -1e+30
HIGH = lax.Precision.HIGHEST

def layer_norm(values, gain_vec):
    centered = values - lax.optimization_barrier(jnp.mean(values, axis=-1, keepdims=True))
    spread = lax.optimization_barrier(jnp.mean(centered * centered, axis=-1, keepdims=True))
    return centered * lax.rsqrt(spread + norm_eps) * gain_vec

def doc_tables(starts, places):
    inside = (places >= 0) & (places < L)
    before = starts[..., None, :] <= places[..., :, None]
    number = lax.optimization_barrier(jnp.sum(before.astype(jnp.int32), axis=-1)) - 1
    begins = lax.optimization_barrier(jnp.max(jnp.where(before, starts[..., None, :], 0), axis=-1))
    return (jnp.where(inside, number, -1).astype(jnp.int32), (places - begins).astype(jnp.int32))

def rotate(values, places, direction):
    half_len = values.shape[-1] // 2
    inverse = theta_base ** (-2.0 * jnp.arange(half_len, dtype=jnp.float32) / values.shape[-1])
    angles = places.astype(jnp.float32)[..., None] * inverse
    cosine = jnp.cos(angles)[..., None, :]
    sine_part = direction * jnp.sin(angles)[..., None, :]
    first_half = values[..., :half_len]
    second_half = values[..., half_len:]
    return jnp.concatenate([first_half * cosine - second_half * sine_part, second_half * cosine + first_half * sine_part], axis=-1)

def row_attention(members):
    queries, key_rows, value_rows, starts = members
    seg_len = L // N_CTX
    window = seg_len + 2 * HALF
    blocks = L // seg_len
    scaling = 1.0 / math.sqrt(HD)
    pad_keys = jnp.pad(key_rows, ((HALF, HALF), (0, 0), (0, 0)))
    pad_values = jnp.pad(value_rows, ((HALF, HALF), (0, 0), (0, 0)))
    window_index = (jnp.arange(blocks) * seg_len)[:, None] + jnp.arange(window)[None, :]
    key_blocks = pad_keys[window_index]
    value_blocks = pad_values[window_index]
    query_blocks = queries.reshape(blocks, seg_len, HEADS, HD)
    query_places = jnp.arange(L).reshape(blocks, seg_len)
    key_places = window_index - HALF
    query_doc, unused_one = doc_tables(starts, query_places.reshape(-1))
    key_doc, unused_two = doc_tables(starts, key_places.reshape(-1))
    query_doc = query_doc.reshape(blocks, seg_len)
    key_doc = key_doc.reshape(blocks, window)
    allowed = (jnp.abs(query_places[:, :, None] - key_places[:, None, :]) <= HALF) & (query_doc[:, :, None] == key_doc[:, None, :])
    scores = low_back(jnp.einsum('bqhd,bkhd->bhqk', query_blocks, key_blocks, precision=HIGH) * scaling)
    masked = jnp.where(allowed[:, None], scores, masked_value)
    row_top = lax.optimization_barrier(jnp.max(masked, axis=-1, keepdims=True))
    weights = jnp.exp(masked - row_top)
    chances = weights / lax.optimization_barrier(jnp.sum(weights, axis=-1, keepdims=True))
    mixture = jnp.einsum('bhqk,bkhd->bqhd', low(chances), value_blocks, precision=HIGH)
    return mixture.reshape(L, HEADS * HD)

def forward(hidden, qkv_weight, output_weight, geglu_weight, down_weight, norm_gains, doc_starts):
    qkv_low = low(qkv_weight)
    output_low = low(output_weight)
    geglu_low = low(geglu_weight)
    down_low = low(down_weight)
    gains_low = low(norm_gains)
    row_count = hidden.shape[0]
    flat_rows = hidden.reshape(row_count * L, D)
    normed = low(layer_norm(flat_rows, gains_low[0]))
    mixed_qkv = low_back(jnp.dot(normed, qkv_low.reshape(D, 3 * HEADS * HD), precision=HIGH))
    mixed_qkv = mixed_qkv.reshape(row_count, L, 3, HEADS, HD)
    unused_doc, places = doc_tables(doc_starts, jnp.arange(L))
    queries = low(rotate(mixed_qkv[:, :, 0], places, 1.0))
    key_rows = low(rotate(mixed_qkv[:, :, 1], places, 1.0))
    value_rows = low(mixed_qkv[:, :, 2])
    attended = lax.map(jax.checkpoint(row_attention), (queries, key_rows, value_rows, doc_starts))
    attended = low(low_back(attended.reshape(row_count * L, HEADS * HD)))
    branch = low_back(jnp.dot(attended, output_low, precision=HIGH))
    middle = flat_rows + branch
    normed_two = low(layer_norm(middle, gains_low[1]))
    gate_up = low_back(jnp.dot(normed_two, geglu_low.reshape(D, 2 * FF), precision=HIGH)).reshape(-1, 2, FF)
    inner_act = low(jax.nn.gelu(gate_up[:, 0], approximate=False) * gate_up[:, 1])
    result = middle + low_back(jnp.dot(inner_act, down_low, precision=HIGH))
    return result.reshape(row_count, L, D)

def adam(weight, momentum, variance, gradient, step_rate, shrink_rate):
    momentum_new = beta_first * momentum + (1.0 - beta_first) * gradient
    variance_new = beta_second * variance + (1.0 - beta_second) * gradient * gradient
    first_hat = momentum_new / (1.0 - beta_first ** STEP)
    second_hat = variance_new / (1.0 - beta_second ** STEP)
    updated = weight - step_rate * (first_hat / (jnp.sqrt(second_hat) + adam_eps) + shrink_rate * weight)
    return (updated, momentum_new, variance_new)

def reference(hidden_in, doc_starts, grad_out, qkv_weight, output_weight, geglu_weight, down_weight, norm_gains, qkv_momentum, qkv_variance, output_momentum, output_variance, geglu_momentum, geglu_variance, down_momentum, down_variance, gains_momentum, gains_variance):
    hidden = hidden_in.astype(jnp.float32)
    result, pullback = jax.vjp(partial(forward, doc_starts=doc_starts), hidden, qkv_weight, output_weight, geglu_weight, down_weight, norm_gains)
    gradients = pullback(grad_out)
    qkv_set = adam(qkv_weight, qkv_momentum, qkv_variance, gradients[1], rate_qkv, decay_rate)
    output_set = adam(output_weight, output_momentum, output_variance, gradients[2], rate_output, decay_rate)
    geglu_set = adam(geglu_weight, geglu_momentum, geglu_variance, gradients[3], rate_geglu, decay_rate)
    down_set = adam(down_weight, down_momentum, down_variance, gradients[4], rate_down, decay_rate)
    gains_set = adam(norm_gains, gains_momentum, gains_variance, gradients[5], rate_gains, 0.0)
    return (result.astype(jnp.bfloat16), gradients[0], qkv_set[0], qkv_set[1], qkv_set[2], output_set[0], output_set[1], output_set[2], geglu_set[0], geglu_set[1], geglu_set[2], down_set[0], down_set[1], down_set[2], gains_set[0], gains_set[1], gains_set[2])
```

```python
import functools
import math

import jax
import jax.numpy as jnp
from jax import lax
from jax.experimental import pallas as pl
from jax.experimental.pallas import tpu as pltpu
from jax.sharding import PartitionSpec as P

HD = 64
HALF = 64
L = 1024
STEP = 10
PAIR = 2 * HD
QBLOCK = 128
KBLOCK = QBLOCK + 2 * HALF

theta_base = 10000.0
norm_eps = 1e-05
beta_first = 0.9
beta_second = 0.98
adam_eps = 1e-06
decay_rate = 1e-05
rate_qkv = 0.06
rate_output = 0.35
rate_geglu = 0.06
rate_down = 0.04
rate_gains = 0.5
masked_value = -1e30

low = jnp.bfloat16
wide = jnp.float32
SCALING = 1.0 / math.sqrt(HD)
VMEM = 40 * 1024 * 1024

CORE_SWAP = [(0, 1), (1, 0), (2, 3), (3, 2)]
CHIP_SWAP = [(0, 2), (2, 0), (1, 3), (3, 1)]


def core_swap(values):
    return lax.ppermute(values, "tp", CORE_SWAP)


def chip_swap(values):
    return lax.ppermute(values, "tp", CHIP_SWAP)


def shard_swap(values):
    return lax.ppermute(values, "shard", [(0, 1), (1, 0)])


def dot(a, b):
    return lax.dot_general(a, b, (((1,), (0,)), ((), ())), preferred_element_type=wide)


def dot_nt(a, b):
    return lax.dot_general(a, b, (((1,), (1,)), ((), ())), preferred_element_type=wide)


def dot_tn(a, b):
    return lax.dot_general(a, b, (((0,), (0,)), ((), ())), preferred_element_type=wide)


def normalized(values):
    centered = values - jnp.mean(values, axis=-1, keepdims=True)
    spread = jnp.mean(centered * centered, axis=-1, keepdims=True)
    inverse = lax.rsqrt(spread + norm_eps)
    return centered * inverse, inverse


def norm_back(values, gain, cotangent):
    unit, inverse = normalized(values)
    scaled = cotangent * gain
    first = jnp.mean(scaled, axis=-1, keepdims=True)
    second = jnp.mean(scaled * unit, axis=-1, keepdims=True)
    gain_part = jnp.sum(cotangent * unit, axis=0, keepdims=True)
    return (scaled - first - unit * second) * inverse, gain_part


def turned(values, cosine, sine):
    half_len = HD // 2
    lane = lax.broadcasted_iota(jnp.int32, values.shape, 1)
    ahead = pltpu.roll(values, PAIR - half_len, 1)
    behind = pltpu.roll(values, half_len, 1)
    other = jnp.where(lane % HD < half_len, ahead, behind)
    return values * cosine + other * sine


def head_stack(values):
    lane = lax.broadcasted_iota(jnp.int32, values.shape, 1)
    zero = jnp.zeros_like(values)
    return jnp.concatenate(
        [jnp.where(lane < HD, values, zero), jnp.where(lane < HD, zero, values)], axis=0
    )


def head_join(values):
    rows = values.shape[0] // 2
    upper, lower = values[:rows], values[rows:]
    lane = lax.broadcasted_iota(jnp.int32, upper.shape, 1)
    return jnp.where(lane < HD, upper, lower)


def chances_of(query_stack, keys, bias):
    scores = dot_nt(query_stack, keys) * SCALING + jnp.concatenate([bias, bias], axis=0)
    weights = jnp.exp(scores - jnp.max(scores, axis=-1, keepdims=True))
    return weights * (1.0 / jnp.sum(weights, axis=-1, keepdims=True))


def halves(ref_values, place, half):
    mine = pl.ds(pl.multiple_of(place * half, half), half)
    theirs = pl.ds(pl.multiple_of((1 - place) * half, half), half)
    return mine, theirs


def first_norm_kernel(before_ref, here_ref, after_ref, gain_ref, out_ref, turned_ref):
    tokens = [ref[...].astype(wide) for ref in (before_ref, here_ref, after_ref)]
    normed = normalized(jnp.concatenate(tokens, axis=0))[0] * gain_ref[...]
    out_ref[...] = normed.astype(low)
    turned_ref[...] = normed.T.astype(low)


def attend_kernel(
    place_ref, normed_ref, mine_ref, theirs_ref, cos_ref, sin_ref, bias_ref,
    query_ref, key_ref, value_ref, out_ref,
):
    seg_len = query_ref.shape[0]
    half = mine_ref.shape[1]
    mine, theirs = halves(normed_ref, place_ref[0], half)
    inner = slice(HALF, HALF + seg_len)

    def project(which, rows):
        return dot(normed_ref[rows, mine], mine_ref[which]) + dot(
            normed_ref[rows, theirs], theirs_ref[which]
        )

    whole = slice(0, normed_ref.shape[0])
    queries, keys = project(0, inner), project(1, whole)
    value_ref[...] = project(2, whole).astype(low)
    for first in range(0, query_ref.shape[1], PAIR):
        lanes = slice(first, first + PAIR)
        query_ref[:, lanes] = turned(queries[:, lanes], cos_ref[inner], sin_ref[inner]).astype(low)
        key_ref[:, lanes] = turned(keys[:, lanes], cos_ref[...], sin_ref[...]).astype(low)
    for first in range(0, query_ref.shape[1], PAIR):
        lanes = slice(first, first + PAIR)
        for block in range(seg_len // QBLOCK):
            rows = slice(block * QBLOCK, block * QBLOCK + QBLOCK)
            reach = slice(block * QBLOCK, block * QBLOCK + KBLOCK)
            chances = chances_of(head_stack(query_ref[rows, lanes]), key_ref[reach, lanes], bias_ref[block])
            out_ref[rows, lanes] = head_join(dot(chances.astype(low), value_ref[reach, lanes])).astype(low)


def attend_back_kernel(
    place_ref, grad_ref, grad_turned_ref, normed_ref, attended_ref, mine_ref, theirs_ref,
    query_ref, key_ref, value_ref, cos_ref, sin_ref, bias_ref,
    mixed_ref, own_ref, far_ref, key_sum, value_sum, weight_sum,
):
    seg_len = query_ref.shape[0]
    half = mine_ref.shape[0]
    mine, theirs = halves(grad_ref, place_ref[0], half)
    inner = slice(HALF, HALF + seg_len)
    grad_out = (
        dot(grad_ref[:, mine], mine_ref[...]) + dot(grad_ref[:, theirs], theirs_ref[...])
    ).astype(low)
    key_sum[...] = jnp.zeros_like(key_sum)
    value_sum[...] = jnp.zeros_like(value_sum)
    edge = jnp.zeros((HALF, query_ref.shape[1]), low)
    mixed_ref[0, :HALF] = edge
    mixed_ref[0, HALF + seg_len :] = edge
    for first in range(0, query_ref.shape[1], PAIR):
        lanes = slice(first, first + PAIR)
        for block in range(seg_len // QBLOCK):
            rows = slice(block * QBLOCK, block * QBLOCK + QBLOCK)
            reach = slice(block * QBLOCK, block * QBLOCK + KBLOCK)
            place_rows = slice(HALF + block * QBLOCK, HALF + block * QBLOCK + QBLOCK)
            queries = head_stack(query_ref[rows, lanes])
            grads = head_stack(grad_out[rows, lanes])
            keys, values = key_ref[reach, lanes], value_ref[reach, lanes]
            chances = chances_of(queries, keys, bias_ref[block])
            grad_chances = dot_nt(grads, values)
            weighted = chances * grad_chances
            grad_scores = (
                weighted - chances * jnp.sum(weighted, axis=-1, keepdims=True)
            ).astype(low)
            value_sum[reach, lanes] += dot_tn(chances.astype(low), grads)
            key_sum[reach, lanes] += dot_tn(grad_scores, queries)
            grad_queries = head_join(dot(grad_scores, keys)) * SCALING
            mixed_ref[0, place_rows, lanes] = turned(
                grad_queries, cos_ref[place_rows], -sin_ref[place_rows]
            ).astype(low)
        mixed_ref[1, :, lanes] = turned(
            key_sum[:, lanes] * SCALING, cos_ref[...], -sin_ref[...]
        ).astype(low)
    mixed_ref[2] = value_sum[...].astype(low)

    parts = []
    for lanes in (mine, theirs):
        parts += [dot(normed_ref[lanes], mixed_ref[which]) for which in range(3)]
        parts.append(dot(grad_turned_ref[lanes], attended_ref[...]))

    @pl.when(pl.program_id(0) == 0)
    def _():
        for index, part in enumerate(parts):
            weight_sum[index] = part

    @pl.when(pl.program_id(0) > 0)
    def _():
        for index, part in enumerate(parts):
            weight_sum[index] += part

    @pl.when(pl.program_id(0) == pl.num_programs(0) - 1)
    def _():
        for index in range(4):
            own_ref[index] = weight_sum[index].astype(low)
            far_ref[index] = weight_sum[4 + index].astype(low)


def second_norm_kernel(place_ref, *refs):
    group = (len(refs) - 4) // 3
    attended, mine_refs, theirs_refs = refs[:group], refs[group : 2 * group], refs[2 * group : 3 * group]
    hidden_ref, gain_ref, middle_ref, normed_ref = refs[3 * group :]
    half = mine_refs[0].shape[0]
    mine, theirs = halves(middle_ref, place_ref[0], half)
    for lanes, weights in ((mine, mine_refs), (theirs, theirs_refs)):
        total = hidden_ref[:, lanes].astype(wide)
        for one, weight in zip(attended, weights):
            total += dot_nt(one[...], weight[...])
        middle_ref[:, lanes] = total
    normed_ref[...] = (normalized(middle_ref[...])[0] * gain_ref[...]).astype(low)


def feed_kernel(place_ref, *refs):
    group = (len(refs) - 4) // 5
    tokens, grads = refs[:group], refs[group : 2 * group]
    mine_ref, theirs_ref, down_mine_ref, down_theirs_ref = refs[2 * group : 2 * group + 4]
    outs = refs[2 * group + 4 :]
    half = mine_ref.shape[1]
    units = down_mine_ref.shape[0]
    mine, theirs = halves(mine_ref, place_ref[0], half)
    for index in range(group):
        normed_ref, grad_ref = tokens[index], grads[index]
        act_ref, out_ref, back_ref = outs[3 * index : 3 * index + 3]
        own, far = normed_ref[:, mine], normed_ref[:, theirs]
        gate = dot_nt(own, mine_ref[:units]) + dot_nt(far, theirs_ref[:units])
        up = dot_nt(own, mine_ref[units:]) + dot_nt(far, theirs_ref[units:])
        grad_inner = dot_nt(grad_ref[:, mine], down_mine_ref[...]) + dot_nt(
            grad_ref[:, theirs], down_theirs_ref[...]
        )
        normal = 0.5 * (1.0 + lax.erf(gate * math.sqrt(0.5)))
        density = jnp.exp(-0.5 * gate * gate) * (1.0 / math.sqrt(2.0 * math.pi))
        gelu = gate * normal
        inner = (gelu * up).astype(low)
        grad_gate = (grad_inner * up * (normal + gate * density)).astype(low)
        grad_up = (grad_inner * gelu).astype(low)
        act_ref[0] = grad_gate
        act_ref[1] = grad_up
        act_ref[2] = inner
        for lanes, weight, down in (
            (mine, mine_ref, down_mine_ref), (theirs, theirs_ref, down_theirs_ref)
        ):
            back_ref[:, lanes] = (
                dot(grad_gate, weight[:units]) + dot(grad_up, weight[units:])
            ).astype(low)
            out_ref[:, lanes] = dot(inner, down[...]).astype(low)


def update(weight, momentum, variance, gradient, rate):
    momentum_new = beta_first * momentum + (1.0 - beta_first) * gradient
    variance_new = beta_second * variance + (1.0 - beta_second) * gradient * gradient
    first_hat = momentum_new * (1.0 / (1.0 - beta_first**STEP))
    second_hat = variance_new * (1.0 / (1.0 - beta_second**STEP))
    new = weight - rate * (first_hat / (jnp.sqrt(second_hat) + adam_eps) + decay_rate * weight)
    return new, momentum_new, variance_new


def update_kernel(rate, flip, by_half, count, *refs):
    which = pl.program_id(1) if by_half else 0
    state, outs = refs[count : count + 3], refs[count + 3 :]
    for index in range(count):

        @pl.when(which == index)
        def _():
            gradient = refs[index][...].astype(wide)
            if flip:
                gradient = gradient.T
            for out, value in zip(outs, update(*(one[...] for one in state), gradient, rate)):
                out[...] = value


def run_update(name, rate, pieces, state, skip, flip, by_half):
    dim = 1 if flip else 0
    size = list(state[0].shape[1:])
    size[dim] //= 2
    if size[0] % 8 or size[1] % 128:
        if by_half:
            gradient = jnp.concatenate(pieces, axis=1)[skip : skip + state[0].shape[0]]
        else:
            gradient = pieces[0]
        gradient = gradient.astype(wide)
        if flip:
            gradient = jnp.transpose(gradient, (0, 2, 1))
        return update(*state, gradient, rate)

    def place(c, h):
        return (c, h, 0) if dim == 0 else (c, 0, h)

    spec = pl.BlockSpec((None, *size), place)
    grad_spec = spec
    if by_half:
        cut = size[::-1] if flip else size
        grad_spec = pl.BlockSpec((None, *cut), lambda c, h: (c + skip, 0, 0))
    return pl.pallas_call(
        functools.partial(update_kernel, rate, flip, by_half, len(pieces)),
        grid=(state[0].shape[0], 2),
        in_specs=[grad_spec] * len(pieces) + [spec] * 3,
        out_specs=[spec] * 3,
        out_shape=[jax.ShapeDtypeStruct(state[0].shape, wide)] * 3,
        name=name,
        compiler_params=pltpu.CompilerParams(vmem_limit_bytes=VMEM),
        cost_estimate=pl.CostEstimate(flops=1000, bytes_accessed=1000, transcendentals=0),
    )(*pieces, *state)


def feed_weights_kernel(place_ref, *refs):
    group = (len(refs) - 3) // 3
    acts, tokens, grads = refs[:group], refs[group : 2 * group], refs[2 * group : 3 * group]
    own_ref, *far_refs = refs[3 * group :]
    half = own_ref.shape[-1]
    mine, theirs = halves(own_ref, place_ref[0], half)

    for step, rights in enumerate((tokens, tokens, grads)):

        @pl.when(pl.program_id(0) == step)
        def _():
            far_ref = far_refs[0].at[step] if step < 2 else far_refs[1]
            for out, lanes in ((own_ref, mine), (far_ref, theirs)):
                total = None
                for act, right in zip(acts, rights):
                    for row in range(act.shape[0]):
                        part = dot_tn(act[row], right[row, :, lanes])
                        total = part if total is None else total + part
                out[...] = total.astype(low)


def middle_back_kernel(
    one_ref, two_ref, three_ref, middle_ref, gain_ref, grad_ref,
    out_ref, low_ref, turned_ref, gain_out_ref,
):
    cotangent = one_ref[...].astype(wide) + two_ref[...].astype(wide) + three_ref[...].astype(wide)
    back, gain_part = norm_back(middle_ref[...], gain_ref[...], cotangent)
    total = grad_ref[...] + back
    out_ref[...] = total
    low_ref[...] = total.astype(low)
    turned_ref[...] = total.T.astype(low)
    gain_out_ref[...] = gain_part


def normed_grad_kernel(place_ref, *refs):
    group = (len(refs) - 1) // 3
    grads, mine_refs, theirs_refs = refs[:group], refs[group : 2 * group], refs[2 * group : 3 * group]
    out_ref = refs[-1]
    half = mine_refs[0].shape[1]
    mine, theirs = halves(out_ref, place_ref[0], half)
    for lanes, weights in ((mine, mine_refs), (theirs, theirs_refs)):
        total = None
        for grad, weight in zip(grads, weights):
            for which in range(3):
                part = dot_nt(grad[which], weight[which])
                total = part if total is None else total + part
        out_ref[:, lanes] = total


def input_back_kernel(
    here_ref, before_ref, after_ref, hidden_ref, gain_ref, grad_ref, out_ref, gain_out_ref
):
    seg_len = hidden_ref.shape[0]
    gain = gain_ref[...]
    hidden = hidden_ref[...].astype(wide)
    centre = here_ref[HALF : HALF + seg_len]
    cotangent = jnp.concatenate(
        [
            centre[:HALF] + before_ref[...].astype(wide),
            centre[HALF : seg_len - HALF],
            centre[seg_len - HALF :] + after_ref[...].astype(wide),
        ],
        axis=0,
    )
    back, gain_part = norm_back(hidden, gain, cotangent)
    out_ref[...] = grad_ref[...] + back
    gain_out_ref[...] = gain_part


def by_row(shape):
    rest = tuple(shape[1:])
    return pl.BlockSpec((None,) + rest, lambda r: (r,) + (0,) * len(rest))


def fixed(shape):
    return pl.BlockSpec(tuple(shape), lambda r: (0,) * len(shape))


def spec_of(values, kind):
    if kind == "row":
        return by_row(values.shape)
    if kind == "second":
        return pl.BlockSpec(
            (values.shape[0], None) + tuple(values.shape[2:]),
            lambda r: (0, r) + (0,) * (len(values.shape) - 2),
        )
    if kind == "step":
        return pl.BlockSpec((None,) + tuple(values.shape[1:]), lambda r: (r, 0, 0, 0))
    if kind == "head":
        return pl.BlockSpec((3,) + tuple(values.shape[1:]), lambda r: (0, 0, 0))
    if kind == "last":
        return pl.BlockSpec((None,) + tuple(values.shape[1:]), lambda r: (3, 0, 0))
    if kind == "scalar":
        return pl.BlockSpec(memory_space=pltpu.SMEM)
    return fixed(values.shape)


def run(kernel, name, steps, ins, outs, scratch=()):
    return pl.pallas_call(
        kernel,
        grid=(steps,),
        in_specs=[spec_of(value, kind) for value, kind in ins],
        out_specs=[spec_of(shape, kind) for shape, kind in outs],
        out_shape=[shape for shape, kind in outs],
        scratch_shapes=list(scratch),
        name=name,
        compiler_params=pltpu.CompilerParams(vmem_limit_bytes=VMEM),
        cost_estimate=pl.CostEstimate(flops=1000, bytes_accessed=1000, transcendentals=0),
    )(*[value for value, kind in ins])


def doc_tables(starts, places):
    inside = (places >= 0) & (places < L)
    before = starts[..., None, :] <= places[..., :, None]
    number = jnp.sum(before.astype(jnp.int32), axis=-1) - 1
    begins = jnp.max(jnp.where(before, starts[..., None, :], 0), axis=-1)
    return (jnp.where(inside, number, -1), places - begins)


def adam(weight, momentum, variance, gradient, step_rate, shrink_rate):
    momentum_new = beta_first * momentum + (1.0 - beta_first) * gradient
    variance_new = beta_second * variance + (1.0 - beta_second) * gradient * gradient
    first_hat = momentum_new / (1.0 - beta_first**STEP)
    second_hat = variance_new / (1.0 - beta_second**STEP)
    updated = weight - step_rate * (
        first_hat / (jnp.sqrt(second_hat) + adam_eps) + shrink_rate * weight
    )
    return (updated, momentum_new, variance_new)


def take(values, index, size, dim):
    return lax.dynamic_slice_in_dim(values, index * size, size, axis=dim)


def joined(bit, mine, theirs, dim):
    return jnp.where(
        bit == 0,
        jnp.concatenate([mine, theirs], axis=dim),
        jnp.concatenate([theirs, mine], axis=dim),
    )


def after(values, *others):
    return lax.optimization_barrier((values,) + others)[0]


def all_after(values, *others):
    return lax.optimization_barrier(tuple(values) + others)[: len(values)]


EVEN = [(0, 1), (1, 0), (2, 3), (3, 2)]
ACROSS = [(0, 2), (2, 0), (1, 3), (3, 1)]


def line_one(values, dim):
    if lax.axis_size("ctx") != 4:
        return values, None
    parity = lax.rem(lax.axis_index("ctx"), 2)
    size = values.shape[dim] // 2
    got = lax.ppermute(take(values, 1 - parity, size, dim), "ctx", EVEN)
    return take(values, parity, size, dim), got


def line_two(kept, got):
    if got is None:
        return kept, None
    part = added(kept, got)
    return part, lax.ppermute(part, "ctx", ACROSS)


def line_three(kept, got):
    if got is None:
        return kept, None
    part = added(kept, got)
    return part, lax.ppermute(part, "ctx", EVEN)


def line_end(kept, got, dim):
    if got is None:
        return lax.psum(kept.astype(wide), "ctx").astype(low)
    return joined(lax.rem(lax.axis_index("ctx"), 2), kept, got, dim)


def line_sum(values, dim):
    return line_end(*line_three(*line_two(*line_one(values, dim))), dim)


def added(*values):
    return sum(value.astype(wide) for value in values).astype(low)


def body(
    hidden_in,
    doc_starts,
    grad_out,
    qkv_weight,
    output_weight,
    geglu_weight,
    down_weight,
    norm_gains,
    qkv_momentum,
    qkv_variance,
    output_momentum,
    output_variance,
    geglu_momentum,
    geglu_variance,
    down_momentum,
    down_variance,
    gains_momentum,
    gains_variance,
):
    rows, seg_len, model_width = hidden_in.shape
    shards = lax.axis_size("shard")
    paired = shards == 2
    half = model_width // 2
    shard_place = lax.axis_index("shard")
    group_place = lax.axis_index("tp")
    ctx_place = lax.axis_index("ctx")
    place = shard_place if paired else jnp.zeros_like(shard_place)
    place_one = place.astype(jnp.int32).reshape(1)
    group = (0, 1, 2, 3)
    span = seg_len + 2 * HALF
    cols = qkv_weight.shape[2]
    units = down_weight.shape[0]

    count = lax.axis_size("ctx")
    forward = [(i, i + 1) for i in range(count - 1)]
    backward = [(i + 1, i) for i in range(count - 1)]
    before = lax.ppermute(hidden_in[:, seg_len - HALF :], "ctx", forward)
    after_edge = lax.ppermute(hidden_in[:, :HALF], "ctx", backward)

    def both(values, dim):
        if paired:
            return values, shard_swap(values)
        full = lax.all_gather(values, "shard", axis=dim, tiled=True)
        return (
            lax.slice_in_dim(full, 0, half, axis=dim),
            lax.slice_in_dim(full, half, 2 * half, axis=dim),
        )

    gains_near = norm_gains.astype(low)
    if paired:
        gains_low = joined(place, gains_near, shard_swap(gains_near), 1)
    else:
        gains_low = lax.all_gather(gains_near, "shard", axis=1, tiled=True)
    gain_one = gains_low[0:1].astype(wide)
    gain_two = gains_low[1:2].astype(wide)

    qkv_turned = jnp.transpose(qkv_weight, (1, 0, 2))
    geglu_turned = jnp.transpose(geglu_weight, (1, 2, 0))
    block_low = jnp.concatenate(
        [qkv_turned.astype(low), jnp.transpose(output_weight).astype(low)[None]], axis=0
    )
    block_low = after(block_low, gains_low)
    mine, theirs = both(block_low, 1)
    geglu_low = after(geglu_turned, before, after_edge).astype(low).reshape(2 * units, -1)
    geglu_mine, geglu_theirs = both(geglu_low, 1)
    down_low = after(down_weight, before, after_edge).astype(low)
    down_mine, down_theirs = both(down_low, 1)

    grad_low = after(grad_out, before, after_edge).astype(low)
    offset = ctx_place * seg_len
    ext_places = offset - HALF + jnp.arange(span, dtype=jnp.int32)
    tp_rows = lax.dynamic_slice_in_dim(doc_starts, group_place * rows, rows, axis=0)
    ext_doc, ext_place = doc_tables(tp_rows, ext_places)
    inverse = theta_base ** (-2.0 * jnp.arange(HD // 2, dtype=wide) / HD)
    angles = ext_place.astype(wide)[..., None] * inverse
    cosine, sine = jnp.cos(angles), jnp.sin(angles)
    cosine = jnp.concatenate([cosine] * 4, axis=-1)
    sine = jnp.concatenate([-sine, sine, -sine, sine], axis=-1)
    blocks = seg_len // QBLOCK
    query_doc = ext_doc[:, HALF : HALF + seg_len].reshape(rows, blocks, QBLOCK)
    key_doc = jnp.stack(
        [ext_doc[:, b * QBLOCK : b * QBLOCK + KBLOCK] for b in range(blocks)], axis=1
    )
    gap = jnp.arange(QBLOCK)[:, None] + HALF - jnp.arange(KBLOCK)[None, :]
    allowed = (jnp.abs(gap) <= HALF) & (query_doc[..., :, None] == key_doc[..., None, :])
    bias = jnp.where(allowed, 0.0, masked_value).astype(wide)

    normed, normed_turned = run(
        first_norm_kernel, "first_norm", rows,
        [(before, "row"), (hidden_in, "row"), (after_edge, "row"), (gain_one, "all")],
        [
            (jax.ShapeDtypeStruct((rows, span, model_width), low), "row"),
            (jax.ShapeDtypeStruct((rows, model_width, span), low), "row"),
        ],
    )

    far_mine = chip_swap(mine)
    near_mine = core_swap(mine)
    theirs = after(theirs, normed, cosine, sine, bias, geglu_low, down_low, grad_low, far_mine)
    far_theirs = chip_swap(theirs)
    weights = [(mine, theirs), (near_mine, core_swap(theirs))]
    scalar = (place_one, "scalar")
    tables = [(cosine, "row"), (sine, "row"), (bias, "row")]
    short = jax.ShapeDtypeStruct((rows, seg_len, cols), low)
    long = jax.ShapeDtypeStruct((rows, span, cols), low)
    saved = []
    for j in group:
        tokens_here = normed if j == 0 else after(normed, saved[j - 1][3])
        if j == 2:
            far_theirs = after(far_theirs, saved[1][3])
            weights.append((far_mine, far_theirs))
            weights.append((core_swap(far_mine), core_swap(far_theirs)))
            grad_far = chip_swap(after(grad_low, far_theirs))
        if j == 3:
            tokens_here = after(tokens_here, geglu_theirs)
        saved.append(
            run(
                attend_kernel, "attend", rows,
                [scalar, (tokens_here, "row"), (weights[j][0], "head"), (weights[j][1], "head")]
                + tables,
                [(short, "row"), (long, "row"), (long, "row"), (short, "row")],
            )
        )
    attended = [one[3] for one in saved]
    attended[3] = after(attended[3], down_theirs)
    middle, normed_two = run(
        second_norm_kernel, "second_norm", rows,
        [scalar]
        + [(one, "row") for one in attended]
        + [(weights[j][0], "last") for j in group]
        + [(weights[j][1], "last") for j in group]
        + [(hidden_in, "row"), (gain_two, "all")],
        [
            (jax.ShapeDtypeStruct((rows, seg_len, model_width), wide), "row"),
            (jax.ShapeDtypeStruct((rows, seg_len, model_width), low), "row"),
        ],
    )

    normed_far = chip_swap(normed_two)
    normed_one = core_swap(normed_two)
    grad_one = core_swap(grad_low)
    act_rows = jax.ShapeDtypeStruct((3, rows, seg_len, units), low)
    full_rows = jax.ShapeDtypeStruct((rows, seg_len, model_width), low)

    def feed(tokens, grads):
        done = run(
            feed_kernel, "feed", rows,
            [scalar]
            + [(one, "row") for one in tokens]
            + [(one, "row") for one in grads]
            + [(one, "all") for one in (geglu_mine, geglu_theirs, down_mine, down_theirs)],
            [(act_rows, "second"), (full_rows, "row"), (full_rows, "row")] * len(tokens),
        )
        return [done[3 * i : 3 * i + 3] for i in range(len(tokens))]

    tokens, grads = [after(normed_two, grad_far), normed_one], [grad_low, grad_one]
    fed = feed(tokens, grads)
    normed_far = after(normed_far, fed[0][2])
    tokens += [normed_far, core_swap(normed_far)]
    grads += [grad_far, core_swap(grad_far)]
    fed += feed(tokens[2:], grads[2:])
    back_three = core_swap(fed[3][2])
    back_one = core_swap(after(fed[1][2], back_three))
    back_far = chip_swap(added(fed[2][2], back_three))
    out_one = core_swap(after(fed[1][1], back_one))
    out_three = core_swap(after(fed[3][1], back_one))

    feed_part = jax.ShapeDtypeStruct((3, units, half), low)
    feed_own, *feed_other = run(
        feed_weights_kernel, "feed_weights", 3,
        [scalar]
        + [(after(fed[0][0], back_three), "step")]
        + [(one[0], "step") for one in fed[1:]]
        + [(one, "all") for one in tokens]
        + [(one, "all") for one in grads],
        [
            (feed_part, "row"),
            (jax.ShapeDtypeStruct((2, units, half), low), "all"),
            (jax.ShapeDtypeStruct((units, half), low), "all"),
        ],
    )

    out_far = chip_swap(after(added(fed[2][1], out_three), feed_own))
    back_far, unused = lax.optimization_barrier((back_far, feed_own))
    gain_shape = jax.ShapeDtypeStruct((rows, 1, model_width), wide)
    grad_middle, middle_low, middle_turned, gain_two_part = run(
        middle_back_kernel, "middle_back", rows,
        [
            (after(fed[0][2], feed_own), "row"), (back_one, "row"), (back_far, "row"),
            (middle, "row"), (gain_two, "all"), (grad_out, "row"),
        ],
        [
            (jax.ShapeDtypeStruct(grad_out.shape, wide), "row"),
            (jax.ShapeDtypeStruct(grad_out.shape, low), "row"),
            (jax.ShapeDtypeStruct((rows, model_width, seg_len), low), "row"),
            (gain_shape, "row"),
        ],
    )

    if paired:
        geglu_got, down_got = [shard_swap(one) for one in feed_other]
    else:
        feed_other[1] = feed_other[1][None]
        feed_got = lax.psum_scatter(
            jnp.concatenate([feed_own, jnp.concatenate(feed_other, axis=0)], axis=2),
            "shard", scatter_dimension=2, tiled=True,
        )
        geglu_got, down_got = feed_got[:2], feed_got[2]

    mixed, own, other = [None] * 4, [None] * 4, [None] * 4
    weight_part = jax.ShapeDtypeStruct((4, half, cols), low)
    def attend_back(j, *before_it):
        queries, keys, values, out = saved[j]
        mixed[j], own[j], other[j] = run(
            attend_back_kernel, "attend_back", rows,
            [
                scalar, (after(middle_low, *before_it), "row"), (middle_turned, "row"),
                (normed_turned, "row"), (out, "row"),
                (weights[j][0], "last"), (weights[j][1], "last"),
                (queries, "row"), (keys, "row"), (values, "row"),
            ]
            + tables,
            [
                (jax.ShapeDtypeStruct((3, rows, span, cols), low), "second"),
                (weight_part, "all"), (weight_part, "all"),
            ],
            scratch=[
                pltpu.VMEM((span, cols), wide), pltpu.VMEM((span, cols), wide),
                pltpu.VMEM((8, half, cols), wide),
            ],
        )

    attend_back(3, back_far)
    far_three, far_other_three = core_swap(own[3]), core_swap(other[3])
    attend_back(2, mixed[3], out_far, out_one)
    far_other = added(other[2], far_other_three)
    far_own = own[2], far_three
    far_got = shard_swap(far_other) if paired else None
    geglu_got = after(geglu_got, mixed[2])
    geglu_part = added(feed_own[:2], geglu_got) if paired else geglu_got
    geglu_line = line_one(geglu_part, 0)
    attend_back(1, mixed[2], geglu_got)
    near_one, near_other_one = core_swap(own[1]), core_swap(other[1])
    geglu_line = line_two(*all_after(geglu_line, mixed[1]))
    down_got = after(down_got, mixed[1])
    down_part = added(feed_own[2], down_got) if paired else down_got
    down_line = line_one(down_part, 1)
    attend_back(0, mixed[1], geglu_line[0], down_got)
    down_line = line_two(*all_after(down_line, mixed[0]))

    (normed_grad,) = run(
        normed_grad_kernel, "normed_grad", rows,
        [scalar]
        + [(after(mixed[0], down_line[0]), "second")]
        + [(mixed[j], "second") for j in group[1:]]
        + [(weights[j][0], "head") for j in group]
        + [(weights[j][1], "head") for j in group],
        [(jax.ShapeDtypeStruct((rows, span, model_width), wide), "row")],
    )
    near_one, near_other_one = all_after((near_one, near_other_one), normed_grad)
    to_before = lax.ppermute(normed_grad[:, :HALF].astype(low), "ctx", backward)
    to_after = lax.ppermute(normed_grad[:, HALF + seg_len :].astype(low), "ctx", forward)

    near_other = added(other[0], near_other_one)
    near_own = own[0], near_one
    cut = half // 2
    near_got = [shard_swap(near_other[:, i * cut : (i + 1) * cut]) for i in (0, 1)] if paired else None
    if paired:
        far_part = added(*far_own, after(far_got, near_other))
    else:
        scatter = functools.partial(
            lax.psum_scatter, axis_name="shard", scatter_dimension=1, tiled=True
        )
        far_part = scatter(jnp.concatenate([added(*far_own), far_other], axis=1))
        near_sum = scatter(jnp.concatenate([added(*near_own), near_other], axis=1))
    far_rows = far_part.shape[1] // 2
    far = [chip_swap(far_part[:, i * far_rows : (i + 1) * far_rows]) for i in (0, 1)]

    to_before, to_after = all_after((to_before, to_after), near_other, far_part)
    grad_in, gain_one_part = run(
        input_back_kernel, "input_back", rows,
        [
            (normed_grad, "row"), (to_after, "row"), (to_before, "row"), (hidden_in, "row"),
            (gain_one, "all"), (grad_middle, "row"),
        ],
        [(jax.ShapeDtypeStruct(grad_out.shape, wide), "row"), (gain_shape, "row")],
    )
    result = middle + fed[0][1].astype(wide) + out_one.astype(wide) + out_far.astype(wide)
    hidden_out = result.astype(low)
    gain_sum = jnp.concatenate(
        [jnp.sum(gain_one_part, axis=0), jnp.sum(gain_two_part, axis=0)], axis=0
    )
    gain_sum = gain_sum + core_swap(gain_sum)
    if lax.axis_size("ctx") == 4:
        gain_sum = gain_sum + lax.ppermute(gain_sum, "ctx", EVEN)
        gain_sum = gain_sum + lax.ppermute(gain_sum, "ctx", ACROSS)
    else:
        gain_sum = lax.psum(gain_sum, "ctx")
    gain_sum = gain_sum + chip_swap(gain_sum)
    gain_sum = gain_sum + shard_swap(gain_sum) if paired else lax.psum(gain_sum, "shard")
    gains_here = norm_gains.shape[1]
    gain_grad = lax.dynamic_slice_in_dim(gain_sum, shard_place * gains_here, gains_here, axis=1)

    def cut_of(index):
        rows_at = slice(index * far_rows, (index + 1) * far_rows)
        if paired:
            return added(*(v[:, rows_at] for v in near_own), near_got[index], far[index])
        return added(near_sum[:, rows_at], far[index])

    geglu_sum = line_end(*line_three(*all_after(geglu_line, grad_in)), 0)
    down_sum = line_end(*line_three(*all_after(down_line, grad_in)), 1)
    block_sums = [line_sum(cut_of(i), 0) for i in (0, 1)]

    def turned_state(axes, *values):
        return [jnp.transpose(v, axes) for v in values]

    def turned_back(axes, values):
        return tuple(jnp.transpose(v, axes) for v in values)

    geglu_set = turned_back(
        (2, 0, 1),
        run_update(
            "update_geglu", rate_geglu, [geglu_sum],
            turned_state((1, 2, 0), geglu_weight, geglu_momentum, geglu_variance), 0, False, False,
        ),
    )
    down_set = tuple(
        v[0]
        for v in run_update(
            "update_down", rate_down, [down_sum[None]],
            [v[None] for v in (down_weight, down_momentum, down_variance)], 0, False, False,
        )
    )
    qkv_set = turned_back(
        (1, 0, 2),
        run_update(
            "update_qkv", rate_qkv, block_sums,
            turned_state((1, 0, 2), qkv_weight, qkv_momentum, qkv_variance), 0, False, True,
        ),
    )
    output_set = tuple(
        v[0]
        for v in run_update(
            "update_output", rate_output, block_sums,
            [v[None] for v in (output_weight, output_momentum, output_variance)], 3, True, True,
        )
    )
    gains_set = adam(norm_gains, gains_momentum, gains_variance, gain_grad, rate_gains, 0.0)
    return (hidden_out, grad_in) + qkv_set + output_set + geglu_set + down_set + gains_set


def solution(mesh):
    tokens = P(("shard", "tp"), "ctx", None)
    split_in = P("shard", None, "tp")
    split_out = P("tp", "shard")
    gains = P(None, "shard")
    return jax.shard_map(
        body,
        mesh=mesh,
        in_specs=(
            (tokens, P("shard", None), tokens, split_in, split_out, split_in, split_out, gains)
            + (split_in, split_in, split_out, split_out)
            + (split_in, split_in, split_out, split_out)
            + (gains, gains)
        ),
        out_specs=(
            (tokens, tokens)
            + (split_in,) * 3
            + (split_out,) * 3
            + (split_in,) * 3
            + (split_out,) * 3
            + (gains,) * 3
        ),
        check_vma=False,
    )
```

```python
import functools
import math

import jax
import jax.numpy as jnp
from jax import lax
from jax.experimental import pallas as pl
from jax.experimental.pallas import tpu as pltpu
from jax.sharding import PartitionSpec as P

HD = 64
HALF = 64
L = 1024
STEP = 10
PAIR = 2 * HD
QBLOCK = 128
KBLOCK = QBLOCK + 2 * HALF

theta_base = 10000.0
norm_eps = 1e-05
beta_first = 0.9
beta_second = 0.98
adam_eps = 1e-06
decay_rate = 1e-05
rate_qkv = 0.06
rate_output = 0.35
rate_geglu = 0.06
rate_down = 0.04
rate_gains = 0.5
masked_value = -1e30

low = jnp.bfloat16
wide = jnp.float32
SCALING = 1.0 / math.sqrt(HD)
VMEM = 40 * 1024 * 1024

CORE_SWAP = [(0, 1), (1, 0), (2, 3), (3, 2)]
CHIP_SWAP = [(0, 2), (2, 0), (1, 3), (3, 1)]


def core_swap(values):
    return lax.ppermute(values, "tp", CORE_SWAP)


def chip_swap(values):
    return lax.ppermute(values, "tp", CHIP_SWAP)


def shard_swap(values):
    return lax.ppermute(values, "shard", [(0, 1), (1, 0)])


def dot(a, b):
    return lax.dot_general(a, b, (((1,), (0,)), ((), ())), preferred_element_type=wide)


def dot_nt(a, b):
    return lax.dot_general(a, b, (((1,), (1,)), ((), ())), preferred_element_type=wide)


def dot_tn(a, b):
    return lax.dot_general(a, b, (((0,), (0,)), ((), ())), preferred_element_type=wide)


def normalized(values):
    centered = values - jnp.mean(values, axis=-1, keepdims=True)
    spread = jnp.mean(centered * centered, axis=-1, keepdims=True)
    inverse = lax.rsqrt(spread + norm_eps)
    return centered * inverse, inverse


def norm_back(values, gain, cotangent):
    unit, inverse = normalized(values)
    scaled = cotangent * gain
    first = jnp.mean(scaled, axis=-1, keepdims=True)
    second = jnp.mean(scaled * unit, axis=-1, keepdims=True)
    gain_part = jnp.sum(cotangent * unit, axis=0, keepdims=True)
    return (scaled - first - unit * second) * inverse, gain_part


def turned(values, cosine, sine):
    half_len = HD // 2
    lane = lax.broadcasted_iota(jnp.int32, values.shape, 1)
    ahead = pltpu.roll(values, PAIR - half_len, 1)
    behind = pltpu.roll(values, half_len, 1)
    other = jnp.where(lane % HD < half_len, ahead, behind)
    return values * cosine + other * sine


def head_stack(values):
    lane = lax.broadcasted_iota(jnp.int32, values.shape, 1)
    zero = jnp.zeros_like(values)
    return jnp.concatenate(
        [jnp.where(lane < HD, values, zero), jnp.where(lane < HD, zero, values)], axis=0
    )


def head_join(values):
    rows = values.shape[0] // 2
    upper, lower = values[:rows], values[rows:]
    lane = lax.broadcasted_iota(jnp.int32, upper.shape, 1)
    return jnp.where(lane < HD, upper, lower)


def chances_of(query_stack, keys, bias):
    scores = dot_nt(query_stack, keys) * SCALING + jnp.concatenate([bias, bias], axis=0)
    weights = jnp.exp(scores - jnp.max(scores, axis=-1, keepdims=True))
    return weights * (1.0 / jnp.sum(weights, axis=-1, keepdims=True))


def halves(ref_values, place, half):
    mine = pl.ds(pl.multiple_of(place * half, half), half)
    theirs = pl.ds(pl.multiple_of((1 - place) * half, half), half)
    return mine, theirs


def first_norm_kernel(before_ref, here_ref, after_ref, gain_ref, out_ref, turned_ref):
    tokens = [ref[...].astype(wide) for ref in (before_ref, here_ref, after_ref)]
    normed = normalized(jnp.concatenate(tokens, axis=0))[0] * gain_ref[...]
    out_ref[...] = normed.astype(low)
    turned_ref[...] = normed.T.astype(low)


def attend_kernel(
    place_ref, normed_ref, mine_ref, theirs_ref, cos_ref, sin_ref, bias_ref,
    query_ref, key_ref, value_ref, out_ref,
):
    seg_len = query_ref.shape[0]
    half = mine_ref.shape[1]
    mine, theirs = halves(normed_ref, place_ref[0], half)
    inner = slice(HALF, HALF + seg_len)

    def project(which, rows):
        return dot(normed_ref[rows, mine], mine_ref[which]) + dot(
            normed_ref[rows, theirs], theirs_ref[which]
        )

    whole = slice(0, normed_ref.shape[0])
    queries, keys = project(0, inner), project(1, whole)
    value_ref[...] = project(2, whole).astype(low)
    for first in range(0, query_ref.shape[1], PAIR):
        lanes = slice(first, first + PAIR)
        query_ref[:, lanes] = turned(queries[:, lanes], cos_ref[inner], sin_ref[inner]).astype(low)
        key_ref[:, lanes] = turned(keys[:, lanes], cos_ref[...], sin_ref[...]).astype(low)
    for first in range(0, query_ref.shape[1], PAIR):
        lanes = slice(first, first + PAIR)
        for block in range(seg_len // QBLOCK):
            rows = slice(block * QBLOCK, block * QBLOCK + QBLOCK)
            reach = slice(block * QBLOCK, block * QBLOCK + KBLOCK)
            chances = chances_of(head_stack(query_ref[rows, lanes]), key_ref[reach, lanes], bias_ref[block])
            out_ref[rows, lanes] = head_join(dot(chances.astype(low), value_ref[reach, lanes])).astype(low)


def attend_back_kernel(
    place_ref, grad_ref, grad_turned_ref, normed_ref, attended_ref, mine_ref, theirs_ref,
    query_ref, key_ref, value_ref, cos_ref, sin_ref, bias_ref,
    mixed_ref, own_ref, far_ref, key_sum, value_sum, weight_sum,
):
    seg_len = query_ref.shape[0]
    half = mine_ref.shape[0]
    mine, theirs = halves(grad_ref, place_ref[0], half)
    inner = slice(HALF, HALF + seg_len)
    grad_out = (
        dot(grad_ref[:, mine], mine_ref[...]) + dot(grad_ref[:, theirs], theirs_ref[...])
    ).astype(low)
    key_sum[...] = jnp.zeros_like(key_sum)
    value_sum[...] = jnp.zeros_like(value_sum)
    edge = jnp.zeros((HALF, query_ref.shape[1]), low)
    mixed_ref[0, :HALF] = edge
    mixed_ref[0, HALF + seg_len :] = edge
    for first in range(0, query_ref.shape[1], PAIR):
        lanes = slice(first, first + PAIR)
        for block in range(seg_len // QBLOCK):
            rows = slice(block * QBLOCK, block * QBLOCK + QBLOCK)
            reach = slice(block * QBLOCK, block * QBLOCK + KBLOCK)
            place_rows = slice(HALF + block * QBLOCK, HALF + block * QBLOCK + QBLOCK)
            queries = head_stack(query_ref[rows, lanes])
            grads = head_stack(grad_out[rows, lanes])
            keys, values = key_ref[reach, lanes], value_ref[reach, lanes]
            chances = chances_of(queries, keys, bias_ref[block])
            grad_chances = dot_nt(grads, values)
            weighted = chances * grad_chances
            grad_scores = (
                weighted - chances * jnp.sum(weighted, axis=-1, keepdims=True)
            ).astype(low)
            value_sum[reach, lanes] += dot_tn(chances.astype(low), grads)
            key_sum[reach, lanes] += dot_tn(grad_scores, queries)
            grad_queries = head_join(dot(grad_scores, keys)) * SCALING
            mixed_ref[0, place_rows, lanes] = turned(
                grad_queries, cos_ref[place_rows], -sin_ref[place_rows]
            ).astype(low)
        mixed_ref[1, :, lanes] = turned(
            key_sum[:, lanes] * SCALING, cos_ref[...], -sin_ref[...]
        ).astype(low)
    mixed_ref[2] = value_sum[...].astype(low)

    parts = []
    for lanes in (mine, theirs):
        parts += [dot(normed_ref[lanes], mixed_ref[which]) for which in range(3)]
        parts.append(dot(grad_turned_ref[lanes], attended_ref[...]))

    @pl.when(pl.program_id(0) == 0)
    def _():
        for index, part in enumerate(parts):
            weight_sum[index] = part

    @pl.when(pl.program_id(0) > 0)
    def _():
        for index, part in enumerate(parts):
            weight_sum[index] += part

    @pl.when(pl.program_id(0) == pl.num_programs(0) - 1)
    def _():
        for index in range(4):
            own_ref[index] = weight_sum[index].astype(low)
            far_ref[index] = weight_sum[4 + index].astype(low)


def second_norm_kernel(place_ref, *refs):
    group = (len(refs) - 4) // 3
    attended, mine_refs, theirs_refs = refs[:group], refs[group : 2 * group], refs[2 * group : 3 * group]
    hidden_ref, gain_ref, middle_ref, normed_ref = refs[3 * group :]
    half = mine_refs[0].shape[0]
    mine, theirs = halves(middle_ref, place_ref[0], half)
    for lanes, weights in ((mine, mine_refs), (theirs, theirs_refs)):
        total = hidden_ref[:, lanes].astype(wide)
        for one, weight in zip(attended, weights):
            total += dot_nt(one[...], weight[...])
        middle_ref[:, lanes] = total
    normed_ref[...] = (normalized(middle_ref[...])[0] * gain_ref[...]).astype(low)


def feed_kernel(place_ref, *refs):
    group = (len(refs) - 4) // 5
    tokens, grads = refs[:group], refs[group : 2 * group]
    mine_ref, theirs_ref, down_mine_ref, down_theirs_ref = refs[2 * group : 2 * group + 4]
    outs = refs[2 * group + 4 :]
    half = mine_ref.shape[1]
    units = down_mine_ref.shape[0]
    mine, theirs = halves(mine_ref, place_ref[0], half)
    for index in range(group):
        normed_ref, grad_ref = tokens[index], grads[index]
        act_ref, out_ref, back_ref = outs[3 * index : 3 * index + 3]
        own, far = normed_ref[:, mine], normed_ref[:, theirs]
        gate = dot_nt(own, mine_ref[:units]) + dot_nt(far, theirs_ref[:units])
        up = dot_nt(own, mine_ref[units:]) + dot_nt(far, theirs_ref[units:])
        grad_inner = dot_nt(grad_ref[:, mine], down_mine_ref[...]) + dot_nt(
            grad_ref[:, theirs], down_theirs_ref[...]
        )
        normal = 0.5 * (1.0 + lax.erf(gate * math.sqrt(0.5)))
        density = jnp.exp(-0.5 * gate * gate) * (1.0 / math.sqrt(2.0 * math.pi))
        gelu = gate * normal
        inner = (gelu * up).astype(low)
        grad_gate = (grad_inner * up * (normal + gate * density)).astype(low)
        grad_up = (grad_inner * gelu).astype(low)
        act_ref[0] = grad_gate
        act_ref[1] = grad_up
        act_ref[2] = inner
        for lanes, weight, down in (
            (mine, mine_ref, down_mine_ref), (theirs, theirs_ref, down_theirs_ref)
        ):
            back_ref[:, lanes] = (
                dot(grad_gate, weight[:units]) + dot(grad_up, weight[units:])
            ).astype(low)
            out_ref[:, lanes] = dot(inner, down[...]).astype(low)


def update(weight, momentum, variance, gradient, rate):
    momentum_new = beta_first * momentum + (1.0 - beta_first) * gradient
    variance_new = beta_second * variance + (1.0 - beta_second) * gradient * gradient
    first_hat = momentum_new * (1.0 / (1.0 - beta_first**STEP))
    second_hat = variance_new * (1.0 / (1.0 - beta_second**STEP))
    new = weight - rate * (first_hat / (jnp.sqrt(second_hat) + adam_eps) + decay_rate * weight)
    return new, momentum_new, variance_new


def update_kernel(rate, flip, by_half, count, *refs):
    which = pl.program_id(1) if by_half else 0
    state, outs = refs[count : count + 3], refs[count + 3 :]
    for index in range(count):

        @pl.when(which == index)
        def _():
            gradient = refs[index][...].astype(wide)
            if flip:
                gradient = gradient.T
            for out, value in zip(outs, update(*(one[...] for one in state), gradient, rate)):
                out[...] = value


def run_update(name, rate, pieces, state, skip, flip, by_half):
    dim = 1 if flip else 0
    size = list(state[0].shape[1:])
    size[dim] //= 2
    if size[0] % 8 or size[1] % 128:
        if by_half:
            gradient = jnp.concatenate(pieces, axis=1)[skip : skip + state[0].shape[0]]
        else:
            gradient = pieces[0]
        gradient = gradient.astype(wide)
        if flip:
            gradient = jnp.transpose(gradient, (0, 2, 1))
        return update(*state, gradient, rate)

    def place(c, h):
        return (c, h, 0) if dim == 0 else (c, 0, h)

    spec = pl.BlockSpec((None, *size), place)
    grad_spec = spec
    if by_half:
        cut = size[::-1] if flip else size
        grad_spec = pl.BlockSpec((None, *cut), lambda c, h: (c + skip, 0, 0))
    return pl.pallas_call(
        functools.partial(update_kernel, rate, flip, by_half, len(pieces)),
        grid=(state[0].shape[0], 2),
        in_specs=[grad_spec] * len(pieces) + [spec] * 3,
        out_specs=[spec] * 3,
        out_shape=[jax.ShapeDtypeStruct(state[0].shape, wide)] * 3,
        name=name,
        compiler_params=pltpu.CompilerParams(vmem_limit_bytes=VMEM),
        cost_estimate=pl.CostEstimate(flops=1000, bytes_accessed=1000, transcendentals=0),
    )(*pieces, *state)


def feed_weights_kernel(place_ref, *refs):
    group = (len(refs) - 3) // 3
    acts, tokens, grads = refs[:group], refs[group : 2 * group], refs[2 * group : 3 * group]
    own_ref, *far_refs = refs[3 * group :]
    half = own_ref.shape[-1]
    mine, theirs = halves(own_ref, place_ref[0], half)

    for step, rights in enumerate((tokens, tokens, grads)):

        @pl.when(pl.program_id(0) == step)
        def _():
            far_ref = far_refs[0].at[step] if step < 2 else far_refs[1]
            for out, lanes in ((own_ref, mine), (far_ref, theirs)):
                total = None
                for act, right in zip(acts, rights):
                    for row in range(act.shape[0]):
                        part = dot_tn(act[row], right[row, :, lanes])
                        total = part if total is None else total + part
                out[...] = total.astype(low)


def middle_back_kernel(
    one_ref, two_ref, three_ref, middle_ref, gain_ref, grad_ref,
    out_ref, low_ref, turned_ref, gain_out_ref,
):
    cotangent = one_ref[...].astype(wide) + two_ref[...].astype(wide) + three_ref[...].astype(wide)
    back, gain_part = norm_back(middle_ref[...], gain_ref[...], cotangent)
    total = grad_ref[...] + back
    out_ref[...] = total
    low_ref[...] = total.astype(low)
    turned_ref[...] = total.T.astype(low)
    gain_out_ref[...] = gain_part


def normed_grad_kernel(place_ref, *refs):
    group = (len(refs) - 1) // 3
    grads, mine_refs, theirs_refs = refs[:group], refs[group : 2 * group], refs[2 * group : 3 * group]
    out_ref = refs[-1]
    half = mine_refs[0].shape[1]
    mine, theirs = halves(out_ref, place_ref[0], half)
    for lanes, weights in ((mine, mine_refs), (theirs, theirs_refs)):
        total = None
        for grad, weight in zip(grads, weights):
            for which in range(3):
                part = dot_nt(grad[which], weight[which])
                total = part if total is None else total + part
        out_ref[:, lanes] = total


def input_back_kernel(
    here_ref, before_ref, after_ref, hidden_ref, gain_ref, grad_ref, out_ref, gain_out_ref
):
    seg_len = hidden_ref.shape[0]
    gain = gain_ref[...]
    hidden = hidden_ref[...].astype(wide)
    centre = here_ref[HALF : HALF + seg_len]
    cotangent = jnp.concatenate(
        [
            centre[:HALF] + before_ref[...].astype(wide),
            centre[HALF : seg_len - HALF],
            centre[seg_len - HALF :] + after_ref[...].astype(wide),
        ],
        axis=0,
    )
    back, gain_part = norm_back(hidden, gain, cotangent)
    out_ref[...] = grad_ref[...] + back
    gain_out_ref[...] = gain_part


def by_row(shape):
    rest = tuple(shape[1:])
    return pl.BlockSpec((None,) + rest, lambda r: (r,) + (0,) * len(rest))


def fixed(shape):
    return pl.BlockSpec(tuple(shape), lambda r: (0,) * len(shape))


def spec_of(values, kind):
    if kind == "row":
        return by_row(values.shape)
    if kind == "second":
        return pl.BlockSpec(
            (values.shape[0], None) + tuple(values.shape[2:]),
            lambda r: (0, r) + (0,) * (len(values.shape) - 2),
        )
    if kind == "step":
        return pl.BlockSpec((None,) + tuple(values.shape[1:]), lambda r: (r, 0, 0, 0))
    if kind == "head":
        return pl.BlockSpec((3,) + tuple(values.shape[1:]), lambda r: (0, 0, 0))
    if kind == "last":
        return pl.BlockSpec((None,) + tuple(values.shape[1:]), lambda r: (3, 0, 0))
    if kind == "scalar":
        return pl.BlockSpec(memory_space=pltpu.SMEM)
    return fixed(values.shape)


def run(kernel, name, steps, ins, outs, scratch=()):
    return pl.pallas_call(
        kernel,
        grid=(steps,),
        in_specs=[spec_of(value, kind) for value, kind in ins],
        out_specs=[spec_of(shape, kind) for shape, kind in outs],
        out_shape=[shape for shape, kind in outs],
        scratch_shapes=list(scratch),
        name=name,
        compiler_params=pltpu.CompilerParams(vmem_limit_bytes=VMEM),
        cost_estimate=pl.CostEstimate(flops=1000, bytes_accessed=1000, transcendentals=0),
    )(*[value for value, kind in ins])


def doc_tables(starts, places):
    inside = (places >= 0) & (places < L)
    before = starts[..., None, :] <= places[..., :, None]
    number = jnp.sum(before.astype(jnp.int32), axis=-1) - 1
    begins = jnp.max(jnp.where(before, starts[..., None, :], 0), axis=-1)
    return (jnp.where(inside, number, -1), places - begins)


def adam(weight, momentum, variance, gradient, step_rate, shrink_rate):
    momentum_new = beta_first * momentum + (1.0 - beta_first) * gradient
    variance_new = beta_second * variance + (1.0 - beta_second) * gradient * gradient
    first_hat = momentum_new / (1.0 - beta_first**STEP)
    second_hat = variance_new / (1.0 - beta_second**STEP)
    updated = weight - step_rate * (
        first_hat / (jnp.sqrt(second_hat) + adam_eps) + shrink_rate * weight
    )
    return (updated, momentum_new, variance_new)


def take(values, index, size, dim):
    return lax.dynamic_slice_in_dim(values, index * size, size, axis=dim)


def joined(bit, mine, theirs, dim):
    return jnp.where(
        bit == 0,
        jnp.concatenate([mine, theirs], axis=dim),
        jnp.concatenate([theirs, mine], axis=dim),
    )


def after(values, *others):
    return lax.optimization_barrier((values,) + others)[0]


def all_after(values, *others):
    return lax.optimization_barrier(tuple(values) + others)[: len(values)]


EVEN = [(0, 1), (1, 0), (2, 3), (3, 2)]
ACROSS = [(0, 2), (2, 0), (1, 3), (3, 1)]


def line_one(values, dim):
    if lax.axis_size("ctx") != 4:
        return values, None
    parity = lax.rem(lax.axis_index("ctx"), 2)
    size = values.shape[dim] // 2
    got = lax.ppermute(take(values, 1 - parity, size, dim), "ctx", EVEN)
    return take(values, parity, size, dim), got


def line_two(kept, got):
    if got is None:
        return kept, None
    part = added(kept, got)
    return part, lax.ppermute(part, "ctx", ACROSS)


def line_three(kept, got):
    if got is None:
        return kept, None
    part = added(kept, got)
    return part, lax.ppermute(part, "ctx", EVEN)


def line_end(kept, got, dim):
    if got is None:
        return lax.psum(kept.astype(wide), "ctx").astype(low)
    return joined(lax.rem(lax.axis_index("ctx"), 2), kept, got, dim)


def added(*values):
    return sum(value.astype(wide) for value in values).astype(low)


def body(
    hidden_in,
    doc_starts,
    grad_out,
    qkv_weight,
    output_weight,
    geglu_weight,
    down_weight,
    norm_gains,
    qkv_momentum,
    qkv_variance,
    output_momentum,
    output_variance,
    geglu_momentum,
    geglu_variance,
    down_momentum,
    down_variance,
    gains_momentum,
    gains_variance,
):
    rows, seg_len, model_width = hidden_in.shape
    shards = lax.axis_size("shard")
    paired = shards == 2
    half = model_width // 2
    shard_place = lax.axis_index("shard")
    group_place = lax.axis_index("tp")
    ctx_place = lax.axis_index("ctx")
    place = shard_place if paired else jnp.zeros_like(shard_place)
    place_one = place.astype(jnp.int32).reshape(1)
    group = (0, 1, 2, 3)
    span = seg_len + 2 * HALF
    cols = qkv_weight.shape[2]
    units = down_weight.shape[0]

    count = lax.axis_size("ctx")
    forward = [(i, i + 1) for i in range(count - 1)]
    backward = [(i + 1, i) for i in range(count - 1)]
    before = lax.ppermute(hidden_in[:, seg_len - HALF :], "ctx", forward)
    after_edge = lax.ppermute(hidden_in[:, :HALF], "ctx", backward)

    def both(values, dim):
        if paired:
            return values, shard_swap(values)
        full = lax.all_gather(values, "shard", axis=dim, tiled=True)
        return (
            lax.slice_in_dim(full, 0, half, axis=dim),
            lax.slice_in_dim(full, half, 2 * half, axis=dim),
        )

    gains_near = norm_gains.astype(low)
    if paired:
        gains_low = joined(place, gains_near, shard_swap(after(gains_near, before, after_edge)), 1)
    else:
        gains_low = lax.all_gather(gains_near, "shard", axis=1, tiled=True)
    gain_one = gains_low[0:1].astype(wide)
    gain_two = gains_low[1:2].astype(wide)

    qkv_turned = jnp.transpose(qkv_weight, (1, 0, 2))
    geglu_turned = jnp.transpose(geglu_weight, (1, 2, 0))
    block_low = jnp.concatenate(
        [qkv_turned.astype(low), jnp.transpose(output_weight).astype(low)[None]], axis=0
    )
    mine, theirs = both(block_low, 1)
    geglu_low = after(geglu_turned, before, after_edge).astype(low).reshape(2 * units, -1)
    geglu_mine, geglu_theirs = both(geglu_low, 1)
    down_low = after(down_weight, before, after_edge).astype(low)
    down_mine, down_theirs = both(down_low, 1)

    grad_low = after(grad_out, before, after_edge).astype(low)
    offset = ctx_place * seg_len
    ext_places = offset - HALF + jnp.arange(span, dtype=jnp.int32)
    tp_rows = lax.dynamic_slice_in_dim(doc_starts, group_place * rows, rows, axis=0)
    ext_doc, ext_place = doc_tables(tp_rows, ext_places)
    inverse = theta_base ** (-2.0 * jnp.arange(HD // 2, dtype=wide) / HD)
    angles = ext_place.astype(wide)[..., None] * inverse
    cosine, sine = jnp.cos(angles), jnp.sin(angles)
    cosine = jnp.concatenate([cosine] * 4, axis=-1)
    sine = jnp.concatenate([-sine, sine, -sine, sine], axis=-1)
    blocks = seg_len // QBLOCK
    query_doc = ext_doc[:, HALF : HALF + seg_len].reshape(rows, blocks, QBLOCK)
    key_doc = jnp.stack(
        [ext_doc[:, b * QBLOCK : b * QBLOCK + KBLOCK] for b in range(blocks)], axis=1
    )
    gap = jnp.arange(QBLOCK)[:, None] + HALF - jnp.arange(KBLOCK)[None, :]
    allowed = (jnp.abs(gap) <= HALF) & (query_doc[..., :, None] == key_doc[..., None, :])
    bias = jnp.where(allowed, 0.0, masked_value).astype(wide)

    normed, normed_turned = run(
        first_norm_kernel, "first_norm", rows,
        [(before, "row"), (hidden_in, "row"), (after_edge, "row"), (gain_one, "all")],
        [
            (jax.ShapeDtypeStruct((rows, span, model_width), low), "row"),
            (jax.ShapeDtypeStruct((rows, model_width, span), low), "row"),
        ],
    )

    far_mine = chip_swap(mine)
    near_mine = core_swap(mine)
    theirs = after(
        theirs, before, after_edge, cosine, sine, bias, geglu_low, down_low, grad_low, far_mine
    )
    far_theirs = chip_swap(theirs)
    weights = [(mine, theirs), (near_mine, core_swap(theirs))]
    scalar = (place_one, "scalar")
    tables = [(cosine, "row"), (sine, "row"), (bias, "row")]
    short = jax.ShapeDtypeStruct((rows, seg_len, cols), low)
    long = jax.ShapeDtypeStruct((rows, span, cols), low)
    saved = []
    for j in group:
        tokens_here = normed if j == 0 else after(normed, saved[j - 1][3])
        if j == 2:
            far_theirs = after(far_theirs, saved[1][3])
            weights.append((far_mine, far_theirs))
            weights.append((core_swap(far_mine), core_swap(far_theirs)))
            grad_far = chip_swap(after(grad_low, far_theirs))
        if j == 3:
            tokens_here = after(tokens_here, geglu_theirs)
        saved.append(
            run(
                attend_kernel, "attend", rows,
                [scalar, (tokens_here, "row"), (weights[j][0], "head"), (weights[j][1], "head")]
                + tables,
                [(short, "row"), (long, "row"), (long, "row"), (short, "row")],
            )
        )
    attended = [one[3] for one in saved]
    attended[3] = after(attended[3], down_theirs)
    middle, normed_two = run(
        second_norm_kernel, "second_norm", rows,
        [scalar]
        + [(one, "row") for one in attended]
        + [(weights[j][0], "last") for j in group]
        + [(weights[j][1], "last") for j in group]
        + [(hidden_in, "row"), (gain_two, "all")],
        [
            (jax.ShapeDtypeStruct((rows, seg_len, model_width), wide), "row"),
            (jax.ShapeDtypeStruct((rows, seg_len, model_width), low), "row"),
        ],
    )

    normed_far = chip_swap(normed_two)
    normed_one = core_swap(normed_two)
    grad_one = core_swap(grad_low)
    act_rows = jax.ShapeDtypeStruct((3, rows, seg_len, units), low)
    full_rows = jax.ShapeDtypeStruct((rows, seg_len, model_width), low)

    def feed(tokens, grads):
        done = run(
            feed_kernel, "feed", rows,
            [scalar]
            + [(one, "row") for one in tokens]
            + [(one, "row") for one in grads]
            + [(one, "all") for one in (geglu_mine, geglu_theirs, down_mine, down_theirs)],
            [(act_rows, "second"), (full_rows, "row"), (full_rows, "row")] * len(tokens),
        )
        return [done[3 * i : 3 * i + 3] for i in range(len(tokens))]

    tokens, grads = [after(normed_two, grad_far), normed_one], [grad_low, grad_one]
    fed = feed(tokens, grads)
    back_one, out_one = core_swap(fed[1][2]), core_swap(fed[1][1])
    normed_far = after(normed_far, fed[0][2], back_one, out_one)
    tokens += [normed_far, core_swap(normed_far)]
    grads += [grad_far, core_swap(grad_far)]
    fed += feed(tokens[2:], grads[2:])
    back_three = core_swap(fed[3][2])
    back_far = chip_swap(added(fed[2][2], back_three))
    out_three = core_swap(after(fed[3][1], back_three))

    feed_part = jax.ShapeDtypeStruct((3, units, half), low)
    feed_own, *feed_other = run(
        feed_weights_kernel, "feed_weights", 3,
        [scalar]
        + [(after(fed[0][0], back_three), "step")]
        + [(one[0], "step") for one in fed[1:]]
        + [(one, "all") for one in tokens]
        + [(one, "all") for one in grads],
        [
            (feed_part, "row"),
            (jax.ShapeDtypeStruct((2, units, half), low), "all"),
            (jax.ShapeDtypeStruct((units, half), low), "all"),
        ],
    )

    out_far = chip_swap(after(added(fed[2][1], out_three), feed_own))
    back_far, unused = lax.optimization_barrier((back_far, feed_own))
    gain_shape = jax.ShapeDtypeStruct((rows, 1, model_width), wide)
    grad_middle, middle_low, middle_turned, gain_two_part = run(
        middle_back_kernel, "middle_back", rows,
        [
            (after(fed[0][2], feed_own), "row"), (back_one, "row"), (back_far, "row"),
            (middle, "row"), (gain_two, "all"), (grad_out, "row"),
        ],
        [
            (jax.ShapeDtypeStruct(grad_out.shape, wide), "row"),
            (jax.ShapeDtypeStruct(grad_out.shape, low), "row"),
            (jax.ShapeDtypeStruct((rows, model_width, seg_len), low), "row"),
            (gain_shape, "row"),
        ],
    )

    if paired:
        geglu_got, down_got = [shard_swap(one) for one in feed_other]
    else:
        feed_other[1] = feed_other[1][None]
        feed_got = lax.psum_scatter(
            jnp.concatenate([feed_own, jnp.concatenate(feed_other, axis=0)], axis=2),
            "shard", scatter_dimension=2, tiled=True,
        )
        geglu_got, down_got = feed_got[:2], feed_got[2]

    mixed, own, other = [None] * 4, [None] * 4, [None] * 4
    weight_part = jax.ShapeDtypeStruct((4, half, cols), low)
    def attend_back(j, *before_it):
        queries, keys, values, out = saved[j]
        mixed[j], own[j], other[j] = run(
            attend_back_kernel, "attend_back", rows,
            [
                scalar, (after(middle_low, *before_it), "row"), (middle_turned, "row"),
                (normed_turned, "row"), (out, "row"),
                (weights[j][0], "last"), (weights[j][1], "last"),
                (queries, "row"), (keys, "row"), (values, "row"),
            ]
            + tables,
            [
                (jax.ShapeDtypeStruct((3, rows, span, cols), low), "second"),
                (weight_part, "all"), (weight_part, "all"),
            ],
            scratch=[
                pltpu.VMEM((span, cols), wide), pltpu.VMEM((span, cols), wide),
                pltpu.VMEM((8, half, cols), wide),
            ],
        )

    attend_back(3, back_far)
    far_three, far_other_three = core_swap(own[3]), core_swap(other[3])
    attend_back(2, mixed[3])
    far_other = added(other[2], far_other_three)
    far_own = own[2], far_three
    far_got = shard_swap(far_other) if paired else None
    geglu_got = after(geglu_got, mixed[2])
    geglu_part = added(feed_own[:2], geglu_got) if paired else geglu_got
    geglu_line = line_one(geglu_part, 0)
    attend_back(1, mixed[2], geglu_got, out_far)
    near_one, near_other_one = core_swap(own[1]), core_swap(other[1])
    geglu_line = line_two(*all_after(geglu_line, mixed[1]))
    down_got = after(down_got, mixed[1])
    down_part = added(feed_own[2], down_got) if paired else down_got
    down_line = line_one(down_part, 1)
    attend_back(0, mixed[1], geglu_line[0], down_got)
    down_line = line_two(*all_after(down_line, mixed[0]))

    near_other = added(other[0], near_other_one)
    near_own = own[0], near_one
    cut = half // 2
    if paired:
        near_got = [shard_swap(near_other[:, i * cut : (i + 1) * cut]) for i in (0, 1)]
        far_part = added(*far_own, after(far_got, mixed[0]))
    else:
        scatter = functools.partial(
            lax.psum_scatter, axis_name="shard", scatter_dimension=1, tiled=True
        )
        far_part = scatter(jnp.concatenate([added(*far_own), far_other], axis=1))
        near_sum = scatter(jnp.concatenate([added(*near_own), near_other], axis=1))
    far_rows = far_part.shape[1] // 2
    far = [chip_swap(far_part[:, i * far_rows : (i + 1) * far_rows]) for i in (0, 1)]

    def cut_of(index, *others):
        rows_at = slice(index * far_rows, (index + 1) * far_rows)
        if paired:
            got = all_after((near_got[index], far[index]), *others)
            return added(*(v[:, rows_at] for v in near_own), *got)
        return added(near_sum[:, rows_at], after(far[index], *others))

    (normed_grad,) = run(
        normed_grad_kernel, "normed_grad", rows,
        [scalar]
        + [(after(mixed[0], down_line[0], near_other, far_part), "second")]
        + [(mixed[j], "second") for j in group[1:]]
        + [(weights[j][0], "head") for j in group]
        + [(weights[j][1], "head") for j in group],
        [(jax.ShapeDtypeStruct((rows, span, model_width), wide), "row")],
    )
    to_before = lax.ppermute(normed_grad[:, :HALF].astype(low), "ctx", backward)
    to_after = lax.ppermute(normed_grad[:, HALF + seg_len :].astype(low), "ctx", forward)

    block_lines = [line_one(cut_of(0, normed_grad), 0)]
    geglu_line = all_after(geglu_line, normed_grad)
    to_before, to_after = all_after((to_before, to_after), block_lines[0][0], *geglu_line)
    grad_in, gain_one_part = run(
        input_back_kernel, "input_back", rows,
        [
            (normed_grad, "row"), (to_after, "row"), (to_before, "row"), (hidden_in, "row"),
            (gain_one, "all"), (grad_middle, "row"),
        ],
        [(jax.ShapeDtypeStruct(grad_out.shape, wide), "row"), (gain_shape, "row")],
    )
    result = middle + fed[0][1].astype(wide) + out_one.astype(wide) + out_far.astype(wide)
    hidden_out = result.astype(low)
    block_lines.append(line_one(cut_of(1, grad_in, hidden_out), 0))
    block_lines[0] = line_two(*all_after(block_lines[0], block_lines[1][0]))
    geglu_line = line_three(*all_after(geglu_line, block_lines[1][0]))
    down_line = line_three(*all_after(down_line, block_lines[1][0]))
    gain_one_part = after(gain_one_part, block_lines[0][0], geglu_line[0], down_line[0])
    gain_sum = jnp.concatenate(
        [jnp.sum(gain_one_part, axis=0), jnp.sum(gain_two_part, axis=0)], axis=0
    )
    gain_sum = gain_sum + core_swap(gain_sum)
    if lax.axis_size("ctx") == 4:
        gain_sum = gain_sum + lax.ppermute(gain_sum, "ctx", EVEN)
        gain_sum = gain_sum + lax.ppermute(gain_sum, "ctx", ACROSS)
    else:
        gain_sum = lax.psum(gain_sum, "ctx")
    gain_sum = gain_sum + chip_swap(gain_sum)
    gain_sum = gain_sum + shard_swap(gain_sum) if paired else lax.psum(gain_sum, "shard")
    gains_here = norm_gains.shape[1]
    gain_grad = lax.dynamic_slice_in_dim(gain_sum, shard_place * gains_here, gains_here, axis=1)

    block_lines[1] = line_two(*block_lines[1])
    block_sums = [line_end(*line_three(*one), 0) for one in block_lines]
    geglu_sum, down_sum = line_end(*geglu_line, 0), line_end(*down_line, 1)

    def turned_state(axes, *values):
        return [jnp.transpose(v, axes) for v in values]

    def turned_back(axes, values):
        return tuple(jnp.transpose(v, axes) for v in values)

    geglu_set = turned_back(
        (2, 0, 1),
        run_update(
            "update_geglu", rate_geglu, [geglu_sum],
            turned_state((1, 2, 0), geglu_weight, geglu_momentum, geglu_variance), 0, False, False,
        ),
    )
    down_set = tuple(
        v[0]
        for v in run_update(
            "update_down", rate_down, [down_sum[None]],
            [v[None] for v in (down_weight, down_momentum, down_variance)], 0, False, False,
        )
    )
    qkv_set = turned_back(
        (1, 0, 2),
        run_update(
            "update_qkv", rate_qkv, block_sums,
            turned_state((1, 0, 2), qkv_weight, qkv_momentum, qkv_variance), 0, False, True,
        ),
    )
    output_set = tuple(
        v[0]
        for v in run_update(
            "update_output", rate_output, block_sums,
            [v[None] for v in (output_weight, output_momentum, output_variance)], 3, True, True,
        )
    )
    gains_set = adam(norm_gains, gains_momentum, gains_variance, gain_grad, rate_gains, 0.0)
    return (hidden_out, grad_in) + qkv_set + output_set + geglu_set + down_set + gains_set


def solution(mesh):
    tokens = P(("shard", "tp"), "ctx", None)
    split_in = P("shard", None, "tp")
    split_out = P("tp", "shard")
    gains = P(None, "shard")
    return jax.shard_map(
        body,
        mesh=mesh,
        in_specs=(
            (tokens, P("shard", None), tokens, split_in, split_out, split_in, split_out, gains)
            + (split_in, split_in, split_out, split_out)
            + (split_in, split_in, split_out, split_out)
            + (gains, gains)
        ),
        out_specs=(
            (tokens, tokens)
            + (split_in,) * 3
            + (split_out,) * 3
            + (split_in,) * 3
            + (split_out,) * 3
            + (gains,) * 3
        ),
        check_vma=False,
    )
```

```python
import functools
import math

import jax
import jax.numpy as jnp
from jax import lax
from jax.experimental import pallas as pl
from jax.experimental.pallas import tpu as pltpu
from jax.sharding import PartitionSpec as P

HD = 64
HALF = 64
L = 1024
STEP = 10
PAIR = 2 * HD
QBLOCK = 128
KBLOCK = QBLOCK + 2 * HALF

theta_base = 10000.0
norm_eps = 1e-05
beta_first = 0.9
beta_second = 0.98
adam_eps = 1e-06
decay_rate = 1e-05
rate_qkv = 0.06
rate_output = 0.35
rate_geglu = 0.06
rate_down = 0.04
rate_gains = 0.5
masked_value = -1e30

low = jnp.bfloat16
wide = jnp.float32
SCALING = 1.0 / math.sqrt(HD)
VMEM = 40 * 1024 * 1024

CORE_SWAP = [(0, 1), (1, 0), (2, 3), (3, 2)]
CHIP_SWAP = [(0, 2), (2, 0), (1, 3), (3, 1)]


def core_swap(values):
    return lax.ppermute(values, "tp", CORE_SWAP)


def chip_swap(values):
    return lax.ppermute(values, "tp", CHIP_SWAP)


def shard_swap(values):
    return lax.ppermute(values, "shard", [(0, 1), (1, 0)])


def dot(a, b):
    return lax.dot_general(a, b, (((1,), (0,)), ((), ())), preferred_element_type=wide)


def dot_nt(a, b):
    return lax.dot_general(a, b, (((1,), (1,)), ((), ())), preferred_element_type=wide)


def dot_tn(a, b):
    return lax.dot_general(a, b, (((0,), (0,)), ((), ())), preferred_element_type=wide)


def normalized(values):
    centered = values - jnp.mean(values, axis=-1, keepdims=True)
    spread = jnp.mean(centered * centered, axis=-1, keepdims=True)
    inverse = lax.rsqrt(spread + norm_eps)
    return centered * inverse, inverse


def norm_back(values, gain, cotangent):
    unit, inverse = normalized(values)
    scaled = cotangent * gain
    first = jnp.mean(scaled, axis=-1, keepdims=True)
    second = jnp.mean(scaled * unit, axis=-1, keepdims=True)
    gain_part = jnp.sum(cotangent * unit, axis=0, keepdims=True)
    return (scaled - first - unit * second) * inverse, gain_part


def turned(values, cosine, sine):
    half_len = HD // 2
    lane = lax.broadcasted_iota(jnp.int32, values.shape, 1)
    ahead = pltpu.roll(values, PAIR - half_len, 1)
    behind = pltpu.roll(values, half_len, 1)
    other = jnp.where(lane % HD < half_len, ahead, behind)
    return values * cosine + other * sine


def head_stack(values):
    lane = lax.broadcasted_iota(jnp.int32, values.shape, 1)
    zero = jnp.zeros_like(values)
    return jnp.concatenate(
        [jnp.where(lane < HD, values, zero), jnp.where(lane < HD, zero, values)], axis=0
    )


def head_join(values):
    rows = values.shape[0] // 2
    upper, lower = values[:rows], values[rows:]
    lane = lax.broadcasted_iota(jnp.int32, upper.shape, 1)
    return jnp.where(lane < HD, upper, lower)


def chances_of(query_stack, keys, bias):
    scores = dot_nt(query_stack, keys) * SCALING + jnp.concatenate([bias, bias], axis=0)
    weights = jnp.exp(scores - jnp.max(scores, axis=-1, keepdims=True))
    return weights * (1.0 / jnp.sum(weights, axis=-1, keepdims=True))


def halves(ref_values, place, half):
    mine = pl.ds(pl.multiple_of(place * half, half), half)
    theirs = pl.ds(pl.multiple_of((1 - place) * half, half), half)
    return mine, theirs


def first_norm_kernel(before_ref, here_ref, after_ref, gain_ref, out_ref, turned_ref):
    tokens = [ref[...].astype(wide) for ref in (before_ref, here_ref, after_ref)]
    normed = normalized(jnp.concatenate(tokens, axis=0))[0] * gain_ref[...]
    out_ref[...] = normed.astype(low)
    turned_ref[...] = normed.T.astype(low)


def attend_kernel(
    place_ref, normed_ref, mine_ref, theirs_ref, cos_ref, sin_ref, bias_ref,
    query_ref, key_ref, value_ref, out_ref,
):
    seg_len = query_ref.shape[0]
    half = mine_ref.shape[1]
    mine, theirs = halves(normed_ref, place_ref[0], half)
    inner = slice(HALF, HALF + seg_len)

    def project(which, rows):
        return dot(normed_ref[rows, mine], mine_ref[which]) + dot(
            normed_ref[rows, theirs], theirs_ref[which]
        )

    whole = slice(0, normed_ref.shape[0])
    queries, keys = project(0, inner), project(1, whole)
    value_ref[...] = project(2, whole).astype(low)
    for first in range(0, query_ref.shape[1], PAIR):
        lanes = slice(first, first + PAIR)
        query_ref[:, lanes] = turned(queries[:, lanes], cos_ref[inner], sin_ref[inner]).astype(low)
        key_ref[:, lanes] = turned(keys[:, lanes], cos_ref[...], sin_ref[...]).astype(low)
    for first in range(0, query_ref.shape[1], PAIR):
        lanes = slice(first, first + PAIR)
        for block in range(seg_len // QBLOCK):
            rows = slice(block * QBLOCK, block * QBLOCK + QBLOCK)
            reach = slice(block * QBLOCK, block * QBLOCK + KBLOCK)
            chances = chances_of(head_stack(query_ref[rows, lanes]), key_ref[reach, lanes], bias_ref[block])
            out_ref[rows, lanes] = head_join(dot(chances.astype(low), value_ref[reach, lanes])).astype(low)


def attend_back_kernel(chained, *refs):
    (
        place_ref, grad_ref, grad_turned_ref, normed_ref, attended_ref, mine_ref, theirs_ref,
        query_ref, key_ref, value_ref, cos_ref, sin_ref, bias_ref,
    ) = refs[:13]
    before_refs = refs[13:15] if chained else ()
    mixed_ref, own_ref, far_ref, key_sum, value_sum, weight_sum = refs[-6:]
    seg_len = query_ref.shape[0]
    half = mine_ref.shape[0]
    mine, theirs = halves(grad_ref, place_ref[0], half)
    inner = slice(HALF, HALF + seg_len)
    grad_out = (
        dot(grad_ref[:, mine], mine_ref[...]) + dot(grad_ref[:, theirs], theirs_ref[...])
    ).astype(low)
    key_sum[...] = jnp.zeros_like(key_sum)
    value_sum[...] = jnp.zeros_like(value_sum)
    edge = jnp.zeros((HALF, query_ref.shape[1]), low)
    mixed_ref[0, :HALF] = edge
    mixed_ref[0, HALF + seg_len :] = edge
    for first in range(0, query_ref.shape[1], PAIR):
        lanes = slice(first, first + PAIR)
        for block in range(seg_len // QBLOCK):
            rows = slice(block * QBLOCK, block * QBLOCK + QBLOCK)
            reach = slice(block * QBLOCK, block * QBLOCK + KBLOCK)
            place_rows = slice(HALF + block * QBLOCK, HALF + block * QBLOCK + QBLOCK)
            queries = head_stack(query_ref[rows, lanes])
            grads = head_stack(grad_out[rows, lanes])
            keys, values = key_ref[reach, lanes], value_ref[reach, lanes]
            chances = chances_of(queries, keys, bias_ref[block])
            grad_chances = dot_nt(grads, values)
            weighted = chances * grad_chances
            grad_scores = (
                weighted - chances * jnp.sum(weighted, axis=-1, keepdims=True)
            ).astype(low)
            value_sum[reach, lanes] += dot_tn(chances.astype(low), grads)
            key_sum[reach, lanes] += dot_tn(grad_scores, queries)
            grad_queries = head_join(dot(grad_scores, keys)) * SCALING
            mixed_ref[0, place_rows, lanes] = turned(
                grad_queries, cos_ref[place_rows], -sin_ref[place_rows]
            ).astype(low)
        mixed_ref[1, :, lanes] = turned(
            key_sum[:, lanes] * SCALING, cos_ref[...], -sin_ref[...]
        ).astype(low)
    mixed_ref[2] = value_sum[...].astype(low)

    parts = []
    for lanes in (mine, theirs):
        parts += [dot(normed_ref[lanes], mixed_ref[which]) for which in range(3)]
        parts.append(dot(grad_turned_ref[lanes], attended_ref[...]))

    @pl.when(pl.program_id(0) == 0)
    def _():
        for index, part in enumerate(parts):
            if chained:
                part += before_refs[index // 4][index % 4].astype(wide)
            weight_sum[index] = part

    @pl.when(pl.program_id(0) > 0)
    def _():
        for index, part in enumerate(parts):
            weight_sum[index] += part

    @pl.when(pl.program_id(0) == pl.num_programs(0) - 1)
    def _():
        for index in range(4):
            own_ref[index] = weight_sum[index].astype(low)
            far_ref[index] = weight_sum[4 + index].astype(low)


def second_norm_kernel(place_ref, *refs):
    group = (len(refs) - 4) // 3
    attended, mine_refs, theirs_refs = refs[:group], refs[group : 2 * group], refs[2 * group : 3 * group]
    hidden_ref, gain_ref, middle_ref, normed_ref = refs[3 * group :]
    half = mine_refs[0].shape[0]
    mine, theirs = halves(middle_ref, place_ref[0], half)
    for lanes, weights in ((mine, mine_refs), (theirs, theirs_refs)):
        total = hidden_ref[:, lanes].astype(wide)
        for one, weight in zip(attended, weights):
            total += dot_nt(one[...], weight[...])
        middle_ref[:, lanes] = total
    normed_ref[...] = (normalized(middle_ref[...])[0] * gain_ref[...]).astype(low)


def feed_kernel(place_ref, *refs):
    group = (len(refs) - 4) // 5
    tokens, grads = refs[:group], refs[group : 2 * group]
    mine_ref, theirs_ref, down_mine_ref, down_theirs_ref = refs[2 * group : 2 * group + 4]
    outs = refs[2 * group + 4 :]
    half = mine_ref.shape[1]
    units = down_mine_ref.shape[0]
    mine, theirs = halves(mine_ref, place_ref[0], half)
    for index in range(group):
        normed_ref, grad_ref = tokens[index], grads[index]
        act_ref, out_ref, back_ref = outs[3 * index : 3 * index + 3]
        own, far = normed_ref[:, mine], normed_ref[:, theirs]
        gate = dot_nt(own, mine_ref[:units]) + dot_nt(far, theirs_ref[:units])
        up = dot_nt(own, mine_ref[units:]) + dot_nt(far, theirs_ref[units:])
        grad_inner = dot_nt(grad_ref[:, mine], down_mine_ref[...]) + dot_nt(
            grad_ref[:, theirs], down_theirs_ref[...]
        )
        normal = 0.5 * (1.0 + lax.erf(gate * math.sqrt(0.5)))
        density = jnp.exp(-0.5 * gate * gate) * (1.0 / math.sqrt(2.0 * math.pi))
        gelu = gate * normal
        inner = (gelu * up).astype(low)
        grad_gate = (grad_inner * up * (normal + gate * density)).astype(low)
        grad_up = (grad_inner * gelu).astype(low)
        act_ref[0] = grad_gate
        act_ref[1] = grad_up
        act_ref[2] = inner
        for lanes, weight, down in (
            (mine, mine_ref, down_mine_ref), (theirs, theirs_ref, down_theirs_ref)
        ):
            back_ref[:, lanes] = (
                dot(grad_gate, weight[:units]) + dot(grad_up, weight[units:])
            ).astype(low)
            out_ref[:, lanes] = dot(inner, down[...]).astype(low)


def update(weight, momentum, variance, gradient, rate):
    momentum_new = beta_first * momentum + (1.0 - beta_first) * gradient
    variance_new = beta_second * variance + (1.0 - beta_second) * gradient * gradient
    first_hat = momentum_new * (1.0 / (1.0 - beta_first**STEP))
    second_hat = variance_new * (1.0 / (1.0 - beta_second**STEP))
    new = weight - rate * (first_hat / (jnp.sqrt(second_hat) + adam_eps) + decay_rate * weight)
    return new, momentum_new, variance_new


def update_kernel(rate, flip, by_half, count, *refs):
    which = pl.program_id(1) if by_half else 0
    state, outs = refs[count : count + 3], refs[count + 3 :]
    for index in range(count):

        @pl.when(which == index)
        def _():
            gradient = refs[index][...].astype(wide)
            if flip:
                gradient = gradient.T
            for out, value in zip(outs, update(*(one[...] for one in state), gradient, rate)):
                out[...] = value


def run_update(name, rate, pieces, state, skip, flip, by_half):
    dim = 1 if flip else 0
    size = list(state[0].shape[1:])
    size[dim] //= 2
    if size[0] % 8 or size[1] % 128:
        if by_half:
            gradient = jnp.concatenate(pieces, axis=1)[skip : skip + state[0].shape[0]]
        else:
            gradient = pieces[0]
        gradient = gradient.astype(wide)
        if flip:
            gradient = jnp.transpose(gradient, (0, 2, 1))
        return update(*state, gradient, rate)

    def place(c, h):
        return (c, h, 0) if dim == 0 else (c, 0, h)

    spec = pl.BlockSpec((None, *size), place)
    grad_spec = spec
    if by_half:
        cut = size[::-1] if flip else size
        grad_spec = pl.BlockSpec((None, *cut), lambda c, h: (c + skip, 0, 0))
    return pl.pallas_call(
        functools.partial(update_kernel, rate, flip, by_half, len(pieces)),
        grid=(state[0].shape[0], 2),
        in_specs=[grad_spec] * len(pieces) + [spec] * 3,
        out_specs=[spec] * 3,
        out_shape=[jax.ShapeDtypeStruct(state[0].shape, wide)] * 3,
        name=name,
        compiler_params=pltpu.CompilerParams(vmem_limit_bytes=VMEM),
        cost_estimate=pl.CostEstimate(flops=1000, bytes_accessed=1000, transcendentals=0),
    )(*pieces, *state)


def feed_weights_kernel(place_ref, *refs):
    group = (len(refs) - 3) // 3
    acts, tokens, grads = refs[:group], refs[group : 2 * group], refs[2 * group : 3 * group]
    own_ref, *far_refs = refs[3 * group :]
    half = own_ref.shape[-1]
    mine, theirs = halves(own_ref, place_ref[0], half)

    for step, rights in enumerate((tokens, tokens, grads)):

        @pl.when(pl.program_id(0) == step)
        def _():
            far_ref = far_refs[0].at[step] if step < 2 else far_refs[1]
            for out, lanes in ((own_ref, mine), (far_ref, theirs)):
                total = None
                for act, right in zip(acts, rights):
                    for row in range(act.shape[0]):
                        part = dot_tn(act[row], right[row, :, lanes])
                        total = part if total is None else total + part
                out[...] = total.astype(low)


def middle_back_kernel(
    one_ref, two_ref, three_ref, middle_ref, gain_ref, grad_ref,
    out_ref, low_ref, turned_ref, gain_out_ref,
):
    cotangent = one_ref[...].astype(wide) + two_ref[...].astype(wide) + three_ref[...].astype(wide)
    back, gain_part = norm_back(middle_ref[...], gain_ref[...], cotangent)
    total = grad_ref[...] + back
    out_ref[...] = total
    low_ref[...] = total.astype(low)
    turned_ref[...] = total.T.astype(low)
    gain_out_ref[...] = gain_part


def normed_grad_kernel(place_ref, *refs):
    group = (len(refs) - 1) // 3
    grads, mine_refs, theirs_refs = refs[:group], refs[group : 2 * group], refs[2 * group : 3 * group]
    out_ref = refs[-1]
    half = mine_refs[0].shape[1]
    mine, theirs = halves(out_ref, place_ref[0], half)
    for lanes, weights in ((mine, mine_refs), (theirs, theirs_refs)):
        total = None
        for grad, weight in zip(grads, weights):
            for which in range(3):
                part = dot_nt(grad[which], weight[which])
                total = part if total is None else total + part
        out_ref[:, lanes] = total


def input_back_kernel(
    here_ref, before_ref, after_ref, hidden_ref, gain_ref, grad_ref, out_ref, gain_out_ref
):
    seg_len = hidden_ref.shape[0]
    gain = gain_ref[...]
    hidden = hidden_ref[...].astype(wide)
    centre = here_ref[HALF : HALF + seg_len]
    cotangent = jnp.concatenate(
        [
            centre[:HALF] + before_ref[...].astype(wide),
            centre[HALF : seg_len - HALF],
            centre[seg_len - HALF :] + after_ref[...].astype(wide),
        ],
        axis=0,
    )
    back, gain_part = norm_back(hidden, gain, cotangent)
    out_ref[...] = grad_ref[...] + back
    gain_out_ref[...] = gain_part


def by_row(shape):
    rest = tuple(shape[1:])
    return pl.BlockSpec((None,) + rest, lambda r: (r,) + (0,) * len(rest))


def fixed(shape):
    return pl.BlockSpec(tuple(shape), lambda r: (0,) * len(shape))


def spec_of(values, kind):
    if kind == "row":
        return by_row(values.shape)
    if kind == "second":
        return pl.BlockSpec(
            (values.shape[0], None) + tuple(values.shape[2:]),
            lambda r: (0, r) + (0,) * (len(values.shape) - 2),
        )
    if kind == "step":
        return pl.BlockSpec((None,) + tuple(values.shape[1:]), lambda r: (r, 0, 0, 0))
    if kind == "head":
        return pl.BlockSpec((3,) + tuple(values.shape[1:]), lambda r: (0, 0, 0))
    if kind == "last":
        return pl.BlockSpec((None,) + tuple(values.shape[1:]), lambda r: (3, 0, 0))
    if kind == "scalar":
        return pl.BlockSpec(memory_space=pltpu.SMEM)
    return fixed(values.shape)


def in_hbm(values):
    return pltpu.with_memory_space_constraint(values, pltpu.HBM)


def run(kernel, name, steps, ins, outs, scratch=(), far_outs=()):
    return pl.pallas_call(
        kernel,
        grid=(steps,),
        in_specs=[spec_of(value, kind) for value, kind in ins],
        out_specs=[spec_of(shape, kind) for shape, kind in outs],
        out_shape=[
            pltpu.HBM(shape.shape, shape.dtype) if index in far_outs else shape
            for index, (shape, kind) in enumerate(outs)
        ],
        scratch_shapes=list(scratch),
        name=name,
        compiler_params=pltpu.CompilerParams(vmem_limit_bytes=VMEM),
        cost_estimate=pl.CostEstimate(flops=1000, bytes_accessed=1000, transcendentals=0),
    )(*[value for value, kind in ins])


def doc_tables(starts, places):
    inside = (places >= 0) & (places < L)
    before = starts[..., None, :] <= places[..., :, None]
    number = jnp.sum(before.astype(jnp.int32), axis=-1) - 1
    begins = jnp.max(jnp.where(before, starts[..., None, :], 0), axis=-1)
    return (jnp.where(inside, number, -1), places - begins)


def adam(weight, momentum, variance, gradient, step_rate, shrink_rate):
    momentum_new = beta_first * momentum + (1.0 - beta_first) * gradient
    variance_new = beta_second * variance + (1.0 - beta_second) * gradient * gradient
    first_hat = momentum_new / (1.0 - beta_first**STEP)
    second_hat = variance_new / (1.0 - beta_second**STEP)
    updated = weight - step_rate * (
        first_hat / (jnp.sqrt(second_hat) + adam_eps) + shrink_rate * weight
    )
    return (updated, momentum_new, variance_new)


def take(values, index, size, dim):
    return lax.dynamic_slice_in_dim(values, index * size, size, axis=dim)


def joined(bit, mine, theirs, dim):
    return jnp.where(
        bit == 0,
        jnp.concatenate([mine, theirs], axis=dim),
        jnp.concatenate([theirs, mine], axis=dim),
    )


def after(values, *others):
    return lax.optimization_barrier((values,) + others)[0]


def all_after(values, *others):
    return lax.optimization_barrier(tuple(values) + others)[: len(values)]


EVEN = [(0, 1), (1, 0), (2, 3), (3, 2)]
ACROSS = [(0, 2), (2, 0), (1, 3), (3, 1)]


def line_one(values, dim):
    if lax.axis_size("ctx") != 4:
        return values, None
    parity = lax.rem(lax.axis_index("ctx"), 2)
    size = values.shape[dim] // 2
    got = lax.ppermute(take(values, 1 - parity, size, dim), "ctx", EVEN)
    return take(values, parity, size, dim), got


def line_two(kept, got):
    if got is None:
        return kept, None
    part = added(kept, got)
    return part, lax.ppermute(part, "ctx", ACROSS)


def line_three(kept, got):
    if got is None:
        return kept, None
    part = added(kept, got)
    return part, lax.ppermute(part, "ctx", EVEN)


def line_end(kept, got, dim):
    if got is None:
        return lax.psum(kept.astype(wide), "ctx").astype(low)
    return joined(lax.rem(lax.axis_index("ctx"), 2), kept, got, dim)


def added(*values):
    return sum(value.astype(wide) for value in values).astype(low)


def turned_state(axes, *values):
    return [jnp.transpose(v, axes) for v in values]


def turned_back(axes, values):
    return tuple(jnp.transpose(v, axes) for v in values)


def body(
    hidden_in,
    doc_starts,
    grad_out,
    qkv_weight,
    output_weight,
    geglu_weight,
    down_weight,
    norm_gains,
    qkv_momentum,
    qkv_variance,
    output_momentum,
    output_variance,
    geglu_momentum,
    geglu_variance,
    down_momentum,
    down_variance,
    gains_momentum,
    gains_variance,
):
    rows, seg_len, model_width = hidden_in.shape
    shards = lax.axis_size("shard")
    paired = shards == 2
    half = model_width // 2
    shard_place = lax.axis_index("shard")
    group_place = lax.axis_index("tp")
    ctx_place = lax.axis_index("ctx")
    place = shard_place if paired else jnp.zeros_like(shard_place)
    place_one = place.astype(jnp.int32).reshape(1)
    group = (0, 1, 2, 3)
    span = seg_len + 2 * HALF
    cols = qkv_weight.shape[2]
    units = down_weight.shape[0]

    count = lax.axis_size("ctx")
    forward = [(i, i + 1) for i in range(count - 1)]
    backward = [(i + 1, i) for i in range(count - 1)]
    before = lax.ppermute(hidden_in[:, seg_len - HALF :], "ctx", forward)
    after_edge = lax.ppermute(hidden_in[:, :HALF], "ctx", backward)

    def both(values, dim):
        if paired:
            return values, shard_swap(values)
        full = lax.all_gather(values, "shard", axis=dim, tiled=True)
        return (
            lax.slice_in_dim(full, 0, half, axis=dim),
            lax.slice_in_dim(full, half, 2 * half, axis=dim),
        )

    gains_near = norm_gains.astype(low)
    if paired:
        gains_low = joined(place, gains_near, shard_swap(after(gains_near, before, after_edge)), 1)
    else:
        gains_low = lax.all_gather(gains_near, "shard", axis=1, tiled=True)
    gain_one = gains_low[0:1].astype(wide)
    gain_two = gains_low[1:2].astype(wide)

    qkv_turned = jnp.transpose(qkv_weight, (1, 0, 2))
    geglu_turned = jnp.transpose(geglu_weight, (1, 2, 0))
    block_low = jnp.concatenate(
        [qkv_turned.astype(low), jnp.transpose(output_weight).astype(low)[None]], axis=0
    )
    mine, theirs = both(block_low, 1)
    geglu_low = after(geglu_turned, before, after_edge).astype(low).reshape(2 * units, -1)
    geglu_mine, geglu_theirs = both(geglu_low, 1)
    down_low = after(down_weight, before, after_edge).astype(low)
    down_mine, down_theirs = both(down_low, 1)

    grad_low = after(grad_out, before, after_edge).astype(low)
    offset = ctx_place * seg_len
    ext_places = offset - HALF + jnp.arange(span, dtype=jnp.int32)
    tp_rows = lax.dynamic_slice_in_dim(doc_starts, group_place * rows, rows, axis=0)
    ext_doc, ext_place = doc_tables(tp_rows, ext_places)
    inverse = theta_base ** (-2.0 * jnp.arange(HD // 2, dtype=wide) / HD)
    angles = ext_place.astype(wide)[..., None] * inverse
    cosine, sine = jnp.cos(angles), jnp.sin(angles)
    cosine = jnp.concatenate([cosine] * 4, axis=-1)
    sine = jnp.concatenate([-sine, sine, -sine, sine], axis=-1)
    blocks = seg_len // QBLOCK
    query_doc = ext_doc[:, HALF : HALF + seg_len].reshape(rows, blocks, QBLOCK)
    key_doc = jnp.stack(
        [ext_doc[:, b * QBLOCK : b * QBLOCK + KBLOCK] for b in range(blocks)], axis=1
    )
    gap = jnp.arange(QBLOCK)[:, None] + HALF - jnp.arange(KBLOCK)[None, :]
    allowed = (jnp.abs(gap) <= HALF) & (query_doc[..., :, None] == key_doc[..., None, :])
    bias = jnp.where(allowed, 0.0, masked_value).astype(wide)

    normed, normed_turned = run(
        first_norm_kernel, "first_norm", rows,
        [(before, "row"), (hidden_in, "row"), (after_edge, "row"), (gain_one, "all")],
        [
            (jax.ShapeDtypeStruct((rows, span, model_width), low), "row"),
            (jax.ShapeDtypeStruct((rows, model_width, span), low), "row"),
        ],
        far_outs=(1,),
    )

    far_mine = chip_swap(mine)
    near_mine = core_swap(mine)
    theirs = after(
        theirs, before, after_edge, cosine, sine, bias, geglu_low, down_low, grad_low, far_mine
    )
    far_theirs = chip_swap(theirs)
    weights = [(mine, theirs), (near_mine, core_swap(theirs))]
    scalar = (place_one, "scalar")
    tables = [(cosine, "row"), (sine, "row"), (bias, "row")]
    short = jax.ShapeDtypeStruct((rows, seg_len, cols), low)
    long = jax.ShapeDtypeStruct((rows, span, cols), low)
    saved = []
    for j in group:
        tokens_here = normed if j == 0 else after(normed, saved[j - 1][3])
        if j == 2:
            far_theirs = after(far_theirs, saved[1][3])
            weights.append((far_mine, far_theirs))
            weights.append((core_swap(far_mine), core_swap(far_theirs)))
            grad_far = chip_swap(after(grad_low, far_theirs))
        if j == 3:
            tokens_here = after(tokens_here, geglu_theirs)
        saved.append(
            run(
                attend_kernel, "attend", rows,
                [scalar, (tokens_here, "row"), (weights[j][0], "head"), (weights[j][1], "head")]
                + tables,
                [(short, "row"), (long, "row"), (long, "row"), (short, "row")],
                far_outs=(0, 1, 2),
            )
        )
    attended = [one[3] for one in saved]
    attended[3] = after(attended[3], down_theirs, grad_far)
    middle, normed_two = run(
        second_norm_kernel, "second_norm", rows,
        [scalar]
        + [(one, "row") for one in attended]
        + [(weights[j][0], "last") for j in group]
        + [(weights[j][1], "last") for j in group]
        + [(hidden_in, "row"), (gain_two, "all")],
        [
            (jax.ShapeDtypeStruct((rows, seg_len, model_width), wide), "row"),
            (jax.ShapeDtypeStruct((rows, seg_len, model_width), low), "row"),
        ],
    )

    normed_far = chip_swap(normed_two)
    normed_one = core_swap(normed_two)
    grad_one = core_swap(grad_low)
    act_rows = jax.ShapeDtypeStruct((3, rows, seg_len, units), low)
    full_rows = jax.ShapeDtypeStruct((rows, seg_len, model_width), low)

    def feed(tokens, grads):
        done = run(
            feed_kernel, "feed", rows,
            [scalar]
            + [(one, "row") for one in tokens]
            + [(one, "row") for one in grads]
            + [(one, "all") for one in (geglu_mine, geglu_theirs, down_mine, down_theirs)],
            [(act_rows, "second"), (full_rows, "row"), (full_rows, "row")] * len(tokens),
            far_outs=(1, 4),
        )
        return [done[3 * i : 3 * i + 3] for i in range(len(tokens))]

    tokens, grads = [normed_two, normed_one], [grad_low, grad_one]
    fed = feed(tokens, grads)
    back_one, out_one = core_swap(fed[1][2]), core_swap(fed[1][1])
    normed_far = after(normed_far, fed[0][2], back_one, out_one)
    tokens += [normed_far, core_swap(normed_far)]
    grads += [grad_far, core_swap(grad_far)]
    fed += feed(tokens[2:], grads[2:])
    back_three = core_swap(fed[3][2])
    back_far = chip_swap(added(fed[2][2], back_three))
    out_three = core_swap(after(fed[3][1], back_three))

    feed_part = jax.ShapeDtypeStruct((3, units, half), low)
    feed_own, *feed_other = run(
        feed_weights_kernel, "feed_weights", 3,
        [scalar]
        + [(after(fed[0][0], back_three), "step")]
        + [(one[0], "step") for one in fed[1:]]
        + [(one, "all") for one in tokens]
        + [(one, "all") for one in grads],
        [
            (feed_part, "row"),
            (jax.ShapeDtypeStruct((2, units, half), low), "all"),
            (jax.ShapeDtypeStruct((units, half), low), "all"),
        ],
    )

    out_sum = added(fed[2][1], after(out_three, feed_own))
    out_far = chip_swap(out_sum)
    back_far = after(back_far, feed_own, out_sum)
    gain_shape = jax.ShapeDtypeStruct((rows, 1, model_width), wide)
    grad_middle, middle_low, middle_turned, gain_two_part = run(
        middle_back_kernel, "middle_back", rows,
        [
            (after(fed[0][2], feed_own), "row"), (back_one, "row"), (back_far, "row"),
            (middle, "row"), (gain_two, "all"), (grad_out, "row"),
        ],
        [
            (jax.ShapeDtypeStruct(grad_out.shape, wide), "row"),
            (jax.ShapeDtypeStruct(grad_out.shape, low), "row"),
            (jax.ShapeDtypeStruct((rows, model_width, seg_len), low), "row"),
            (gain_shape, "row"),
        ],
        far_outs=(0, 1, 2),
    )

    if paired:
        geglu_got, down_got = [shard_swap(one) for one in feed_other]
    else:
        feed_other[1] = feed_other[1][None]
        feed_got = lax.psum_scatter(
            jnp.concatenate([feed_own, jnp.concatenate(feed_other, axis=0)], axis=2),
            "shard", scatter_dimension=2, tiled=True,
        )
        geglu_got, down_got = feed_got[:2], feed_got[2]

    mixed, own, other = [None] * 4, [None] * 4, [None] * 4
    weight_part = jax.ShapeDtypeStruct((4, half, cols), low)
    def attend_back(j, sums, *before_it):
        queries, keys, values, out = saved[j]
        mixed[j], own[j], other[j] = run(
            functools.partial(attend_back_kernel, bool(sums)), "attend_back", rows,
            [
                scalar, (in_hbm(after(middle_low, *before_it)), "row"),
                (in_hbm(middle_turned), "row"), (in_hbm(normed_turned), "row"), (out, "row"),
                (weights[j][0], "last"), (weights[j][1], "last"),
                (in_hbm(queries), "row"), (in_hbm(keys), "row"), (in_hbm(values), "row"),
            ]
            + tables
            + [(one, "all") for one in sums],
            [
                (jax.ShapeDtypeStruct((3, rows, span, cols), low), "second"),
                (weight_part, "all"), (weight_part, "all"),
            ],
            scratch=[
                pltpu.VMEM((span, cols), wide), pltpu.VMEM((span, cols), wide),
                pltpu.VMEM((8, half, cols), wide),
            ],
            far_outs=(0,),
        )

    attend_back(3, (), back_far)
    far_sums = core_swap(own[3]), core_swap(other[3])
    attend_back(1, (), mixed[3])
    near_sums = core_swap(own[1]), core_swap(other[1])
    geglu_got = after(geglu_got, mixed[1])
    geglu_part = added(feed_own[:2], geglu_got) if paired else geglu_got
    geglu_line = line_one(geglu_part, 0)
    attend_back(2, far_sums, mixed[1], geglu_got, out_far)
    far_got = shard_swap(other[2]) if paired else None
    geglu_line = line_two(*all_after(geglu_line, mixed[2]))
    down_got = after(down_got, mixed[2])
    down_part = added(feed_own[2], down_got) if paired else down_got
    down_line = line_one(down_part, 1)
    attend_back(0, near_sums, mixed[2], geglu_line[0], down_got)
    down_line = line_two(*all_after(down_line, mixed[0]))

    cut = half // 2
    if paired:
        near_got = [shard_swap(other[0][:, i * cut : (i + 1) * cut]) for i in (0, 1)]
        far_part = added(own[2], after(far_got, down_line[0]))
    else:
        scatter = functools.partial(
            lax.psum_scatter, axis_name="shard", scatter_dimension=1, tiled=True
        )
        far_part = scatter(jnp.concatenate([own[2], other[2]], axis=1))
        near_sum = scatter(jnp.concatenate([own[0], other[0]], axis=1))
    far_rows = far_part.shape[1] // 2
    far = [chip_swap(far_part[:, i * far_rows : (i + 1) * far_rows]) for i in (0, 1)]

    def cut_of(index, *others):
        rows_at = slice(index * far_rows, (index + 1) * far_rows)
        if paired:
            got = all_after((near_got[index], far[index]), *others)
            return added(own[0][:, rows_at], *got)
        return added(near_sum[:, rows_at], after(far[index], *others))

    (normed_grad,) = run(
        normed_grad_kernel, "normed_grad", rows,
        [scalar]
        + [(after(mixed[0], far_part), "second")]
        + [(mixed[j], "second") for j in group[1:]]
        + [(weights[j][0], "head") for j in group]
        + [(weights[j][1], "head") for j in group],
        [(jax.ShapeDtypeStruct((rows, span, model_width), wide), "row")],
    )
    to_before = lax.ppermute(normed_grad[:, :HALF].astype(low), "ctx", backward)
    to_after = lax.ppermute(normed_grad[:, HALF + seg_len :].astype(low), "ctx", forward)


    geglu_line = line_three(*all_after(geglu_line, normed_grad))
    down_line = line_three(*all_after(down_line, normed_grad))
    first = line_one(cut_of(0, normed_grad), 0)
    if paired:
        far[1] = after(far[1], near_got[1])
    to_before, to_after = all_after(
        (to_before, to_after), first[0], far[1], *geglu_line, down_line[0]
    )
    grad_in, gain_one_part = run(
        input_back_kernel, "input_back", rows,
        [
            (normed_grad, "row"), (to_after, "row"), (to_before, "row"), (hidden_in, "row"),
            (gain_one, "all"), (grad_middle, "row"),
        ],
        [(jax.ShapeDtypeStruct(grad_out.shape, wide), "row"), (gain_shape, "row")],
    )
    result = middle + fed[0][1].astype(wide) + out_one.astype(wide) + out_far.astype(wide)
    hidden_out = result.astype(low)

    first = line_two(*all_after(first, grad_in))
    second = line_one(cut_of(1, hidden_out, first[0]), 0)
    geglu_sum, down_sum = line_end(*geglu_line, 0), line_end(*down_line, 1)
    geglu_set = turned_back(
        (2, 0, 1),
        run_update(
            "update_geglu", rate_geglu, [after(geglu_sum, second[0])],
            turned_state((1, 2, 0), geglu_weight, geglu_momentum, geglu_variance), 0, False, False,
        ),
    )
    first = line_three(*all_after(first, geglu_set[0]))
    second = line_two(*all_after(second, first[0]))
    down_set = tuple(
        v[0]
        for v in run_update(
            "update_down", rate_down, [after(down_sum, second[0])[None]],
            [v[None] for v in (down_weight, down_momentum, down_variance)], 0, False, False,
        )
    )
    gain_one_part = after(gain_one_part, second[0])
    second = line_three(*all_after(second, down_set[0]))
    gain_sum = jnp.concatenate(
        [jnp.sum(gain_one_part, axis=0), jnp.sum(gain_two_part, axis=0)], axis=0
    )
    gain_sum = gain_sum + core_swap(gain_sum)
    gain_sum = gain_sum + chip_swap(gain_sum)
    gain_sum = gain_sum + shard_swap(gain_sum) if paired else lax.psum(gain_sum, "shard")
    if lax.axis_size("ctx") == 4:
        gain_sum = gain_sum + lax.ppermute(gain_sum, "ctx", EVEN)
        gain_sum = gain_sum + lax.ppermute(gain_sum, "ctx", ACROSS)
    else:
        gain_sum = lax.psum(gain_sum, "ctx")
    gains_here = norm_gains.shape[1]
    gain_grad = lax.dynamic_slice_in_dim(gain_sum, shard_place * gains_here, gains_here, axis=1)

    block_sums = [line_end(*one, 0) for one in (first, second)]
    qkv_set = turned_back(
        (1, 0, 2),
        run_update(
            "update_qkv", rate_qkv, block_sums,
            turned_state((1, 0, 2), qkv_weight, qkv_momentum, qkv_variance), 0, False, True,
        ),
    )
    output_set = tuple(
        v[0]
        for v in run_update(
            "update_output", rate_output, block_sums,
            [v[None] for v in (output_weight, output_momentum, output_variance)], 3, True, True,
        )
    )
    gains_set = adam(norm_gains, gains_momentum, gains_variance, gain_grad, rate_gains, 0.0)
    return (hidden_out, grad_in) + qkv_set + output_set + geglu_set + down_set + gains_set


def solution(mesh):
    tokens = P(("shard", "tp"), "ctx", None)
    split_in = P("shard", None, "tp")
    split_out = P("tp", "shard")
    gains = P(None, "shard")
    return jax.shard_map(
        body,
        mesh=mesh,
        in_specs=(
            (tokens, P("shard", None), tokens, split_in, split_out, split_in, split_out, gains)
            + (split_in, split_in, split_out, split_out)
            + (split_in, split_in, split_out, split_out)
            + (gains, gains)
        ),
        out_specs=(
            (tokens, tokens)
            + (split_in,) * 3
            + (split_out,) * 3
            + (split_in,) * 3
            + (split_out,) * 3
            + (gains,) * 3
        ),
        check_vma=False,
    )
```

```python
import functools
import math

import jax
import jax.numpy as jnp
from jax import lax
from jax.experimental import pallas as pl
from jax.experimental.pallas import tpu as pltpu
from jax.sharding import PartitionSpec as P

HD = 64
HALF = 64
L = 1024
STEP = 10
PAIR = 2 * HD
QBLOCK = 128
KBLOCK = QBLOCK + 2 * HALF

theta_base = 10000.0
norm_eps = 1e-05
beta_first = 0.9
beta_second = 0.98
adam_eps = 1e-06
decay_rate = 1e-05
rate_qkv = 0.06
rate_output = 0.35
rate_geglu = 0.06
rate_down = 0.04
rate_gains = 0.5
masked_value = -1e30

low = jnp.bfloat16
wide = jnp.float32
SCALING = 1.0 / math.sqrt(HD)
VMEM = 40 * 1024 * 1024

CORE_SWAP = [(0, 1), (1, 0), (2, 3), (3, 2)]
CHIP_SWAP = [(0, 2), (2, 0), (1, 3), (3, 1)]


def core_swap(values):
    return lax.ppermute(values, "tp", CORE_SWAP)


def chip_swap(values):
    return lax.ppermute(values, "tp", CHIP_SWAP)


def shard_swap(values):
    return lax.ppermute(values, "shard", [(0, 1), (1, 0)])


def dot(a, b):
    return lax.dot_general(a, b, (((1,), (0,)), ((), ())), preferred_element_type=wide)


def dot_nt(a, b):
    return lax.dot_general(a, b, (((1,), (1,)), ((), ())), preferred_element_type=wide)


def dot_tn(a, b):
    return lax.dot_general(a, b, (((0,), (0,)), ((), ())), preferred_element_type=wide)


def normalized(values):
    centered = values - jnp.mean(values, axis=-1, keepdims=True)
    spread = jnp.mean(centered * centered, axis=-1, keepdims=True)
    inverse = lax.rsqrt(spread + norm_eps)
    return centered * inverse, inverse


def norm_back(values, gain, cotangent):
    unit, inverse = normalized(values)
    scaled = cotangent * gain
    first = jnp.mean(scaled, axis=-1, keepdims=True)
    second = jnp.mean(scaled * unit, axis=-1, keepdims=True)
    gain_part = jnp.sum(cotangent * unit, axis=0, keepdims=True)
    return (scaled - first - unit * second) * inverse, gain_part


def turned(values, cosine, sine):
    half_len = HD // 2
    lane = lax.broadcasted_iota(jnp.int32, values.shape, 1)
    ahead = pltpu.roll(values, PAIR - half_len, 1)
    behind = pltpu.roll(values, half_len, 1)
    other = jnp.where(lane % HD < half_len, ahead, behind)
    return values * cosine + other * sine


def head_stack(values):
    lane = lax.broadcasted_iota(jnp.int32, values.shape, 1)
    zero = jnp.zeros_like(values)
    return jnp.concatenate(
        [jnp.where(lane < HD, values, zero), jnp.where(lane < HD, zero, values)], axis=0
    )


def head_join(values):
    rows = values.shape[0] // 2
    upper, lower = values[:rows], values[rows:]
    lane = lax.broadcasted_iota(jnp.int32, upper.shape, 1)
    return jnp.where(lane < HD, upper, lower)


def chances_of(query_stack, keys, bias):
    scores = dot_nt(query_stack, keys) * SCALING + jnp.concatenate([bias, bias], axis=0)
    weights = jnp.exp(scores - jnp.max(scores, axis=-1, keepdims=True))
    return weights * (1.0 / jnp.sum(weights, axis=-1, keepdims=True))


def halves(ref_values, place, half):
    mine = pl.ds(pl.multiple_of(place * half, half), half)
    theirs = pl.ds(pl.multiple_of((1 - place) * half, half), half)
    return mine, theirs


def first_norm_kernel(before_ref, here_ref, after_ref, gain_ref, out_ref, turned_ref):
    tokens = [ref[...].astype(wide) for ref in (before_ref, here_ref, after_ref)]
    normed = normalized(jnp.concatenate(tokens, axis=0))[0] * gain_ref[...]
    out_ref[...] = normed.astype(low)
    turned_ref[...] = normed.T.astype(low)


def attend_kernel(
    place_ref, normed_ref, mine_ref, theirs_ref, cos_ref, sin_ref, bias_ref,
    query_ref, key_ref, value_ref, out_ref,
):
    seg_len = query_ref.shape[0]
    half = mine_ref.shape[1]
    mine, theirs = halves(normed_ref, place_ref[0], half)
    inner = slice(HALF, HALF + seg_len)

    def project(which, rows):
        return dot(normed_ref[rows, mine], mine_ref[which]) + dot(
            normed_ref[rows, theirs], theirs_ref[which]
        )

    whole = slice(0, normed_ref.shape[0])
    queries, keys = project(0, inner), project(1, whole)
    value_ref[...] = project(2, whole).astype(low)
    for first in range(0, query_ref.shape[1], PAIR):
        lanes = slice(first, first + PAIR)
        query_ref[:, lanes] = turned(queries[:, lanes], cos_ref[inner], sin_ref[inner]).astype(low)
        key_ref[:, lanes] = turned(keys[:, lanes], cos_ref[...], sin_ref[...]).astype(low)
    for first in range(0, query_ref.shape[1], PAIR):
        lanes = slice(first, first + PAIR)
        for block in range(seg_len // QBLOCK):
            rows = slice(block * QBLOCK, block * QBLOCK + QBLOCK)
            reach = slice(block * QBLOCK, block * QBLOCK + KBLOCK)
            chances = chances_of(head_stack(query_ref[rows, lanes]), key_ref[reach, lanes], bias_ref[block])
            out_ref[rows, lanes] = head_join(dot(chances.astype(low), value_ref[reach, lanes])).astype(low)


def attend_back_kernel(chained, *refs):
    (
        place_ref, grad_ref, grad_turned_ref, normed_ref, attended_ref, mine_ref, theirs_ref,
        query_ref, key_ref, value_ref, cos_ref, sin_ref, bias_ref,
    ) = refs[:13]
    before_refs = refs[13:15] if chained else ()
    mixed_ref, own_ref, far_ref, key_sum, value_sum, weight_sum = refs[-6:]
    seg_len = query_ref.shape[0]
    half = mine_ref.shape[0]
    mine, theirs = halves(grad_ref, place_ref[0], half)
    inner = slice(HALF, HALF + seg_len)
    grad_out = (
        dot(grad_ref[:, mine], mine_ref[...]) + dot(grad_ref[:, theirs], theirs_ref[...])
    ).astype(low)
    key_sum[...] = jnp.zeros_like(key_sum)
    value_sum[...] = jnp.zeros_like(value_sum)
    edge = jnp.zeros((HALF, query_ref.shape[1]), low)
    mixed_ref[0, :HALF] = edge
    mixed_ref[0, HALF + seg_len :] = edge
    for first in range(0, query_ref.shape[1], PAIR):
        lanes = slice(first, first + PAIR)
        for block in range(seg_len // QBLOCK):
            rows = slice(block * QBLOCK, block * QBLOCK + QBLOCK)
            reach = slice(block * QBLOCK, block * QBLOCK + KBLOCK)
            place_rows = slice(HALF + block * QBLOCK, HALF + block * QBLOCK + QBLOCK)
            queries = head_stack(query_ref[rows, lanes])
            grads = head_stack(grad_out[rows, lanes])
            keys, values = key_ref[reach, lanes], value_ref[reach, lanes]
            chances = chances_of(queries, keys, bias_ref[block])
            grad_chances = dot_nt(grads, values)
            weighted = chances * grad_chances
            grad_scores = (
                weighted - chances * jnp.sum(weighted, axis=-1, keepdims=True)
            ).astype(low)
            value_sum[reach, lanes] += dot_tn(chances.astype(low), grads)
            key_sum[reach, lanes] += dot_tn(grad_scores, queries)
            grad_queries = head_join(dot(grad_scores, keys)) * SCALING
            mixed_ref[0, place_rows, lanes] = turned(
                grad_queries, cos_ref[place_rows], -sin_ref[place_rows]
            ).astype(low)
        mixed_ref[1, :, lanes] = turned(
            key_sum[:, lanes] * SCALING, cos_ref[...], -sin_ref[...]
        ).astype(low)
    mixed_ref[2] = value_sum[...].astype(low)

    parts = []
    for lanes in (mine, theirs):
        parts += [dot(normed_ref[lanes], mixed_ref[which]) for which in range(3)]
        parts.append(dot(grad_turned_ref[lanes], attended_ref[...]))

    @pl.when(pl.program_id(0) == 0)
    def _():
        for index, part in enumerate(parts):
            if chained:
                part += before_refs[index // 4][index % 4].astype(wide)
            weight_sum[index] = part

    @pl.when(pl.program_id(0) > 0)
    def _():
        for index, part in enumerate(parts):
            weight_sum[index] += part

    @pl.when(pl.program_id(0) == pl.num_programs(0) - 1)
    def _():
        for index in range(4):
            own_ref[index] = weight_sum[index].astype(low)
            far_ref[index] = weight_sum[4 + index].astype(low)


def second_norm_kernel(place_ref, *refs):
    group = (len(refs) - 4) // 3
    attended, mine_refs, theirs_refs = refs[:group], refs[group : 2 * group], refs[2 * group : 3 * group]
    hidden_ref, gain_ref, middle_ref, normed_ref = refs[3 * group :]
    half = mine_refs[0].shape[0]
    mine, theirs = halves(middle_ref, place_ref[0], half)
    for lanes, weights in ((mine, mine_refs), (theirs, theirs_refs)):
        total = hidden_ref[:, lanes].astype(wide)
        for one, weight in zip(attended, weights):
            total += dot_nt(one[...], weight[...])
        middle_ref[:, lanes] = total
    normed_ref[...] = (normalized(middle_ref[...])[0] * gain_ref[...]).astype(low)


def feed_kernel(place_ref, *refs):
    group = (len(refs) - 4) // 5
    tokens, grads = refs[:group], refs[group : 2 * group]
    mine_ref, theirs_ref, down_mine_ref, down_theirs_ref = refs[2 * group : 2 * group + 4]
    outs = refs[2 * group + 4 :]
    half = mine_ref.shape[1]
    units = down_mine_ref.shape[0]
    mine, theirs = halves(mine_ref, place_ref[0], half)
    for index in range(group):
        normed_ref, grad_ref = tokens[index], grads[index]
        act_ref, out_ref, back_ref = outs[3 * index : 3 * index + 3]
        own, far = normed_ref[:, mine], normed_ref[:, theirs]
        gate = dot_nt(own, mine_ref[:units]) + dot_nt(far, theirs_ref[:units])
        up = dot_nt(own, mine_ref[units:]) + dot_nt(far, theirs_ref[units:])
        grad_inner = dot_nt(grad_ref[:, mine], down_mine_ref[...]) + dot_nt(
            grad_ref[:, theirs], down_theirs_ref[...]
        )
        normal = 0.5 * (1.0 + lax.erf(gate * math.sqrt(0.5)))
        density = jnp.exp(-0.5 * gate * gate) * (1.0 / math.sqrt(2.0 * math.pi))
        gelu = gate * normal
        inner = (gelu * up).astype(low)
        grad_gate = (grad_inner * up * (normal + gate * density)).astype(low)
        grad_up = (grad_inner * gelu).astype(low)
        act_ref[0] = grad_gate
        act_ref[1] = grad_up
        act_ref[2] = inner
        for lanes, weight, down in (
            (mine, mine_ref, down_mine_ref), (theirs, theirs_ref, down_theirs_ref)
        ):
            back_ref[:, lanes] = (
                dot(grad_gate, weight[:units]) + dot(grad_up, weight[units:])
            ).astype(low)
            out_ref[:, lanes] = dot(inner, down[...]).astype(low)


def update(weight, momentum, variance, gradient, rate):
    momentum_new = beta_first * momentum + (1.0 - beta_first) * gradient
    variance_new = beta_second * variance + (1.0 - beta_second) * gradient * gradient
    first_hat = momentum_new * (1.0 / (1.0 - beta_first**STEP))
    second_hat = variance_new * (1.0 / (1.0 - beta_second**STEP))
    new = weight - rate * (first_hat / (jnp.sqrt(second_hat) + adam_eps) + decay_rate * weight)
    return new, momentum_new, variance_new


def update_kernel(rate, flip, by_half, count, *refs):
    which = pl.program_id(1) if by_half else 0
    state, outs = refs[count : count + 3], refs[count + 3 :]
    for index in range(count):

        @pl.when(which == index)
        def _():
            gradient = refs[index][...].astype(wide)
            if flip:
                gradient = gradient.T
            for out, value in zip(outs, update(*(one[...] for one in state), gradient, rate)):
                out[...] = value


def run_update(name, rate, pieces, state, skip, flip, by_half):
    dim = 1 if flip else 0
    size = list(state[0].shape[1:])
    size[dim] //= 2
    if size[0] % 8 or size[1] % 128:
        if by_half:
            gradient = jnp.concatenate(pieces, axis=1)[skip : skip + state[0].shape[0]]
        else:
            gradient = pieces[0]
        gradient = gradient.astype(wide)
        if flip:
            gradient = jnp.transpose(gradient, (0, 2, 1))
        return update(*state, gradient, rate)

    def place(c, h):
        return (c, h, 0) if dim == 0 else (c, 0, h)

    spec = pl.BlockSpec((None, *size), place)
    grad_spec = spec
    if by_half:
        cut = size[::-1] if flip else size
        grad_spec = pl.BlockSpec((None, *cut), lambda c, h: (c + skip, 0, 0))
    return pl.pallas_call(
        functools.partial(update_kernel, rate, flip, by_half, len(pieces)),
        grid=(state[0].shape[0], 2),
        in_specs=[grad_spec] * len(pieces) + [spec] * 3,
        out_specs=[spec] * 3,
        out_shape=[jax.ShapeDtypeStruct(state[0].shape, wide)] * 3,
        name=name,
        compiler_params=pltpu.CompilerParams(vmem_limit_bytes=VMEM),
        cost_estimate=pl.CostEstimate(flops=1000, bytes_accessed=1000, transcendentals=0),
    )(*pieces, *state)


def feed_weights_kernel(place_ref, *refs):
    group = (len(refs) - 3) // 3
    acts, tokens, grads = refs[:group], refs[group : 2 * group], refs[2 * group : 3 * group]
    own_ref, *far_refs = refs[3 * group :]
    half = own_ref.shape[-1]
    mine, theirs = halves(own_ref, place_ref[0], half)

    for step, rights in enumerate((tokens, tokens, grads)):

        @pl.when(pl.program_id(0) == step)
        def _():
            far_ref = far_refs[0].at[step] if step < 2 else far_refs[1]
            for out, lanes in ((own_ref, mine), (far_ref, theirs)):
                total = None
                for act, right in zip(acts, rights):
                    for row in range(act.shape[0]):
                        part = dot_tn(act[row], right[row, :, lanes])
                        total = part if total is None else total + part
                out[...] = total.astype(low)


def middle_back_kernel(
    one_ref, two_ref, three_ref, middle_ref, gain_ref, grad_ref,
    out_ref, low_ref, turned_ref, gain_out_ref,
):
    cotangent = one_ref[...].astype(wide) + two_ref[...].astype(wide) + three_ref[...].astype(wide)
    back, gain_part = norm_back(middle_ref[...], gain_ref[...], cotangent)
    total = grad_ref[...] + back
    out_ref[...] = total
    low_ref[...] = total.astype(low)
    turned_ref[...] = total.T.astype(low)
    gain_out_ref[...] = gain_part


def normed_grad_kernel(place_ref, *refs):
    group = (len(refs) - 1) // 3
    grads, mine_refs, theirs_refs = refs[:group], refs[group : 2 * group], refs[2 * group : 3 * group]
    out_ref = refs[-1]
    half = mine_refs[0].shape[1]
    mine, theirs = halves(out_ref, place_ref[0], half)
    for lanes, weights in ((mine, mine_refs), (theirs, theirs_refs)):
        total = None
        for grad, weight in zip(grads, weights):
            for which in range(3):
                part = dot_nt(grad[which], weight[which])
                total = part if total is None else total + part
        out_ref[:, lanes] = total


def input_back_kernel(
    here_ref, before_ref, after_ref, hidden_ref, gain_ref, grad_ref, out_ref, gain_out_ref
):
    seg_len = hidden_ref.shape[0]
    gain = gain_ref[...]
    hidden = hidden_ref[...].astype(wide)
    centre = here_ref[HALF : HALF + seg_len]
    cotangent = jnp.concatenate(
        [
            centre[:HALF] + before_ref[...].astype(wide),
            centre[HALF : seg_len - HALF],
            centre[seg_len - HALF :] + after_ref[...].astype(wide),
        ],
        axis=0,
    )
    back, gain_part = norm_back(hidden, gain, cotangent)
    out_ref[...] = grad_ref[...] + back
    gain_out_ref[...] = gain_part


def by_row(shape):
    rest = tuple(shape[1:])
    return pl.BlockSpec((None,) + rest, lambda r: (r,) + (0,) * len(rest))


def fixed(shape):
    return pl.BlockSpec(tuple(shape), lambda r: (0,) * len(shape))


def spec_of(values, kind):
    if kind == "row":
        return by_row(values.shape)
    if kind == "second":
        return pl.BlockSpec(
            (values.shape[0], None) + tuple(values.shape[2:]),
            lambda r: (0, r) + (0,) * (len(values.shape) - 2),
        )
    if kind == "step":
        return pl.BlockSpec((None,) + tuple(values.shape[1:]), lambda r: (r, 0, 0, 0))
    if kind == "head":
        return pl.BlockSpec((3,) + tuple(values.shape[1:]), lambda r: (0, 0, 0))
    if kind == "last":
        return pl.BlockSpec((None,) + tuple(values.shape[1:]), lambda r: (3, 0, 0))
    if kind == "scalar":
        return pl.BlockSpec(memory_space=pltpu.SMEM)
    return fixed(values.shape)


def in_hbm(values):
    return pltpu.with_memory_space_constraint(values, pltpu.HBM)


def run(kernel, name, steps, ins, outs, scratch=(), far_outs=()):
    return pl.pallas_call(
        kernel,
        grid=(steps,),
        in_specs=[spec_of(value, kind) for value, kind in ins],
        out_specs=[spec_of(shape, kind) for shape, kind in outs],
        out_shape=[
            pltpu.HBM(shape.shape, shape.dtype) if index in far_outs else shape
            for index, (shape, kind) in enumerate(outs)
        ],
        scratch_shapes=list(scratch),
        name=name,
        compiler_params=pltpu.CompilerParams(vmem_limit_bytes=VMEM),
        cost_estimate=pl.CostEstimate(flops=1000, bytes_accessed=1000, transcendentals=0),
    )(*[value for value, kind in ins])


def doc_tables(starts, places):
    inside = (places >= 0) & (places < L)
    before = starts[..., None, :] <= places[..., :, None]
    number = jnp.sum(before.astype(jnp.int32), axis=-1) - 1
    begins = jnp.max(jnp.where(before, starts[..., None, :], 0), axis=-1)
    return (jnp.where(inside, number, -1), places - begins)


def adam(weight, momentum, variance, gradient, step_rate, shrink_rate):
    momentum_new = beta_first * momentum + (1.0 - beta_first) * gradient
    variance_new = beta_second * variance + (1.0 - beta_second) * gradient * gradient
    first_hat = momentum_new / (1.0 - beta_first**STEP)
    second_hat = variance_new / (1.0 - beta_second**STEP)
    updated = weight - step_rate * (
        first_hat / (jnp.sqrt(second_hat) + adam_eps) + shrink_rate * weight
    )
    return (updated, momentum_new, variance_new)


def take(values, index, size, dim):
    return lax.dynamic_slice_in_dim(values, index * size, size, axis=dim)


def joined(bit, mine, theirs, dim):
    return jnp.where(
        bit == 0,
        jnp.concatenate([mine, theirs], axis=dim),
        jnp.concatenate([theirs, mine], axis=dim),
    )


def after(values, *others):
    return lax.optimization_barrier((values,) + others)[0]


def all_after(values, *others):
    return lax.optimization_barrier(tuple(values) + others)[: len(values)]


EVEN = [(0, 1), (1, 0), (2, 3), (3, 2)]
ACROSS = [(0, 2), (2, 0), (1, 3), (3, 1)]


def line_one(values, dim):
    if lax.axis_size("ctx") != 4:
        return values, None
    parity = lax.rem(lax.axis_index("ctx"), 2)
    size = values.shape[dim] // 2
    got = lax.ppermute(take(values, 1 - parity, size, dim), "ctx", EVEN)
    return take(values, parity, size, dim), got


def line_two(kept, got):
    if got is None:
        return kept, None
    part = added(kept, got)
    return part, lax.ppermute(part, "ctx", ACROSS)


def line_three(kept, got):
    if got is None:
        return kept, None
    part = added(kept, got)
    return part, lax.ppermute(part, "ctx", EVEN)


def line_end(kept, got, dim):
    if got is None:
        return lax.psum(kept.astype(wide), "ctx").astype(low)
    return joined(lax.rem(lax.axis_index("ctx"), 2), kept, got, dim)


def added(*values):
    return sum(value.astype(wide) for value in values).astype(low)


def turned_state(axes, *values):
    return [jnp.transpose(v, axes) for v in values]


def turned_back(axes, values):
    return tuple(jnp.transpose(v, axes) for v in values)


def body(
    hidden_in,
    doc_starts,
    grad_out,
    qkv_weight,
    output_weight,
    geglu_weight,
    down_weight,
    norm_gains,
    qkv_momentum,
    qkv_variance,
    output_momentum,
    output_variance,
    geglu_momentum,
    geglu_variance,
    down_momentum,
    down_variance,
    gains_momentum,
    gains_variance,
):
    rows, seg_len, model_width = hidden_in.shape
    shards = lax.axis_size("shard")
    paired = shards == 2
    half = model_width // 2
    shard_place = lax.axis_index("shard")
    group_place = lax.axis_index("tp")
    ctx_place = lax.axis_index("ctx")
    place = shard_place if paired else jnp.zeros_like(shard_place)
    place_one = place.astype(jnp.int32).reshape(1)
    group = (0, 1, 2, 3)
    span = seg_len + 2 * HALF
    cols = qkv_weight.shape[2]
    units = down_weight.shape[0]

    count = lax.axis_size("ctx")
    forward = [(i, i + 1) for i in range(count - 1)]
    backward = [(i + 1, i) for i in range(count - 1)]
    before = lax.ppermute(hidden_in[:, seg_len - HALF :], "ctx", forward)
    after_edge = lax.ppermute(hidden_in[:, :HALF], "ctx", backward)

    def both(values, dim):
        if paired:
            return values, shard_swap(values)
        full = lax.all_gather(values, "shard", axis=dim, tiled=True)
        return (
            lax.slice_in_dim(full, 0, half, axis=dim),
            lax.slice_in_dim(full, half, 2 * half, axis=dim),
        )

    gains_near = norm_gains.astype(low)
    if paired:
        gains_low = joined(place, gains_near, shard_swap(after(gains_near, before, after_edge)), 1)
    else:
        gains_low = lax.all_gather(gains_near, "shard", axis=1, tiled=True)
    gain_one = gains_low[0:1].astype(wide)
    gain_two = gains_low[1:2].astype(wide)

    qkv_turned = jnp.transpose(qkv_weight, (1, 0, 2))
    geglu_turned = jnp.transpose(geglu_weight, (1, 2, 0))
    block_low = jnp.concatenate(
        [qkv_turned.astype(low), jnp.transpose(output_weight).astype(low)[None]], axis=0
    )
    mine, theirs = both(block_low, 1)
    geglu_low = after(geglu_turned, before, after_edge).astype(low).reshape(2 * units, -1)
    geglu_mine, geglu_theirs = both(geglu_low, 1)
    down_low = after(down_weight, before, after_edge).astype(low)
    down_mine, down_theirs = both(down_low, 1)

    grad_low = after(grad_out, before, after_edge).astype(low)
    offset = ctx_place * seg_len
    ext_places = offset - HALF + jnp.arange(span, dtype=jnp.int32)
    tp_rows = lax.dynamic_slice_in_dim(doc_starts, group_place * rows, rows, axis=0)
    ext_doc, ext_place = doc_tables(tp_rows, ext_places)
    inverse = theta_base ** (-2.0 * jnp.arange(HD // 2, dtype=wide) / HD)
    angles = ext_place.astype(wide)[..., None] * inverse
    cosine, sine = jnp.cos(angles), jnp.sin(angles)
    cosine = jnp.concatenate([cosine] * 4, axis=-1)
    sine = jnp.concatenate([-sine, sine, -sine, sine], axis=-1)
    blocks = seg_len // QBLOCK
    query_doc = ext_doc[:, HALF : HALF + seg_len].reshape(rows, blocks, QBLOCK)
    key_doc = jnp.stack(
        [ext_doc[:, b * QBLOCK : b * QBLOCK + KBLOCK] for b in range(blocks)], axis=1
    )
    gap = jnp.arange(QBLOCK)[:, None] + HALF - jnp.arange(KBLOCK)[None, :]
    allowed = (jnp.abs(gap) <= HALF) & (query_doc[..., :, None] == key_doc[..., None, :])
    bias = jnp.where(allowed, 0.0, masked_value).astype(wide)

    normed, normed_turned = run(
        first_norm_kernel, "first_norm", rows,
        [(before, "row"), (hidden_in, "row"), (after_edge, "row"), (gain_one, "all")],
        [
            (jax.ShapeDtypeStruct((rows, span, model_width), low), "row"),
            (jax.ShapeDtypeStruct((rows, model_width, span), low), "row"),
        ],
        far_outs=(1,),
    )

    far_mine = chip_swap(mine)
    near_mine = core_swap(mine)
    theirs = after(
        theirs, before, after_edge, cosine, sine, bias, geglu_low, down_low, grad_low, far_mine
    )
    far_theirs = chip_swap(theirs)
    weights = [(mine, theirs), (near_mine, core_swap(theirs))]
    scalar = (place_one, "scalar")
    tables = [(cosine, "row"), (sine, "row"), (bias, "row")]
    short = jax.ShapeDtypeStruct((rows, seg_len, cols), low)
    long = jax.ShapeDtypeStruct((rows, span, cols), low)
    saved = []
    for j in group:
        tokens_here = normed if j == 0 else after(normed, saved[j - 1][3])
        if j == 2:
            far_theirs = after(far_theirs, saved[1][3])
            weights.append((far_mine, far_theirs))
            weights.append((core_swap(far_mine), core_swap(far_theirs)))
            grad_far = chip_swap(after(grad_low, far_theirs))
        if j == 3:
            tokens_here = after(tokens_here, geglu_theirs)
        saved.append(
            run(
                attend_kernel, "attend", rows,
                [scalar, (tokens_here, "row"), (weights[j][0], "head"), (weights[j][1], "head")]
                + tables,
                [(short, "row"), (long, "row"), (long, "row"), (short, "row")],
                far_outs=(0, 1, 2),
            )
        )
    attended = [one[3] for one in saved]
    attended[3] = after(attended[3], down_theirs, grad_far)
    middle, normed_two = run(
        second_norm_kernel, "second_norm", rows,
        [scalar]
        + [(one, "row") for one in attended]
        + [(weights[j][0], "last") for j in group]
        + [(weights[j][1], "last") for j in group]
        + [(hidden_in, "row"), (gain_two, "all")],
        [
            (jax.ShapeDtypeStruct((rows, seg_len, model_width), wide), "row"),
            (jax.ShapeDtypeStruct((rows, seg_len, model_width), low), "row"),
        ],
    )

    normed_far = chip_swap(normed_two)
    normed_one = core_swap(normed_two)
    grad_one = core_swap(grad_low)
    act_rows = jax.ShapeDtypeStruct((3, rows, seg_len, units), low)
    full_rows = jax.ShapeDtypeStruct((rows, seg_len, model_width), low)

    def feed(tokens, grads):
        done = run(
            feed_kernel, "feed", rows,
            [scalar]
            + [(one, "row") for one in tokens]
            + [(one, "row") for one in grads]
            + [(one, "all") for one in (geglu_mine, geglu_theirs, down_mine, down_theirs)],
            [(act_rows, "second"), (full_rows, "row"), (full_rows, "row")] * len(tokens),
            far_outs=(1, 4),
        )
        return [done[3 * i : 3 * i + 3] for i in range(len(tokens))]

    tokens, grads = [normed_two, normed_one], [grad_low, grad_one]
    fed = feed(tokens, grads)
    back_one, out_one = core_swap(fed[1][2]), core_swap(fed[1][1])
    normed_far = after(normed_far, fed[0][2], back_one, out_one)
    tokens += [normed_far, core_swap(normed_far)]
    grads += [grad_far, core_swap(grad_far)]
    fed += feed(tokens[2:], grads[2:])
    back_three = core_swap(fed[3][2])
    back_far = chip_swap(added(fed[2][2], back_three))
    out_three = core_swap(after(fed[3][1], back_three))

    feed_part = jax.ShapeDtypeStruct((3, units, half), low)
    feed_own, *feed_other = run(
        feed_weights_kernel, "feed_weights", 3,
        [scalar]
        + [(after(fed[0][0], back_three), "step")]
        + [(one[0], "step") for one in fed[1:]]
        + [(one, "all") for one in tokens]
        + [(one, "all") for one in grads],
        [
            (feed_part, "row"),
            (jax.ShapeDtypeStruct((2, units, half), low), "all"),
            (jax.ShapeDtypeStruct((units, half), low), "all"),
        ],
    )

    out_sum = added(fed[2][1], after(out_three, feed_own))
    out_far = chip_swap(out_sum)
    back_far = after(back_far, feed_own, out_sum)
    gain_shape = jax.ShapeDtypeStruct((rows, 1, model_width), wide)
    grad_middle, middle_low, middle_turned, gain_two_part = run(
        middle_back_kernel, "middle_back", rows,
        [
            (after(fed[0][2], feed_own), "row"), (back_one, "row"), (back_far, "row"),
            (middle, "row"), (gain_two, "all"), (grad_out, "row"),
        ],
        [
            (jax.ShapeDtypeStruct(grad_out.shape, wide), "row"),
            (jax.ShapeDtypeStruct(grad_out.shape, low), "row"),
            (jax.ShapeDtypeStruct((rows, model_width, seg_len), low), "row"),
            (gain_shape, "row"),
        ],
        far_outs=(0, 1, 2),
    )

    if paired:
        geglu_got, down_got = [shard_swap(one) for one in feed_other]
    else:
        feed_other[1] = feed_other[1][None]
        feed_got = lax.psum_scatter(
            jnp.concatenate([feed_own, jnp.concatenate(feed_other, axis=0)], axis=2),
            "shard", scatter_dimension=2, tiled=True,
        )
        geglu_got, down_got = feed_got[:2], feed_got[2]

    mixed, own, other = [None] * 4, [None] * 4, [None] * 4
    weight_part = jax.ShapeDtypeStruct((4, half, cols), low)
    def attend_back(j, sums, *before_it):
        queries, keys, values, out = saved[j]
        mixed[j], own[j], other[j] = run(
            functools.partial(attend_back_kernel, bool(sums)), "attend_back", rows,
            [
                scalar, (in_hbm(after(middle_low, *before_it)), "row"),
                (in_hbm(middle_turned), "row"), (in_hbm(normed_turned), "row"), (out, "row"),
                (weights[j][0], "last"), (weights[j][1], "last"),
                (in_hbm(queries), "row"), (in_hbm(keys), "row"), (in_hbm(values), "row"),
            ]
            + tables
            + [(one, "all") for one in sums],
            [
                (jax.ShapeDtypeStruct((3, rows, span, cols), low), "second"),
                (weight_part, "all"), (weight_part, "all"),
            ],
            scratch=[
                pltpu.VMEM((span, cols), wide), pltpu.VMEM((span, cols), wide),
                pltpu.VMEM((8, half, cols), wide),
            ],
            far_outs=(0,),
        )

    attend_back(3, (), back_far)
    far_sums = core_swap(own[3]), core_swap(other[3])
    attend_back(1, (), mixed[3])
    near_sums = core_swap(own[1]), core_swap(other[1])
    geglu_got = after(geglu_got, mixed[1])
    geglu_part = added(feed_own[:2], geglu_got) if paired else geglu_got
    geglu_line = line_one(geglu_part, 0)
    attend_back(2, far_sums, mixed[1], geglu_got, out_far)
    far_got = shard_swap(other[2]) if paired else None
    geglu_line = line_two(*all_after(geglu_line, mixed[2]))
    down_got = after(down_got, mixed[2])
    down_part = added(feed_own[2], down_got) if paired else down_got
    down_line = line_one(down_part, 1)
    attend_back(0, near_sums, mixed[2], geglu_line[0], down_got)
    down_line = line_two(*all_after(down_line, mixed[0]))

    cut = half // 2
    if paired:
        near_got = [shard_swap(other[0][:, i * cut : (i + 1) * cut]) for i in (0, 1)]
        far_part = added(own[2], after(far_got, down_line[0]))
    else:
        scatter = functools.partial(
            lax.psum_scatter, axis_name="shard", scatter_dimension=1, tiled=True
        )
        far_part = scatter(jnp.concatenate([own[2], other[2]], axis=1))
        near_sum = scatter(jnp.concatenate([own[0], other[0]], axis=1))
    far_rows = far_part.shape[1] // 2
    far = [chip_swap(far_part[:, i * far_rows : (i + 1) * far_rows]) for i in (0, 1)]

    def cut_of(index, *others):
        rows_at = slice(index * far_rows, (index + 1) * far_rows)
        if paired:
            got = all_after((near_got[index], far[index]), *others)
            return added(own[0][:, rows_at], *got)
        return added(near_sum[:, rows_at], after(far[index], *others))

    (normed_grad,) = run(
        normed_grad_kernel, "normed_grad", rows,
        [scalar]
        + [(after(mixed[0], far_part), "second")]
        + [(mixed[j], "second") for j in group[1:]]
        + [(weights[j][0], "head") for j in group]
        + [(weights[j][1], "head") for j in group],
        [(jax.ShapeDtypeStruct((rows, span, model_width), wide), "row")],
    )
    to_before = lax.ppermute(normed_grad[:, :HALF].astype(low), "ctx", backward)
    to_after = lax.ppermute(normed_grad[:, HALF + seg_len :].astype(low), "ctx", forward)


    geglu_line = line_three(*all_after(geglu_line, normed_grad))
    first = line_one(cut_of(0, normed_grad), 0)
    if paired:
        far[1] = after(far[1], near_got[1])
    to_before, to_after = all_after(
        (to_before, to_after), first[0], far[1], *geglu_line, *down_line
    )
    grad_in, gain_one_part = run(
        input_back_kernel, "input_back", rows,
        [
            (normed_grad, "row"), (to_after, "row"), (to_before, "row"), (hidden_in, "row"),
            (gain_one, "all"), (grad_middle, "row"),
        ],
        [(jax.ShapeDtypeStruct(grad_out.shape, wide), "row"), (gain_shape, "row")],
    )
    result = middle + fed[0][1].astype(wide) + out_one.astype(wide) + out_far.astype(wide)
    hidden_out = result.astype(low)

    first = line_two(*all_after(first, grad_in))
    second = line_one(cut_of(1, hidden_out, first[0]), 0)
    down_line = line_three(*all_after(down_line, second[0]))
    geglu_sum, down_sum = line_end(*geglu_line, 0), line_end(*down_line, 1)
    geglu_set = turned_back(
        (2, 0, 1),
        run_update(
            "update_geglu", rate_geglu, [after(geglu_sum, second[0])],
            turned_state((1, 2, 0), geglu_weight, geglu_momentum, geglu_variance), 0, False, False,
        ),
    )
    first = line_three(*all_after(first, geglu_set[0]))
    second = line_two(*all_after(second, first[0], *down_line))
    gain_one_part = after(gain_one_part, second[0])
    second = line_three(*second)
    down_set = tuple(
        v[0]
        for v in run_update(
            "update_down", rate_down, [after(down_sum, second[0])[None]],
            [v[None] for v in (down_weight, down_momentum, down_variance)], 0, False, False,
        )
    )
    gain_sum = jnp.concatenate(
        [jnp.sum(gain_one_part, axis=0), jnp.sum(gain_two_part, axis=0)], axis=0
    )
    gain_sum = gain_sum + core_swap(gain_sum)
    gain_sum = gain_sum + chip_swap(gain_sum)
    gain_sum = gain_sum + shard_swap(gain_sum) if paired else lax.psum(gain_sum, "shard")
    if lax.axis_size("ctx") == 4:
        gain_sum = gain_sum + lax.ppermute(gain_sum, "ctx", EVEN)
        gain_sum = gain_sum + lax.ppermute(gain_sum, "ctx", ACROSS)
    else:
        gain_sum = lax.psum(gain_sum, "ctx")
    gains_here = norm_gains.shape[1]
    gain_grad = lax.dynamic_slice_in_dim(gain_sum, shard_place * gains_here, gains_here, axis=1)

    block_sums = [line_end(*one, 0) for one in (first, second)]
    qkv_set = turned_back(
        (1, 0, 2),
        run_update(
            "update_qkv", rate_qkv, block_sums,
            turned_state((1, 0, 2), qkv_weight, qkv_momentum, qkv_variance), 0, False, True,
        ),
    )
    output_set = tuple(
        v[0]
        for v in run_update(
            "update_output", rate_output, block_sums,
            [v[None] for v in (output_weight, output_momentum, output_variance)], 3, True, True,
        )
    )
    gains_set = adam(norm_gains, gains_momentum, gains_variance, gain_grad, rate_gains, 0.0)
    return (hidden_out, grad_in) + qkv_set + output_set + geglu_set + down_set + gains_set


def solution(mesh):
    tokens = P(("shard", "tp"), "ctx", None)
    split_in = P("shard", None, "tp")
    split_out = P("tp", "shard")
    gains = P(None, "shard")
    return jax.shard_map(
        body,
        mesh=mesh,
        in_specs=(
            (tokens, P("shard", None), tokens, split_in, split_out, split_in, split_out, gains)
            + (split_in, split_in, split_out, split_out)
            + (split_in, split_in, split_out, split_out)
            + (gains, gains)
        ),
        out_specs=(
            (tokens, tokens)
            + (split_in,) * 3
            + (split_out,) * 3
            + (split_in,) * 3
            + (split_out,) * 3
            + (gains,) * 3
        ),
        check_vma=False,
    )
```

```python
import functools
import math

import jax
import jax.numpy as jnp
from jax import lax
from jax.experimental import pallas as pl
from jax.experimental.pallas import tpu as pltpu
from jax.sharding import PartitionSpec as P

HD = 64
HALF = 64
L = 1024
STEP = 10
PAIR = 2 * HD
QBLOCK = 128
KBLOCK = QBLOCK + 2 * HALF

theta_base = 10000.0
norm_eps = 1e-05
beta_first = 0.9
beta_second = 0.98
adam_eps = 1e-06
decay_rate = 1e-05
rate_qkv = 0.06
rate_output = 0.35
rate_geglu = 0.06
rate_down = 0.04
rate_gains = 0.5
masked_value = -1e30

low = jnp.bfloat16
wide = jnp.float32
SCALING = 1.0 / math.sqrt(HD)
VMEM = 40 * 1024 * 1024

CORE_SWAP = [(0, 1), (1, 0), (2, 3), (3, 2)]
CHIP_SWAP = [(0, 2), (2, 0), (1, 3), (3, 1)]


def core_swap(values):
    return lax.ppermute(values, "tp", CORE_SWAP)


def chip_swap(values):
    return lax.ppermute(values, "tp", CHIP_SWAP)


def shard_swap(values):
    return lax.ppermute(values, "shard", [(0, 1), (1, 0)])


def dot(a, b):
    return lax.dot_general(a, b, (((1,), (0,)), ((), ())), preferred_element_type=wide)


def dot_nt(a, b):
    return lax.dot_general(a, b, (((1,), (1,)), ((), ())), preferred_element_type=wide)


def dot_tn(a, b):
    return lax.dot_general(a, b, (((0,), (0,)), ((), ())), preferred_element_type=wide)


def normalized(values):
    centered = values - jnp.mean(values, axis=-1, keepdims=True)
    spread = jnp.mean(centered * centered, axis=-1, keepdims=True)
    inverse = lax.rsqrt(spread + norm_eps)
    return centered * inverse, inverse


def norm_back(values, gain, cotangent):
    unit, inverse = normalized(values)
    scaled = cotangent * gain
    first = jnp.mean(scaled, axis=-1, keepdims=True)
    second = jnp.mean(scaled * unit, axis=-1, keepdims=True)
    gain_part = jnp.sum(cotangent * unit, axis=0, keepdims=True)
    return (scaled - first - unit * second) * inverse, gain_part


def turned(values, cosine, sine):
    half_len = HD // 2
    lane = lax.broadcasted_iota(jnp.int32, values.shape, 1)
    ahead = pltpu.roll(values, PAIR - half_len, 1)
    behind = pltpu.roll(values, half_len, 1)
    other = jnp.where(lane % HD < half_len, ahead, behind)
    return values * cosine + other * sine


def head_stack(values):
    lane = lax.broadcasted_iota(jnp.int32, values.shape, 1)
    zero = jnp.zeros_like(values)
    return jnp.concatenate(
        [jnp.where(lane < HD, values, zero), jnp.where(lane < HD, zero, values)], axis=0
    )


def head_join(values):
    rows = values.shape[0] // 2
    upper, lower = values[:rows], values[rows:]
    lane = lax.broadcasted_iota(jnp.int32, upper.shape, 1)
    return jnp.where(lane < HD, upper, lower)


def chances_of(query_stack, keys, bias):
    scores = dot_nt(query_stack, keys) * SCALING + jnp.concatenate([bias, bias], axis=0)
    weights = jnp.exp(scores - jnp.max(scores, axis=-1, keepdims=True))
    return weights * (1.0 / jnp.sum(weights, axis=-1, keepdims=True))


def halves(ref_values, place, half):
    mine = pl.ds(pl.multiple_of(place * half, half), half)
    theirs = pl.ds(pl.multiple_of((1 - place) * half, half), half)
    return mine, theirs


def first_norm_kernel(before_ref, here_ref, after_ref, gain_ref, out_ref, turned_ref):
    tokens = [ref[...].astype(wide) for ref in (before_ref, here_ref, after_ref)]
    normed = normalized(jnp.concatenate(tokens, axis=0))[0] * gain_ref[...]
    out_ref[...] = normed.astype(low)
    turned_ref[...] = normed.T.astype(low)


def attend_kernel(
    place_ref, normed_ref, mine_ref, theirs_ref, cos_ref, sin_ref, bias_ref,
    query_ref, key_ref, value_ref, out_ref,
):
    seg_len = query_ref.shape[0]
    half = mine_ref.shape[1]
    mine, theirs = halves(normed_ref, place_ref[0], half)
    inner = slice(HALF, HALF + seg_len)

    def project(which, rows):
        return dot(normed_ref[rows, mine], mine_ref[which]) + dot(
            normed_ref[rows, theirs], theirs_ref[which]
        )

    whole = slice(0, normed_ref.shape[0])
    queries, keys = project(0, inner), project(1, whole)
    value_ref[...] = project(2, whole).astype(low)
    for first in range(0, query_ref.shape[1], PAIR):
        lanes = slice(first, first + PAIR)
        query_ref[:, lanes] = turned(queries[:, lanes], cos_ref[inner], sin_ref[inner]).astype(low)
        key_ref[:, lanes] = turned(keys[:, lanes], cos_ref[...], sin_ref[...]).astype(low)
    for first in range(0, query_ref.shape[1], PAIR):
        lanes = slice(first, first + PAIR)
        for block in range(seg_len // QBLOCK):
            rows = slice(block * QBLOCK, block * QBLOCK + QBLOCK)
            reach = slice(block * QBLOCK, block * QBLOCK + KBLOCK)
            chances = chances_of(head_stack(query_ref[rows, lanes]), key_ref[reach, lanes], bias_ref[block])
            out_ref[rows, lanes] = head_join(dot(chances.astype(low), value_ref[reach, lanes])).astype(low)


def attend_back_kernel(chained, *refs):
    (
        place_ref, grad_ref, grad_turned_ref, normed_ref, attended_ref, mine_ref, theirs_ref,
        query_ref, key_ref, value_ref, cos_ref, sin_ref, bias_ref,
    ) = refs[:13]
    before_refs = refs[13:15] if chained else ()
    mixed_ref, own_ref, far_ref, key_sum, value_sum, weight_sum = refs[-6:]
    seg_len = query_ref.shape[0]
    half = mine_ref.shape[0]
    mine, theirs = halves(grad_ref, place_ref[0], half)
    inner = slice(HALF, HALF + seg_len)
    grad_out = (
        dot(grad_ref[:, mine], mine_ref[...]) + dot(grad_ref[:, theirs], theirs_ref[...])
    ).astype(low)
    key_sum[...] = jnp.zeros_like(key_sum)
    value_sum[...] = jnp.zeros_like(value_sum)
    edge = jnp.zeros((HALF, query_ref.shape[1]), low)
    mixed_ref[0, :HALF] = edge
    mixed_ref[0, HALF + seg_len :] = edge
    for first in range(0, query_ref.shape[1], PAIR):
        lanes = slice(first, first + PAIR)
        for block in range(seg_len // QBLOCK):
            rows = slice(block * QBLOCK, block * QBLOCK + QBLOCK)
            reach = slice(block * QBLOCK, block * QBLOCK + KBLOCK)
            place_rows = slice(HALF + block * QBLOCK, HALF + block * QBLOCK + QBLOCK)
            queries = head_stack(query_ref[rows, lanes])
            grads = head_stack(grad_out[rows, lanes])
            keys, values = key_ref[reach, lanes], value_ref[reach, lanes]
            chances = chances_of(queries, keys, bias_ref[block])
            grad_chances = dot_nt(grads, values)
            weighted = chances * grad_chances
            grad_scores = (
                weighted - chances * jnp.sum(weighted, axis=-1, keepdims=True)
            ).astype(low)
            value_sum[reach, lanes] += dot_tn(chances.astype(low), grads)
            key_sum[reach, lanes] += dot_tn(grad_scores, queries)
            grad_queries = head_join(dot(grad_scores, keys)) * SCALING
            mixed_ref[0, place_rows, lanes] = turned(
                grad_queries, cos_ref[place_rows], -sin_ref[place_rows]
            ).astype(low)
        mixed_ref[1, :, lanes] = turned(
            key_sum[:, lanes] * SCALING, cos_ref[...], -sin_ref[...]
        ).astype(low)
    mixed_ref[2] = value_sum[...].astype(low)

    parts = []
    for lanes in (mine, theirs):
        parts += [dot(normed_ref[lanes], mixed_ref[which]) for which in range(3)]
        parts.append(dot(grad_turned_ref[lanes], attended_ref[...]))

    @pl.when(pl.program_id(0) == 0)
    def _():
        for index, part in enumerate(parts):
            if chained:
                part += before_refs[index // 4][index % 4].astype(wide)
            weight_sum[index] = part

    @pl.when(pl.program_id(0) > 0)
    def _():
        for index, part in enumerate(parts):
            weight_sum[index] += part

    @pl.when(pl.program_id(0) == pl.num_programs(0) - 1)
    def _():
        for index in range(4):
            own_ref[index] = weight_sum[index].astype(low)
            far_ref[index] = weight_sum[4 + index].astype(low)


def second_norm_kernel(place_ref, *refs):
    group = (len(refs) - 4) // 3
    attended, mine_refs, theirs_refs = refs[:group], refs[group : 2 * group], refs[2 * group : 3 * group]
    hidden_ref, gain_ref, middle_ref, normed_ref = refs[3 * group :]
    half = mine_refs[0].shape[0]
    mine, theirs = halves(middle_ref, place_ref[0], half)
    for lanes, weights in ((mine, mine_refs), (theirs, theirs_refs)):
        total = hidden_ref[:, lanes].astype(wide)
        for one, weight in zip(attended, weights):
            total += dot_nt(one[...], weight[...])
        middle_ref[:, lanes] = total
    normed_ref[...] = (normalized(middle_ref[...])[0] * gain_ref[...]).astype(low)


def feed_kernel(place_ref, *refs):
    group = (len(refs) - 4) // 5
    tokens, grads = refs[:group], refs[group : 2 * group]
    mine_ref, theirs_ref, down_mine_ref, down_theirs_ref = refs[2 * group : 2 * group + 4]
    outs = refs[2 * group + 4 :]
    half = mine_ref.shape[1]
    units = down_mine_ref.shape[0]
    mine, theirs = halves(mine_ref, place_ref[0], half)
    for index in range(group):
        normed_ref, grad_ref = tokens[index], grads[index]
        act_ref, out_ref, back_ref = outs[3 * index : 3 * index + 3]
        own, far = normed_ref[:, mine], normed_ref[:, theirs]
        gate = dot_nt(own, mine_ref[:units]) + dot_nt(far, theirs_ref[:units])
        up = dot_nt(own, mine_ref[units:]) + dot_nt(far, theirs_ref[units:])
        grad_inner = dot_nt(grad_ref[:, mine], down_mine_ref[...]) + dot_nt(
            grad_ref[:, theirs], down_theirs_ref[...]
        )
        normal = 0.5 * (1.0 + lax.erf(gate * math.sqrt(0.5)))
        density = jnp.exp(-0.5 * gate * gate) * (1.0 / math.sqrt(2.0 * math.pi))
        gelu = gate * normal
        inner = (gelu * up).astype(low)
        grad_gate = (grad_inner * up * (normal + gate * density)).astype(low)
        grad_up = (grad_inner * gelu).astype(low)
        act_ref[0] = grad_gate
        act_ref[1] = grad_up
        act_ref[2] = inner
        for lanes, weight, down in (
            (mine, mine_ref, down_mine_ref), (theirs, theirs_ref, down_theirs_ref)
        ):
            back_ref[:, lanes] = (
                dot(grad_gate, weight[:units]) + dot(grad_up, weight[units:])
            ).astype(low)
            out_ref[:, lanes] = dot(inner, down[...]).astype(low)


def update(weight, momentum, variance, gradient, rate):
    momentum_new = beta_first * momentum + (1.0 - beta_first) * gradient
    variance_new = beta_second * variance + (1.0 - beta_second) * gradient * gradient
    first_hat = momentum_new * (1.0 / (1.0 - beta_first**STEP))
    second_hat = variance_new * (1.0 / (1.0 - beta_second**STEP))
    new = weight - rate * (first_hat / (jnp.sqrt(second_hat) + adam_eps) + decay_rate * weight)
    return new, momentum_new, variance_new


def update_kernel(rate, flip, by_half, count, *refs):
    which = pl.program_id(1) if by_half else 0
    state, outs = refs[count : count + 3], refs[count + 3 :]
    for index in range(count):

        @pl.when(which == index)
        def _():
            gradient = refs[index][...].astype(wide)
            if flip:
                gradient = gradient.T
            for out, value in zip(outs, update(*(one[...] for one in state), gradient, rate)):
                out[...] = value


def run_update(name, rate, pieces, state, skip, flip, by_half):
    dim = 1 if flip else 0
    size = list(state[0].shape[1:])
    size[dim] //= 2
    if size[0] % 8 or size[1] % 128:
        if by_half:
            gradient = jnp.concatenate(pieces, axis=1)[skip : skip + state[0].shape[0]]
        else:
            gradient = pieces[0]
        gradient = gradient.astype(wide)
        if flip:
            gradient = jnp.transpose(gradient, (0, 2, 1))
        return update(*state, gradient, rate)

    def place(c, h):
        return (c, h, 0) if dim == 0 else (c, 0, h)

    spec = pl.BlockSpec((None, *size), place)
    grad_spec = spec
    if by_half:
        cut = size[::-1] if flip else size
        grad_spec = pl.BlockSpec((None, *cut), lambda c, h: (c + skip, 0, 0))
    return pl.pallas_call(
        functools.partial(update_kernel, rate, flip, by_half, len(pieces)),
        grid=(state[0].shape[0], 2),
        in_specs=[grad_spec] * len(pieces) + [spec] * 3,
        out_specs=[spec] * 3,
        out_shape=[jax.ShapeDtypeStruct(state[0].shape, wide)] * 3,
        name=name,
        compiler_params=pltpu.CompilerParams(vmem_limit_bytes=VMEM),
        cost_estimate=pl.CostEstimate(flops=1000, bytes_accessed=1000, transcendentals=0),
    )(*pieces, *state)


def feed_weights_kernel(place_ref, *refs):
    group = (len(refs) - 3) // 3
    acts, tokens, grads = refs[:group], refs[group : 2 * group], refs[2 * group : 3 * group]
    own_ref, *far_refs = refs[3 * group :]
    half = own_ref.shape[-1]
    mine, theirs = halves(own_ref, place_ref[0], half)

    for step, rights in enumerate((tokens, tokens, grads)):

        @pl.when(pl.program_id(0) == step)
        def _():
            far_ref = far_refs[0].at[step] if step < 2 else far_refs[1]
            for out, lanes in ((own_ref, mine), (far_ref, theirs)):
                total = None
                for act, right in zip(acts, rights):
                    for row in range(act.shape[0]):
                        part = dot_tn(act[row], right[row, :, lanes])
                        total = part if total is None else total + part
                out[...] = total.astype(low)


def middle_back_kernel(
    one_ref, two_ref, three_ref, middle_ref, gain_ref, grad_ref,
    out_ref, low_ref, turned_ref, gain_out_ref,
):
    cotangent = one_ref[...].astype(wide) + two_ref[...].astype(wide) + three_ref[...].astype(wide)
    back, gain_part = norm_back(middle_ref[...], gain_ref[...], cotangent)
    total = grad_ref[...] + back
    out_ref[...] = total
    low_ref[...] = total.astype(low)
    turned_ref[...] = total.T.astype(low)
    gain_out_ref[...] = gain_part


def normed_grad_kernel(place_ref, *refs):
    group = (len(refs) - 1) // 3
    grads, mine_refs, theirs_refs = refs[:group], refs[group : 2 * group], refs[2 * group : 3 * group]
    out_ref = refs[-1]
    half = mine_refs[0].shape[1]
    mine, theirs = halves(out_ref, place_ref[0], half)
    for lanes, weights in ((mine, mine_refs), (theirs, theirs_refs)):
        total = None
        for grad, weight in zip(grads, weights):
            for which in range(3):
                part = dot_nt(grad[which], weight[which])
                total = part if total is None else total + part
        out_ref[:, lanes] = total


def input_back_kernel(
    here_ref, before_ref, after_ref, hidden_ref, gain_ref, grad_ref, out_ref, gain_out_ref
):
    seg_len = hidden_ref.shape[0]
    gain = gain_ref[...]
    hidden = hidden_ref[...].astype(wide)
    centre = here_ref[HALF : HALF + seg_len]
    cotangent = jnp.concatenate(
        [
            centre[:HALF] + before_ref[...].astype(wide),
            centre[HALF : seg_len - HALF],
            centre[seg_len - HALF :] + after_ref[...].astype(wide),
        ],
        axis=0,
    )
    back, gain_part = norm_back(hidden, gain, cotangent)
    out_ref[...] = grad_ref[...] + back
    gain_out_ref[...] = gain_part


def by_row(shape):
    rest = tuple(shape[1:])
    return pl.BlockSpec((None,) + rest, lambda r: (r,) + (0,) * len(rest))


def fixed(shape):
    return pl.BlockSpec(tuple(shape), lambda r: (0,) * len(shape))


def spec_of(values, kind):
    if kind == "row":
        return by_row(values.shape)
    if kind == "second":
        return pl.BlockSpec(
            (values.shape[0], None) + tuple(values.shape[2:]),
            lambda r: (0, r) + (0,) * (len(values.shape) - 2),
        )
    if kind == "step":
        return pl.BlockSpec((None,) + tuple(values.shape[1:]), lambda r: (r, 0, 0, 0))
    if kind == "head":
        return pl.BlockSpec((3,) + tuple(values.shape[1:]), lambda r: (0, 0, 0))
    if kind == "last":
        return pl.BlockSpec((None,) + tuple(values.shape[1:]), lambda r: (3, 0, 0))
    if kind == "scalar":
        return pl.BlockSpec(memory_space=pltpu.SMEM)
    return fixed(values.shape)


def in_hbm(values):
    return pltpu.with_memory_space_constraint(values, pltpu.HBM)


def run(kernel, name, steps, ins, outs, scratch=(), far_outs=()):
    return pl.pallas_call(
        kernel,
        grid=(steps,),
        in_specs=[spec_of(value, kind) for value, kind in ins],
        out_specs=[spec_of(shape, kind) for shape, kind in outs],
        out_shape=[
            pltpu.HBM(shape.shape, shape.dtype) if index in far_outs else shape
            for index, (shape, kind) in enumerate(outs)
        ],
        scratch_shapes=list(scratch),
        name=name,
        compiler_params=pltpu.CompilerParams(vmem_limit_bytes=VMEM),
        cost_estimate=pl.CostEstimate(flops=1000, bytes_accessed=1000, transcendentals=0),
    )(*[value for value, kind in ins])


def doc_tables(starts, places):
    inside = (places >= 0) & (places < L)
    before = starts[..., None, :] <= places[..., :, None]
    number = jnp.sum(before.astype(jnp.int32), axis=-1) - 1
    begins = jnp.max(jnp.where(before, starts[..., None, :], 0), axis=-1)
    return (jnp.where(inside, number, -1), places - begins)


def adam(weight, momentum, variance, gradient, step_rate, shrink_rate):
    momentum_new = beta_first * momentum + (1.0 - beta_first) * gradient
    variance_new = beta_second * variance + (1.0 - beta_second) * gradient * gradient
    first_hat = momentum_new / (1.0 - beta_first**STEP)
    second_hat = variance_new / (1.0 - beta_second**STEP)
    updated = weight - step_rate * (
        first_hat / (jnp.sqrt(second_hat) + adam_eps) + shrink_rate * weight
    )
    return (updated, momentum_new, variance_new)


def take(values, index, size, dim):
    return lax.dynamic_slice_in_dim(values, index * size, size, axis=dim)


def joined(bit, mine, theirs, dim):
    return jnp.where(
        bit == 0,
        jnp.concatenate([mine, theirs], axis=dim),
        jnp.concatenate([theirs, mine], axis=dim),
    )


def after(values, *others):
    return lax.optimization_barrier((values,) + others)[0]


def all_after(values, *others):
    return lax.optimization_barrier(tuple(values) + others)[: len(values)]


EVEN = [(0, 1), (1, 0), (2, 3), (3, 2)]
ACROSS = [(0, 2), (2, 0), (1, 3), (3, 1)]


def line_one(values, dim):
    if lax.axis_size("ctx") != 4:
        return values, None
    parity = lax.rem(lax.axis_index("ctx"), 2)
    size = values.shape[dim] // 2
    got = lax.ppermute(take(values, 1 - parity, size, dim), "ctx", EVEN)
    return take(values, parity, size, dim), got


def line_two(kept, got):
    if got is None:
        return kept, None
    part = added(kept, got)
    return part, lax.ppermute(part, "ctx", ACROSS)


def line_three(kept, got):
    if got is None:
        return kept, None
    part = added(kept, got)
    return part, lax.ppermute(part, "ctx", EVEN)


def line_end(kept, got, dim):
    if got is None:
        return lax.psum(kept.astype(wide), "ctx").astype(low)
    return joined(lax.rem(lax.axis_index("ctx"), 2), kept, got, dim)


def added(*values):
    return sum(value.astype(wide) for value in values).astype(low)


def turned_state(axes, *values):
    return [jnp.transpose(v, axes) for v in values]


def turned_back(axes, values):
    return tuple(jnp.transpose(v, axes) for v in values)


def body(
    hidden_in,
    doc_starts,
    grad_out,
    qkv_weight,
    output_weight,
    geglu_weight,
    down_weight,
    norm_gains,
    qkv_momentum,
    qkv_variance,
    output_momentum,
    output_variance,
    geglu_momentum,
    geglu_variance,
    down_momentum,
    down_variance,
    gains_momentum,
    gains_variance,
):
    rows, seg_len, model_width = hidden_in.shape
    shards = lax.axis_size("shard")
    paired = shards == 2
    half = model_width // 2
    shard_place = lax.axis_index("shard")
    group_place = lax.axis_index("tp")
    ctx_place = lax.axis_index("ctx")
    place = shard_place if paired else jnp.zeros_like(shard_place)
    place_one = place.astype(jnp.int32).reshape(1)
    group = (0, 1, 2, 3)
    span = seg_len + 2 * HALF
    cols = qkv_weight.shape[2]
    units = down_weight.shape[0]

    count = lax.axis_size("ctx")
    forward = [(i, i + 1) for i in range(count - 1)]
    backward = [(i + 1, i) for i in range(count - 1)]
    before = lax.ppermute(hidden_in[:, seg_len - HALF :], "ctx", forward)
    after_edge = lax.ppermute(hidden_in[:, :HALF], "ctx", backward)

    def both(values, dim):
        if paired:
            return values, shard_swap(values)
        full = lax.all_gather(values, "shard", axis=dim, tiled=True)
        return (
            lax.slice_in_dim(full, 0, half, axis=dim),
            lax.slice_in_dim(full, half, 2 * half, axis=dim),
        )

    gains_near = norm_gains.astype(low)
    if paired:
        gains_low = joined(place, gains_near, shard_swap(after(gains_near, before, after_edge)), 1)
    else:
        gains_low = lax.all_gather(gains_near, "shard", axis=1, tiled=True)
    gain_one = gains_low[0:1].astype(wide)
    gain_two = gains_low[1:2].astype(wide)

    qkv_turned = jnp.transpose(qkv_weight, (1, 0, 2))
    geglu_turned = jnp.transpose(geglu_weight, (1, 2, 0))
    block_low = jnp.concatenate(
        [qkv_turned.astype(low), jnp.transpose(output_weight).astype(low)[None]], axis=0
    )
    mine, theirs = both(block_low, 1)
    geglu_low = after(geglu_turned, before, after_edge).astype(low).reshape(2 * units, -1)
    geglu_mine, geglu_theirs = both(geglu_low, 1)
    down_low = after(down_weight, before, after_edge).astype(low)
    down_mine, down_theirs = both(down_low, 1)

    grad_low = after(grad_out, before, after_edge).astype(low)
    offset = ctx_place * seg_len
    ext_places = offset - HALF + jnp.arange(span, dtype=jnp.int32)
    tp_rows = lax.dynamic_slice_in_dim(doc_starts, group_place * rows, rows, axis=0)
    ext_doc, ext_place = doc_tables(tp_rows, ext_places)
    inverse = theta_base ** (-2.0 * jnp.arange(HD // 2, dtype=wide) / HD)
    angles = ext_place.astype(wide)[..., None] * inverse
    cosine, sine = jnp.cos(angles), jnp.sin(angles)
    cosine = jnp.concatenate([cosine] * 4, axis=-1)
    sine = jnp.concatenate([-sine, sine, -sine, sine], axis=-1)
    blocks = seg_len // QBLOCK
    query_doc = ext_doc[:, HALF : HALF + seg_len].reshape(rows, blocks, QBLOCK)
    key_doc = jnp.stack(
        [ext_doc[:, b * QBLOCK : b * QBLOCK + KBLOCK] for b in range(blocks)], axis=1
    )
    gap = jnp.arange(QBLOCK)[:, None] + HALF - jnp.arange(KBLOCK)[None, :]
    allowed = (jnp.abs(gap) <= HALF) & (query_doc[..., :, None] == key_doc[..., None, :])
    bias = jnp.where(allowed, 0.0, masked_value).astype(wide)

    normed, normed_turned = run(
        first_norm_kernel, "first_norm", rows,
        [(before, "row"), (hidden_in, "row"), (after_edge, "row"), (gain_one, "all")],
        [
            (jax.ShapeDtypeStruct((rows, span, model_width), low), "row"),
            (jax.ShapeDtypeStruct((rows, model_width, span), low), "row"),
        ],
        far_outs=(1,),
    )

    far_mine = chip_swap(mine)
    near_mine = core_swap(mine)
    theirs = after(
        theirs, before, after_edge, cosine, sine, bias, geglu_low, down_low, grad_low, far_mine
    )
    far_theirs = chip_swap(theirs)
    weights = [(mine, theirs), (near_mine, core_swap(theirs))]
    scalar = (place_one, "scalar")
    tables = [(cosine, "row"), (sine, "row"), (bias, "row")]
    short = jax.ShapeDtypeStruct((rows, seg_len, cols), low)
    long = jax.ShapeDtypeStruct((rows, span, cols), low)
    saved = []
    for j in group:
        tokens_here = normed if j == 0 else after(normed, saved[j - 1][3])
        if j == 2:
            far_theirs = after(far_theirs, saved[1][3])
            weights.append((far_mine, far_theirs))
            weights.append((core_swap(far_mine), core_swap(far_theirs)))
            grad_far = chip_swap(after(grad_low, far_theirs))
        if j == 3:
            tokens_here = after(tokens_here, geglu_theirs)
        saved.append(
            run(
                attend_kernel, "attend", rows,
                [scalar, (tokens_here, "row"), (weights[j][0], "head"), (weights[j][1], "head")]
                + tables,
                [(short, "row"), (long, "row"), (long, "row"), (short, "row")],
                far_outs=(0, 1, 2),
            )
        )
    attended = [one[3] for one in saved]
    attended[3] = after(attended[3], down_theirs, grad_far)
    middle, normed_two = run(
        second_norm_kernel, "second_norm", rows,
        [scalar]
        + [(one, "row") for one in attended]
        + [(weights[j][0], "last") for j in group]
        + [(weights[j][1], "last") for j in group]
        + [(hidden_in, "row"), (gain_two, "all")],
        [
            (jax.ShapeDtypeStruct((rows, seg_len, model_width), wide), "row"),
            (jax.ShapeDtypeStruct((rows, seg_len, model_width), low), "row"),
        ],
    )

    normed_far = chip_swap(normed_two)
    normed_one = core_swap(normed_two)
    grad_one = core_swap(grad_low)
    act_rows = jax.ShapeDtypeStruct((3, rows, seg_len, units), low)
    full_rows = jax.ShapeDtypeStruct((rows, seg_len, model_width), low)

    def feed(tokens, grads):
        done = run(
            feed_kernel, "feed", rows,
            [scalar]
            + [(one, "row") for one in tokens]
            + [(one, "row") for one in grads]
            + [(one, "all") for one in (geglu_mine, geglu_theirs, down_mine, down_theirs)],
            [(act_rows, "second"), (full_rows, "row"), (full_rows, "row")] * len(tokens),
            far_outs=(1, 4),
        )
        return [done[3 * i : 3 * i + 3] for i in range(len(tokens))]

    tokens, grads = [normed_two, normed_one], [grad_low, grad_one]
    fed = feed(tokens, grads)
    back_one, out_one = core_swap(fed[1][2]), core_swap(fed[1][1])
    normed_far = after(normed_far, fed[0][2], back_one, out_one)
    tokens += [normed_far, core_swap(normed_far)]
    grads += [grad_far, core_swap(grad_far)]
    fed += feed(tokens[2:], grads[2:])
    back_three = core_swap(fed[3][2])
    back_far = chip_swap(added(fed[2][2], back_three))
    out_three = core_swap(after(fed[3][1], back_three))

    feed_part = jax.ShapeDtypeStruct((3, units, half), low)
    feed_own, *feed_other = run(
        feed_weights_kernel, "feed_weights", 3,
        [scalar]
        + [(after(fed[0][0], back_three), "step")]
        + [(one[0], "step") for one in fed[1:]]
        + [(one, "all") for one in tokens]
        + [(one, "all") for one in grads],
        [
            (feed_part, "row"),
            (jax.ShapeDtypeStruct((2, units, half), low), "all"),
            (jax.ShapeDtypeStruct((units, half), low), "all"),
        ],
    )

    out_sum = added(fed[2][1], after(out_three, feed_own))
    out_far = chip_swap(out_sum)
    back_far = after(back_far, feed_own, out_sum)
    gain_shape = jax.ShapeDtypeStruct((rows, 1, model_width), wide)
    grad_middle, middle_low, middle_turned, gain_two_part = run(
        middle_back_kernel, "middle_back", rows,
        [
            (after(fed[0][2], feed_own), "row"), (back_one, "row"), (back_far, "row"),
            (middle, "row"), (gain_two, "all"), (grad_out, "row"),
        ],
        [
            (jax.ShapeDtypeStruct(grad_out.shape, wide), "row"),
            (jax.ShapeDtypeStruct(grad_out.shape, low), "row"),
            (jax.ShapeDtypeStruct((rows, model_width, seg_len), low), "row"),
            (gain_shape, "row"),
        ],
        far_outs=(0, 1, 2),
    )

    if paired:
        geglu_got, down_got = [shard_swap(one) for one in feed_other]
    else:
        feed_other[1] = feed_other[1][None]
        feed_got = lax.psum_scatter(
            jnp.concatenate([feed_own, jnp.concatenate(feed_other, axis=0)], axis=2),
            "shard", scatter_dimension=2, tiled=True,
        )
        geglu_got, down_got = feed_got[:2], feed_got[2]

    mixed, own, other = [None] * 4, [None] * 4, [None] * 4
    weight_part = jax.ShapeDtypeStruct((4, half, cols), low)
    def attend_back(j, sums, *before_it):
        queries, keys, values, out = saved[j]
        mixed[j], own[j], other[j] = run(
            functools.partial(attend_back_kernel, bool(sums)), "attend_back", rows,
            [
                scalar, (in_hbm(after(middle_low, *before_it)), "row"),
                (in_hbm(middle_turned), "row"), (in_hbm(normed_turned), "row"), (out, "row"),
                (weights[j][0], "last"), (weights[j][1], "last"),
                (in_hbm(queries), "row"), (in_hbm(keys), "row"), (in_hbm(values), "row"),
            ]
            + tables
            + [(one, "all") for one in sums],
            [
                (jax.ShapeDtypeStruct((3, rows, span, cols), low), "second"),
                (weight_part, "all"), (weight_part, "all"),
            ],
            scratch=[
                pltpu.VMEM((span, cols), wide), pltpu.VMEM((span, cols), wide),
                pltpu.VMEM((8, half, cols), wide),
            ],
            far_outs=(0,),
        )

    attend_back(3, (), back_far)
    far_sums = core_swap(own[3]), core_swap(other[3])
    attend_back(1, (), mixed[3])
    near_sums = core_swap(own[1]), core_swap(other[1])
    geglu_got = after(geglu_got, mixed[1])
    geglu_part = added(feed_own[:2], geglu_got) if paired else geglu_got
    geglu_line = line_one(geglu_part, 0)
    attend_back(2, far_sums, mixed[1], geglu_got, out_far)
    far_got = shard_swap(other[2]) if paired else None
    geglu_line = line_two(*all_after(geglu_line, mixed[2]))
    down_got = after(down_got, mixed[2])
    down_part = added(feed_own[2], down_got) if paired else down_got
    down_line = line_one(down_part, 1)
    attend_back(0, near_sums, mixed[2], geglu_line[0], down_got)
    down_line = line_two(*all_after(down_line, mixed[0]))

    cut = half // 2
    if paired:
        near_got = [shard_swap(other[0][:, i * cut : (i + 1) * cut]) for i in (0, 1)]
        far_part = added(own[2], after(far_got, down_line[0]))
    else:
        scatter = functools.partial(
            lax.psum_scatter, axis_name="shard", scatter_dimension=1, tiled=True
        )
        far_part = scatter(jnp.concatenate([own[2], other[2]], axis=1))
        near_sum = scatter(jnp.concatenate([own[0], other[0]], axis=1))
    far_rows = far_part.shape[1] // 2
    far = [chip_swap(far_part[:, i * far_rows : (i + 1) * far_rows]) for i in (0, 1)]

    def cut_of(index, *others):
        rows_at = slice(index * far_rows, (index + 1) * far_rows)
        if paired:
            got = all_after((near_got[index], far[index]), *others)
            return added(own[0][:, rows_at], *got)
        return added(near_sum[:, rows_at], after(far[index], *others))

    (normed_grad,) = run(
        normed_grad_kernel, "normed_grad", rows,
        [scalar]
        + [(after(mixed[0], far_part), "second")]
        + [(mixed[j], "second") for j in group[1:]]
        + [(weights[j][0], "head") for j in group]
        + [(weights[j][1], "head") for j in group],
        [(jax.ShapeDtypeStruct((rows, span, model_width), wide), "row")],
    )
    to_before = lax.ppermute(normed_grad[:, :HALF].astype(low), "ctx", backward)
    to_after = lax.ppermute(normed_grad[:, HALF + seg_len :].astype(low), "ctx", forward)


    geglu_line = line_three(*all_after(geglu_line, normed_grad))
    first = line_one(cut_of(0, normed_grad), 0)
    if paired:
        far[1] = after(far[1], near_got[1])
    to_before, to_after = all_after(
        (to_before, to_after), first[0], far[1], *geglu_line, *down_line
    )
    grad_in, gain_one_part = run(
        input_back_kernel, "input_back", rows,
        [
            (normed_grad, "row"), (to_after, "row"), (to_before, "row"), (hidden_in, "row"),
            (gain_one, "all"), (grad_middle, "row"),
        ],
        [(jax.ShapeDtypeStruct(grad_out.shape, wide), "row"), (gain_shape, "row")],
    )
    result = middle + fed[0][1].astype(wide) + out_one.astype(wide) + out_far.astype(wide)
    hidden_out = result.astype(low)

    first = line_two(*all_after(first, grad_in))
    second = line_one(cut_of(1, hidden_out, first[0]), 0)
    down_line = line_three(*all_after(down_line, second[0]))
    geglu_sum, down_sum = line_end(*geglu_line, 0), line_end(*down_line, 1)
    geglu_set = turned_back(
        (2, 0, 1),
        run_update(
            "update_geglu", rate_geglu, [after(geglu_sum, second[0])],
            turned_state((1, 2, 0), geglu_weight, geglu_momentum, geglu_variance), 0, False, False,
        ),
    )
    first = line_three(*all_after(first, geglu_set[0]))
    second = line_two(*all_after(second, first[0], *down_line))
    gain_one_part = after(gain_one_part, second[0])
    second = line_three(*second)
    down_set = tuple(
        v[0]
        for v in run_update(
            "update_down", rate_down, [after(down_sum, second[0])[None]],
            [v[None] for v in (down_weight, down_momentum, down_variance)], 0, False, False,
        )
    )
    gain_sum = jnp.concatenate(
        [jnp.sum(gain_one_part, axis=0), jnp.sum(gain_two_part, axis=0)], axis=0
    )
    gain_sum = gain_sum + core_swap(gain_sum)
    gain_sum = gain_sum + chip_swap(gain_sum)
    gain_sum = gain_sum + shard_swap(gain_sum) if paired else lax.psum(gain_sum, "shard")
    if lax.axis_size("ctx") == 4:
        gain_sum = after(gain_sum, second[0])
        gain_sum = gain_sum + lax.ppermute(gain_sum, "ctx", EVEN)
        gain_sum = gain_sum + lax.ppermute(gain_sum, "ctx", ACROSS)
    else:
        gain_sum = lax.psum(gain_sum, "ctx")
    gains_here = norm_gains.shape[1]
    gain_grad = lax.dynamic_slice_in_dim(gain_sum, shard_place * gains_here, gains_here, axis=1)

    block_sums = [line_end(*one, 0) for one in (first, second)]
    qkv_set = turned_back(
        (1, 0, 2),
        run_update(
            "update_qkv", rate_qkv, block_sums,
            turned_state((1, 0, 2), qkv_weight, qkv_momentum, qkv_variance), 0, False, True,
        ),
    )
    output_set = tuple(
        v[0]
        for v in run_update(
            "update_output", rate_output, block_sums,
            [v[None] for v in (output_weight, output_momentum, output_variance)], 3, True, True,
        )
    )
    gains_set = adam(norm_gains, gains_momentum, gains_variance, gain_grad, rate_gains, 0.0)
    return (hidden_out, grad_in) + qkv_set + output_set + geglu_set + down_set + gains_set


def solution(mesh):
    tokens = P(("shard", "tp"), "ctx", None)
    split_in = P("shard", None, "tp")
    split_out = P("tp", "shard")
    gains = P(None, "shard")
    return jax.shard_map(
        body,
        mesh=mesh,
        in_specs=(
            (tokens, P("shard", None), tokens, split_in, split_out, split_in, split_out, gains)
            + (split_in, split_in, split_out, split_out)
            + (split_in, split_in, split_out, split_out)
            + (gains, gains)
        ),
        out_specs=(
            (tokens, tokens)
            + (split_in,) * 3
            + (split_out,) * 3
            + (split_in,) * 3
            + (split_out,) * 3
            + (gains,) * 3
        ),
        check_vma=False,
    )
```
